32 devices in a mesh: sect: 2 (over x), lon: 4 (over z), lat: 4 (over y, core).
Axes of the slice: x: 2, y: 2, z: 4, core: 2. Of those that a mesh axis runs over, the one named last changes fastest.
Arguments:
- fields: float32 [2, 6, 16, 32, 512], P('sect', None, None, 'lat', 'lon'), may hold values from -3 to 3, as said below
- levels: int32 [32, 512], P('lat', 'lon'), may hold values from 0 to 16, as said below
Outputs:
- new_fields: float32 [2, 6, 16, 32, 512], P('sect', None, None, 'lat', 'lon')
The draws below stay inside these ranges and needn't reach their ends.
Inputs may be any that keep to these rules, and one draw needn't show every extreme that they name: `fields`: section 0: velocities of magnitude below 0.95, temperature and salinity, lateral viscosity between 0.02 and 0.2, background diffusivity between 0.05 and 2. Later sections: tracers. In each device's block of 8 x 128 columns at most 768 columns have levels above 0, and some block has exactly 768; the value 16 occurs in every draw.
All inputs are finite; a program needn't handle non-finite values.
Results may differ from the reference program's by a relative error of at most 0.00002.
Values sent between devices are 32-bit elements; how exact they have to be, the bound alone decides.
No kernel may reach another device: no remote copies, remote signals or barrier semaphores. Data moves between devices by JAX's collectives and lax.ppermute only.
A program may use at most 64 MiB of HBM per device.

```python
import math
import jax
import jax.numpy as jnp
from jax import lax

CLON = 128
CLAT = 8
LEV = 16
NSUB = 2
NF = 6
NLON = 512
NLAT = 32
WET_DEV = 768
N_SECT = 2
N_LON = 4
N_LAT = 4


def draw_fields(key, part):
    keys = jax.random.split(key, 8)
    shape = (LEV, NLAT, NLON)
    zonal_vel = jax.random.uniform(keys[0], shape, jnp.float32, -0.8, 0.8)
    merid_vel = jax.random.uniform(keys[1], shape, jnp.float32, -0.8, 0.8)
    temper = jnp.clip(jax.random.normal(keys[3], shape, jnp.float32), -3.0, 3.0)
    saline = jnp.clip(jax.random.normal(keys[4], shape, jnp.float32), -3.0, 3.0)
    viscosity = jnp.exp(jax.random.uniform(keys[5], shape, jnp.float32, math.log(0.02), math.log(0.2)))
    background = jnp.exp(jax.random.uniform(keys[6], shape, jnp.float32, math.log(0.05), math.log(2.0)))
    dyn_slot = jnp.stack([zonal_vel, merid_vel, temper, saline, viscosity, background])
    tracer_shape = (N_SECT - 1, NF, LEV, NLAT, NLON)
    tracers = jax.random.uniform(keys[7], tracer_shape, jnp.float32, 0.5, 2.0)
    return jnp.concatenate([dyn_slot[None], tracers], axis=0).astype(jnp.float32)


def draw_levels(key, part):
    key_first, key_second, key_forced, key_ranks, key_depth = jax.random.split(key, 5)
    blocks = N_LAT * N_LON
    block_cols = CLAT * CLON
    first = jax.random.randint(key_first, (blocks,), 0, WET_DEV + 1)
    second = jax.random.randint(key_second, (blocks,), 0, WET_DEV + 1)
    forced_id = jax.random.randint(key_forced, (), 0, blocks)
    block_ids = jnp.arange(blocks, dtype=jnp.int32)
    counts_wet = jnp.where(block_ids == forced_id, WET_DEV, jnp.minimum(first, second))

    def shuffled(sub_key):
        return jax.random.permutation(sub_key, block_cols)
    ranks = jax.vmap(shuffled)(jax.random.split(key_ranks, blocks)).astype(jnp.int32)
    depth = jax.random.randint(key_depth, (blocks, block_cols), 1, LEV + 1)
    deep_mark = (ranks == 0) & (block_ids == forced_id)[:, None]
    depth = jnp.where(deep_mark, LEV, depth)
    levels_flat = jnp.where(ranks < counts_wet[:, None], depth, 0)
    levels_grid = levels_flat.reshape(N_LAT, N_LON, CLAT, CLON).transpose(0, 2, 1, 3)
    return levels_grid.reshape(NLAT, NLON).astype(jnp.int32)


def shard_levels(key, extent, cuts, smallest, high):
    def one(dim, shards_of):
        heights = jax.random.uniform(jax.random.fold_in(jax.random.fold_in(key, 6), dim), (shards_of,), jnp.float32, smallest / len(cuts), high / len(cuts))
        return jnp.repeat(jnp.exp(heights), extent[dim] // shards_of).reshape((-1,) + (1,) * (len(extent) - dim - 1))

    factor_of = one(*cuts[0])
    for cut in cuts[1:]:
        factor_of = factor_of * one(*cut)
    return factor_of


def setup_inputs(seed: int = 0) -> dict:
    splits = jax.random.split(jax.random.key(seed), 3)
    fields = draw_fields(jax.random.fold_in(splits[2], 71), 0)
    levels = draw_levels(jax.random.fold_in(splits[2], 71), 0)
    return {"fields": fields, "levels": levels}


TIME_STEP = 1.0
CORIOLIS = 0.3
THERMAL = 0.2
HALINE = 0.15
GRAVITY_SCALE = 0.05
MIX_BOOST = 4.0
RICHARDSON = 1.0


def centre(extended):
    return extended[..., 1:-1, 1:-1]


def to_east(extended):
    return extended[..., 1:-1, 2:]


def to_west(extended):
    return extended[..., 1:-1, :-2]


def to_north(extended):
    return extended[..., 2:, 1:-1]


def to_south(extended):
    return extended[..., :-2, 1:-1]


def extend(quantity, rim_width):
    spec = [(0, 0)] * (quantity.ndim - 2) + [(rim_width, rim_width), (0, 0)]
    padded = jnp.pad(quantity, spec)
    return jnp.concatenate([padded[..., -rim_width:], padded, padded[..., :rim_width]], axis=-1)


def physics(extended, background):
    zonal_vel, merid_vel, temper, saline, viscosity, wetness = extended
    wet_mid = centre(wetness)
    mask_east = wet_mid * to_east(wetness)
    mask_west = to_west(wetness) * wet_mid
    mask_north = wet_mid * to_north(wetness)
    mask_south = to_south(wetness) * wet_mid
    flow_east = centre(zonal_vel) * mask_east
    flow_west = to_west(zonal_vel) * mask_west
    flow_north = centre(merid_vel) * mask_north
    flow_south = to_south(merid_vel) * mask_south
    divergence = (flow_east - flow_west) + (flow_north - flow_south)
    column_sum = jnp.cumsum(divergence[::-1], axis=0)[::-1]
    vertical = jnp.concatenate([jnp.zeros_like(column_sum[:1]), -column_sum[1:]], axis=0)
    visc_mid = centre(viscosity)
    coef_east = 0.5 * (visc_mid + to_east(viscosity)) * mask_east
    coef_west = 0.5 * (to_west(viscosity) + visc_mid) * mask_west
    coef_north = 0.5 * (visc_mid + to_north(viscosity)) * mask_north
    coef_south = 0.5 * (to_south(viscosity) + visc_mid) * mask_south

    def diffuse(quantity):
        middle = centre(quantity)
        return (coef_east * (to_east(quantity) - middle) - coef_west * (middle - to_west(quantity))
                + coef_north * (to_north(quantity) - middle) - coef_south * (middle - to_south(quantity)))

    density = HALINE * saline - THERMAL * temper
    pressure = GRAVITY_SCALE * jnp.cumsum(density * wetness, axis=0)
    press_mid = centre(pressure)
    zonal_new = (centre(zonal_vel) + TIME_STEP * (diffuse(zonal_vel) + CORIOLIS * centre(merid_vel)
                 - (to_east(pressure) - press_mid))) * mask_east
    merid_new = (centre(merid_vel) + TIME_STEP * (diffuse(merid_vel) - CORIOLIS * centre(zonal_vel)
                 - (to_north(pressure) - press_mid))) * mask_north
    temper_new = centre(temper) + TIME_STEP * diffuse(temper)
    saline_new = centre(saline) + TIME_STEP * diffuse(saline)
    temp_jump = THERMAL * (temper_new[:-1] - temper_new[1:])
    mixing = background[1:] * (1.0 + MIX_BOOST / (1.0 + RICHARDSON * temp_jump * temp_jump)) * wet_mid[1:]
    diffusivity = jnp.concatenate([jnp.zeros_like(mixing[:1]), mixing], axis=0)
    return (zonal_new, merid_new, temper_new, saline_new, vertical, diffusivity), (flow_east, flow_north, vertical, diffusivity)


def advect(tracer_ext, east_ext, north_ext, step_size):
    east_mid = centre(east_ext)
    east_side = to_west(east_ext)
    north_mid = centre(north_ext)
    north_side = to_south(north_ext)
    middle = centre(tracer_ext)
    flux_east = jnp.maximum(east_mid, 0.0) * middle + jnp.minimum(east_mid, 0.0) * to_east(tracer_ext)
    flux_west = jnp.maximum(east_side, 0.0) * to_west(tracer_ext) + jnp.minimum(east_side, 0.0) * middle
    flux_north = jnp.maximum(north_mid, 0.0) * middle + jnp.minimum(north_mid, 0.0) * to_north(tracer_ext)
    flux_south = jnp.maximum(north_side, 0.0) * to_south(tracer_ext) + jnp.minimum(north_side, 0.0) * middle
    return middle - step_size * ((flux_east - flux_west) + (flux_north - flux_south))


def vertical_factor(vertical, diffusivity):
    up_part = jnp.maximum(vertical, 0.0) + diffusivity
    down_part = jnp.minimum(vertical, 0.0) - diffusivity
    zero_row = jnp.zeros_like(up_part[:1])
    up_next = jnp.concatenate([up_part[1:], zero_row], axis=0)
    down_next = jnp.concatenate([down_part[1:], zero_row], axis=0)
    lower_band = TIME_STEP * down_part
    diagonal = 1.0 + TIME_STEP * (up_part - down_next)
    upper_band = -TIME_STEP * up_next
    ratios = []
    inverses = []
    for index_k in range(vertical.shape[0]):
        pivot_value = diagonal[index_k]
        if index_k > 0:
            pivot_value = pivot_value - lower_band[index_k] * ratios[-1]
        inverse = 1.0 / pivot_value
        ratios.append(upper_band[index_k] * inverse)
        inverses.append(inverse)
    return lower_band, ratios, inverses


def thomas_solve(lower_band, ratios, inverses, rhs):
    level_count = rhs.shape[-2]
    forward = [rhs[..., 0, :] * inverses[0]]
    for index_k in range(1, level_count):
        forward.append((rhs[..., index_k, :] - lower_band[index_k] * forward[-1]) * inverses[index_k])
    result = [forward[-1]]
    for index_k in range(level_count - 2, -1, -1):
        result.append(forward[index_k] - ratios[index_k] * result[-1])
    return jnp.stack(result[::-1], axis=-2)


def reference(fields, levels):
    depth_ids = lax.broadcasted_iota(jnp.int32, (LEV, NLAT, NLON), 0)
    wetness = (depth_ids < levels[None]).astype(jnp.float32)
    dyn_slot = fields[0]
    extended = extend(jnp.concatenate([dyn_slot[:5], wetness[None]], axis=0), 1)
    outputs, flow_parts = physics(extended, dyn_slot[5])
    flow_east, flow_north, vertical, diffusivity = flow_parts
    east_ext = extend(flow_east, 1)
    north_ext = extend(flow_north, 1)
    all_cols = NLAT * NLON
    lower_band, ratios, inverses = vertical_factor(vertical.reshape(LEV, all_cols), diffusivity.reshape(LEV, all_cols))

    def one_tracer(tracer):
        current = tracer
        for substep in range(NSUB):
            current = advect(extend(current, 1), east_ext, north_ext, TIME_STEP / NSUB)
        settled = thomas_solve(lower_band, ratios, inverses, current.reshape(LEV, all_cols))
        return settled.reshape(LEV, NLAT, NLON) * wetness

    tracers = fields[1:].reshape((N_SECT - 1) * NF, LEV, NLAT, NLON)
    advanced = lax.map(one_tracer, tracers).reshape(N_SECT - 1, NF, LEV, NLAT, NLON)
    return jnp.concatenate([jnp.stack(outputs)[None], advanced], axis=0)
```

```python
import functools
import jax
import jax.numpy as jnp
from jax import lax
from jax.experimental import pallas as pl
from jax.experimental.pallas import tpu as pltpu
from jax.sharding import PartitionSpec as P

NSUB = 2
TIME_STEP = 1.0
CORIOLIS = 0.3
THERMAL = 0.2
HALINE = 0.15
GRAVITY_SCALE = 0.05
MIX_BOOST = 4.0
RICHARDSON = 1.0

VMEM_LIMIT = 8 * 1024 * 1024

ZONAL_ROW, MERID_ROW, MERID_ROW2, TEMPER_ROW, VISC_ROW = range(5)


def call_kernel(body, outputs, inputs, scratch=()):
    in_vmem = pl.BlockSpec(memory_space=pltpu.VMEM)
    return pl.pallas_call(
        body,
        out_shape=[jax.ShapeDtypeStruct(shape, jnp.float32) for shape in outputs],
        in_specs=[in_vmem] * len(inputs),
        out_specs=[in_vmem] * len(outputs),
        scratch_shapes=[pltpu.VMEM(shape, jnp.float32) for shape in scratch],
        compiler_params=pltpu.CompilerParams(vmem_limit_bytes=VMEM_LIMIT),
    )(*inputs)


class Sizes:
    def __init__(self, fields, levels):
        self.nf, self.lev = fields.shape[1], fields.shape[2]
        self.rows, self.cols = levels.shape
        self.slab = self.lev * self.rows


def lane_ids(shape):
    return lax.broadcasted_iota(jnp.int32, shape, 1)


def row_ids(shape):
    return lax.broadcasted_iota(jnp.int32, shape, 0)


def turn(value, shift, axis):
    size = value.shape[axis]
    shift = shift % size
    return value if shift == 0 else pltpu.roll(value, shift, axis)


def to_lane(value, source, target):
    return turn(value, target - source, 1)


def level_rows(ref, first, row, sz):
    return ref[pl.ds(first + row, sz.lev, stride=sz.rows), :]


def pack_rows(sz, fields, levels, row_a, row_b, cross_a, cross_b, bulk):
    lev = levels[...].astype(jnp.float32)
    even = lax.axis_index("lat") % 2 == 0
    top, second = sz.rows - 1, sz.rows - 2

    def fill(message, cross, near, far):
        for f in range(sz.nf):
            for r, row in enumerate((near, far)):
                at = (2 * f + r) * sz.lev
                message[at : at + sz.lev, :] = level_rows(fields, f * sz.slab, row, sz)
        at = 2 * sz.nf * sz.lev
        message[at : at + 1, :] = lev[near : near + 1, :]
        message[at + 1 : at + 2, :] = lev[far : far + 1, :]
        message[at + 2 : at + 8, :] = jnp.zeros((6, sz.cols), jnp.float32)
        for at, (f, row) in enumerate(((0, near), (1, near), (1, far), (2, near), (4, near))):
            cross[at * sz.lev : (at + 1) * sz.lev, :] = level_rows(fields, f * sz.slab, row, sz)

    @pl.when(even)
    def _():
        fill(row_a, cross_a, top, second)
        fill(row_b, cross_b, 0, 1)

    @pl.when(jnp.logical_not(even))
    def _():
        fill(row_a, cross_a, 0, 1)
        fill(row_b, cross_b, top, second)

    bulk[0 : 2 * sz.slab, :] = fields[0 : 2 * sz.slab, :]
    lane = lane_ids((sz.rows, sz.cols))
    west = jnp.zeros((sz.rows, sz.cols), jnp.float32)
    east = west
    last = sz.cols - 1
    for t, f in enumerate((2, 4)):
        for k in range(sz.lev):
            lane_at = t * sz.lev + k
            at = f * sz.slab + k * sz.rows
            moved = to_lane(fields[at : at + sz.rows, :], last, lane_at)
            east = jnp.where(lane == lane_at, moved, east)
            west = jnp.where(lane == lane_at + 1, moved, west)
    bulk[2 * sz.slab : 2 * sz.slab + sz.rows, :] = jnp.where(
        lane < 2 * sz.lev, turn(west, -1, 1), turn(east, 2 * sz.lev, 1)
    )


def pack_columns(
    sz, fields, levels, row_a, row_b, cross_a, cross_b, bulk,
    to_east, to_west, south, north, cross_south, cross_north, bulk_two,
):
    position = lax.axis_index("lat")
    even = position % 2 == 0
    has_south = position > 0
    has_north = position < lax.axis_size("lat") - 1
    for low, high, from_a, from_b in ((south, north, row_a, row_b), (cross_south, cross_north, cross_a, cross_b)):
        first, other = from_a[...], from_b[...]
        low[...] = jnp.where(has_south, jnp.where(even, other, first), 0.0)
        high[...] = jnp.where(has_north, jnp.where(even, first, other), 0.0)

    for at, f in enumerate((2, 4, 5)):
        bulk_two[at * sz.slab : (at + 1) * sz.slab, :] = fields[f * sz.slab : (f + 1) * sz.slab, :]

    tile = (sz.rows, sz.cols)
    lane = lane_ids(tile)
    zero = jnp.zeros(tile, jnp.float32)
    last = sz.cols - 1
    east_one, west_one, west_two, east_two = zero, zero, zero, zero
    for f in range(sz.nf + 2):
        for k in range(sz.lev):
            if f < sz.nf:
                at = f * sz.slab + k * sz.rows
                values = fields[at : at + sz.rows, :]
            else:
                at = (f - sz.nf) * sz.slab + k * sz.rows
                values = bulk[at : at + sz.rows, :]
            p = f * sz.lev + k
            moved = to_lane(values, last, p)
            east_one = jnp.where(lane == p, moved, east_one)
            west_one = jnp.where(lane == (p + 1) % sz.cols, moved, west_one)
            if f <= sz.nf:
                west_two = jnp.where(lane == (p + 2) % sz.cols, moved, west_two)
                east_two = jnp.where(lane == (p - 1) % sz.cols, moved, east_two)
    to_east[0 : sz.rows, :] = east_one
    to_east[sz.rows : 2 * sz.rows, :] = turn(east_two, 1, 1)
    to_west[0 : sz.rows, :] = turn(west_one, -1, 1)
    to_west[sz.rows : 2 * sz.rows, :] = turn(west_two, -2, 1)

    lev = levels[...].astype(jnp.float32)
    side = bulk[2 * sz.slab : 2 * sz.slab + sz.rows, :]
    level_row = 2 * sz.nf * sz.lev
    south_lev = south[level_row : level_row + 1, :]
    north_lev = north[level_row : level_row + 1, :]
    base = 2 * sz.lev
    for message, near, far, shift in ((to_east, last, last - 1, -base), (to_west, 0, 1, 0)):
        part = turn(side, shift, 1)
        part = jnp.where(lane == base, to_lane(lev, near, base), part)
        part = jnp.where(lane == base + 1, to_lane(lev, far, base + 1), part)
        low = jnp.broadcast_to(to_lane(south_lev, near, base + 2), tile)
        high = jnp.broadcast_to(to_lane(north_lev, near, base + 3), tile)
        part = jnp.where(lane == base + 2, low, part)
        part = jnp.where(lane == base + 3, high, part)
        message[2 * sz.rows : 3 * sz.rows, :] = part

    tall = (sz.lev, sz.cols)
    tall_lane = lane_ids(tall)
    east_corner = jnp.zeros(tall, jnp.float32)
    west_corner = east_corner
    for r, (rows, cross) in enumerate(((south, cross_south), (north, cross_north))):
        for f in range(sz.nf + 2):
            if f < sz.nf:
                values = rows[2 * f * sz.lev : (2 * f + 1) * sz.lev, :]
            else:
                at = (ZONAL_ROW, MERID_ROW)[f - sz.nf] * sz.lev
                values = cross[at : at + sz.lev, :]
            p = r * (sz.nf + 2) + f
            moved = to_lane(values, last, p)
            east_corner = jnp.where(tall_lane == p, moved, east_corner)
            west_corner = jnp.where(tall_lane == p + 1, moved, west_corner)
    to_east[3 * sz.rows : 3 * sz.rows + sz.lev, :] = east_corner
    to_west[3 * sz.rows : 3 * sz.rows + sz.lev, :] = turn(west_corner, -1, 1)


def shift_west(value, lane, edge):
    return jnp.where(lane == 0, edge, turn(value, 1, 1))


def shift_east(value, lane, edge):
    return jnp.where(lane == value.shape[1] - 1, edge, turn(value, -1, 1))


def shift_south(value, row, edge):
    return jnp.where(row == 0, edge, turn(value, 1, 0))


def shift_north(value, row, edge):
    return jnp.where(row == value.shape[0] - 1, edge, turn(value, -1, 0))


class Weights:
    def __init__(self, east, west, north, south, step):
        self.own = 1.0 - step * (
            jnp.maximum(east, 0.0) - jnp.minimum(west, 0.0) + (jnp.maximum(north, 0.0) - jnp.minimum(south, 0.0))
        )
        self.east = -step * jnp.minimum(east, 0.0)
        self.west = step * jnp.maximum(west, 0.0)
        self.north = -step * jnp.minimum(north, 0.0)
        self.south = step * jnp.maximum(south, 0.0)

    def apply(self, own, east, west, north, south):
        return self.own * own + self.east * east + self.west * west + (self.north * north + self.south * south)


def finish(
    sz, fields, levels, south, north, cross_south, cross_north, bulk, bulk_two,
    own_east, own_west, from_west, from_east,
    out, div, mix, vert, low_strip, high_strip, side_strips, ratio, forward,
):
    tile = (sz.rows, sz.cols)
    lane, row = lane_ids(tile), row_ids(tile)
    last_lane, last_row = sz.cols - 1, sz.rows - 1
    lev = levels[...].astype(jnp.float32)
    level_row = 2 * sz.nf * sz.lev
    side_base = 2 * sz.lev
    west_side = from_west[2 * sz.rows : 3 * sz.rows, :]
    east_side = from_east[2 * sz.rows : 3 * sz.rows, :]
    lev_w = shift_west(lev, lane, to_lane(west_side, side_base, 0))
    lev_e = shift_east(lev, lane, to_lane(east_side, side_base, last_lane))
    south_lev, north_lev = south[level_row : level_row + 1, :], north[level_row : level_row + 1, :]
    lev_s = shift_south(lev, row, south_lev)
    lev_n = shift_north(lev, row, north_lev)

    def masks(k):
        wet = lev > k
        return wet, wet & (lev_e > k), wet & (lev_w > k), wet & (lev_n > k), wet & (lev_s > k)

    def keep(mask, value):
        return jnp.where(mask, value, 0.0)

    is_dynamics = lax.axis_index("sect") == 0

    def physics(full):
        cross_of = {0: ZONAL_ROW, 1: MERID_ROW, 2: TEMPER_ROW, 4: VISC_ROW}

        def own(f, k):
            at = k * sz.rows
            if full:
                return fields[f * sz.slab + at : f * sz.slab + at + sz.rows, :]
            if f < 2:
                return bulk[f * sz.slab + at : f * sz.slab + at + sz.rows, :]
            at += {2: 0, 4: 1, 5: 2}[f] * sz.slab
            return bulk_two[at : at + sz.rows, :]

        def beyond_row(f, k, ref, cross):
            if full:
                at = 2 * f * sz.lev + k
                return ref[at : at + 1, :]
            at = cross_of[f] * sz.lev + k
            return cross[at : at + 1, :]

        def beyond_column(f, k, message, target):
            if full:
                return to_lane(message[0 : sz.rows, :], f * sz.lev + k, target)
            if f < 2:
                return to_lane(message[0 : sz.rows, :], (sz.nf + f) * sz.lev + k, target)
            return to_lane(message[2 * sz.rows : 3 * sz.rows, :], {2: 0, 4: 1}[f] * sz.lev + k, target)

        def west_of(value, f, k):
            return shift_west(value, lane, beyond_column(f, k, from_west, 0))

        def east_of(value, f, k):
            return shift_east(value, lane, beyond_column(f, k, from_east, last_lane))

        def south_of(value, f, k):
            return shift_south(value, row, beyond_row(f, k, south, cross_south))

        def north_of(value, f, k):
            return shift_north(value, row, beyond_row(f, k, north, cross_north))

        def around(f, k):
            value = own(f, k)
            return value, east_of(value, f, k), west_of(value, f, k), north_of(value, f, k), south_of(value, f, k)

        press = jnp.zeros(tile, jnp.float32)
        press_e, press_n, warm_above = press, press, press
        for k in range(sz.lev):
            at = k * sz.rows
            wet, wet_e, wet_w, wet_n, wet_s = masks(k)
            if full:
                zonal = around(0, k)
                merid = around(1, k)
                zonal_mid, zonal_west, merid_mid, merid_south = zonal[0], zonal[2], merid[0], merid[4]
            else:
                zonal_mid, merid_mid = own(0, k), own(1, k)
                zonal_west, merid_south = west_of(zonal_mid, 0, k), south_of(merid_mid, 1, k)
            flow_east, flow_west = keep(wet_e, zonal_mid), keep(wet_w, zonal_west)
            flow_north, flow_south = keep(wet_n, merid_mid), keep(wet_s, merid_south)
            div[at : at + sz.rows, :] = flow_east - flow_west + (flow_north - flow_south)
            visc, visc_e, visc_w, visc_n, visc_s = around(4, k)
            coef_e = keep(wet_e, 0.5 * (visc + visc_e))
            coef_w = keep(wet_w, 0.5 * (visc_w + visc))
            coef_n = keep(wet_n, 0.5 * (visc + visc_n))
            coef_s = keep(wet_s, 0.5 * (visc_s + visc))

            def diffuse(parts):
                mid, e, w, n, s = parts
                return coef_e * (e - mid) - coef_w * (mid - w) + coef_n * (n - mid) - coef_s * (mid - s)

            temper = around(2, k)
            warm = temper[0] + TIME_STEP * diffuse(temper)
            if k == 0:
                mixing = jnp.zeros(tile, jnp.float32)
            else:
                jump = THERMAL * (warm_above - warm)
                mixing = keep(wet, own(5, k) * (1.0 + MIX_BOOST / (1.0 + RICHARDSON * jump * jump)))
            warm_above = warm
            if not full:
                mix[at : at + sz.rows, :] = mixing
                continue
            saline = around(3, k)

            def weight(place, mask):
                return keep(mask, HALINE * saline[place] - THERMAL * temper[place])

            press = press + GRAVITY_SCALE * weight(0, wet)
            press_e = press_e + GRAVITY_SCALE * weight(1, lev_e > k)
            press_n = press_n + GRAVITY_SCALE * weight(3, lev_n > k)
            zonal_new = zonal_mid + TIME_STEP * (diffuse(zonal) + CORIOLIS * merid_mid - (press_e - press))
            merid_new = merid_mid + TIME_STEP * (diffuse(merid) - CORIOLIS * zonal_mid - (press_n - press))
            out[at : at + sz.rows, :] = keep(wet_e, zonal_new)
            out[sz.slab + at : sz.slab + at + sz.rows, :] = keep(wet_n, merid_new)
            out[2 * sz.slab + at : 2 * sz.slab + at + sz.rows, :] = warm
            out[3 * sz.slab + at : 3 * sz.slab + at + sz.rows, :] = saline[0] + TIME_STEP * diffuse(saline)
            out[5 * sz.slab + at : 5 * sz.slab + at + sz.rows, :] = mixing
        total = jnp.zeros(tile, jnp.float32)
        for k in range(sz.lev - 1, -1, -1):
            at = k * sz.rows
            total = total + div[at : at + sz.rows, :]
            value = -total if k > 0 else jnp.zeros(tile, jnp.float32)
            if full:
                out[4 * sz.slab + at : 4 * sz.slab + at + sz.rows, :] = value
            else:
                vert[at : at + sz.rows, :] = value

    def row_strips(step):
        tall = (sz.lev, sz.cols)
        lane16, depth = lane_ids(tall), row_ids(tall).astype(jnp.float32)

        def wet(levels_row):
            return levels_row > depth

        west_corner = from_west[3 * sz.rows : 3 * sz.rows + sz.lev, :]
        east_corner = from_east[3 * sz.rows : 3 * sz.rows + sz.lev, :]
        lane1 = lane_ids((1, sz.cols))
        for r in range(2):
            rows, cross = (south, cross_south) if r == 0 else (north, cross_north)
            strip = low_strip if r == 0 else high_strip
            edge = 0 if r == 0 else last_row
            near_lev = rows[level_row : level_row + 1, :]
            far_lev = rows[level_row + 1 : level_row + 2, :]
            own_lev = lev[edge : edge + 1, :]
            corner_lane = side_base + 2 + r
            lev_at_w = shift_west(near_lev, lane1, to_lane(west_side[0:1, :], corner_lane, 0))
            lev_at_e = shift_east(near_lev, lane1, to_lane(east_side[0:1, :], corner_lane, last_lane))
            wet_near = wet(near_lev)
            zonal = cross[ZONAL_ROW * sz.lev : (ZONAL_ROW + 1) * sz.lev, :]
            p = r * (sz.nf + 2)
            zonal_w = shift_west(zonal, lane16, to_lane(west_corner, p + sz.nf, 0))
            flow_e = keep(wet_near & wet(lev_at_e), zonal)
            flow_w = keep(wet_near & wet(lev_at_w), zonal_w)
            merid = cross[MERID_ROW * sz.lev : (MERID_ROW + 1) * sz.lev, :]
            if r == 0:
                merid_far = cross[MERID_ROW2 * sz.lev : (MERID_ROW2 + 1) * sz.lev, :]
                flow_n = keep(wet_near & wet(own_lev), merid)
                flow_s = keep(wet_near & wet(far_lev), merid_far)
            else:
                flow_n = keep(wet_near & wet(far_lev), merid)
                flow_s = keep(wet_near & wet(own_lev), level_rows(bulk, sz.slab, last_row, sz))
            weights = Weights(flow_e, flow_w, flow_n, flow_s, step)
            for f in range(sz.nf):
                at = 2 * f * sz.lev
                near, far = rows[at : at + sz.lev, :], rows[at + sz.lev : at + 2 * sz.lev, :]
                inside = level_rows(fields, f * sz.slab, edge, sz)
                at_w = shift_west(near, lane16, to_lane(west_corner, p + f, 0))
                at_e = shift_east(near, lane16, to_lane(east_corner, p + f, last_lane))
                up, down = (inside, far) if r == 0 else (far, inside)
                strip[f * sz.lev : (f + 1) * sz.lev, :] = weights.apply(near, at_e, at_w, up, down)

    def column_strips(step):
        tall = (sz.lev, sz.cols)
        lane16, depth16 = lane_ids(tall), row_ids(tall)
        depth = (lane % sz.lev).astype(jnp.float32)

        def column(value, at):
            return jnp.broadcast_to(value[:, at : at + 1], tile)

        def all_fields(value, first):
            value = jnp.where((lane >= first) & (lane < first + sz.lev), value, 0.0)
            width = sz.lev
            while width < sz.cols:
                value = value + turn(value, width, 1)
                width *= 2
            return value

        def corner_rows(message, r):
            items = message[3 * sz.rows : 3 * sz.rows + sz.lev, :]
            p = r * (sz.nf + 2)
            tracers = jnp.zeros(tall, jnp.float32)
            for f in range(sz.nf):
                spread = jnp.broadcast_to(items[:, p + f : p + f + 1], tall)
                tracers = jnp.where(lane16 == f * sz.lev + depth16, spread, tracers)
            spread = jnp.broadcast_to(items[:, p + sz.nf + 1 : p + sz.nf + 2], tall)
            velocity = jnp.where(lane16 % sz.lev == depth16, spread, 0.0)
            return jnp.sum(tracers, axis=0, keepdims=True), jnp.sum(velocity, axis=0, keepdims=True)

        for side in range(2):
            message, own_message = (from_west, own_west) if side == 0 else (from_east, own_east)
            edge = 0 if side == 0 else last_lane
            aside = west_side if side == 0 else east_side
            near, far = message[0 : sz.rows, :], message[sz.rows : 2 * sz.rows, :]
            inside = own_message[0 : sz.rows, :]
            low_tracers, low_merid = corner_rows(message, 0)
            high_tracers, _ = corner_rows(message, 1)
            near_lev, far_lev = column(aside, side_base), column(aside, side_base + 1)
            own_lev = column(lev, edge)
            lev_at_s = shift_south(near_lev, row, column(aside, side_base + 2))
            lev_at_n = shift_north(near_lev, row, column(aside, side_base + 3))
            wet_near = near_lev > depth
            zonal_first = sz.nf * sz.lev
            if side == 0:
                flow_e = keep(wet_near & (own_lev > depth), all_fields(near, zonal_first))
                flow_w = keep(wet_near & (far_lev > depth), all_fields(far, zonal_first))
            else:
                flow_e = keep(wet_near & (far_lev > depth), all_fields(near, zonal_first))
                flow_w = keep(wet_near & (own_lev > depth), all_fields(inside, zonal_first))
            merid = all_fields(near, zonal_first + sz.lev)
            merid_s = shift_south(merid, row, low_merid)
            flow_n = keep(wet_near & (lev_at_n > depth), merid)
            flow_s = keep(wet_near & (lev_at_s > depth), merid_s)
            at_s = shift_south(near, row, low_tracers)
            at_n = shift_north(near, row, high_tracers)
            east, west = (inside, far) if side == 0 else (far, inside)
            weights = Weights(flow_e, flow_w, flow_n, flow_s, step)
            side_strips[side * sz.rows : (side + 1) * sz.rows, :] = weights.apply(near, east, west, at_n, at_s)

    def transport(step):
        west_old, east_old = from_west[0 : sz.rows, :], from_east[0 : sz.rows, :]
        west_new, east_new = side_strips[0 : sz.rows, :], side_strips[sz.rows : 2 * sz.rows, :]
        zero = jnp.zeros(tile, jnp.float32)

        def faces(k):
            if k == sz.lev:
                return zero, zero
            at = k * sz.rows
            speed, mixing = vert[at : at + sz.rows, :], mix[at : at + sz.rows, :]
            return jnp.maximum(speed, 0.0) + mixing, jnp.minimum(speed, 0.0) - mixing

        previous = [None] * sz.nf
        last_ratio = None
        up, down = faces(0)
        for k in range(sz.lev):
            at = k * sz.rows
            wet, wet_e, wet_w, wet_n, wet_s = masks(k)
            zonal, merid = bulk[at : at + sz.rows, :], bulk[sz.slab + at : sz.slab + at + sz.rows, :]
            zonal_first = sz.nf * sz.lev
            zonal_west = shift_west(zonal, lane, to_lane(west_old, zonal_first + k, 0))
            beyond = MERID_ROW * sz.lev + k
            merid_south = shift_south(merid, row, cross_south[beyond : beyond + 1, :])
            weights = Weights(
                keep(wet_e, zonal), keep(wet_w, zonal_west), keep(wet_n, merid), keep(wet_s, merid_south), step
            )
            up_next, down_next = faces(k + 1)
            pivot = 1.0 + TIME_STEP * (up - down_next)
            lower = TIME_STEP * down
            if k > 0:
                pivot = pivot - lower * last_ratio
            inverse = 1.0 / pivot
            last_ratio = -TIME_STEP * up_next * inverse
            ratio[at : at + sz.rows, :] = last_ratio
            up, down = up_next, down_next
            for f in range(sz.nf):
                p = f * sz.lev + k
                value = fields[f * sz.slab + at : f * sz.slab + at + sz.rows, :]
                near = 2 * f * sz.lev + k
                for west, east, low, high in (
                    (west_old, east_old, south[near : near + 1, :], north[near : near + 1, :]),
                    (west_new, east_new, low_strip[p : p + 1, :], high_strip[p : p + 1, :]),
                ):
                    value = weights.apply(
                        value,
                        shift_east(value, lane, to_lane(east, p, last_lane)),
                        shift_west(value, lane, to_lane(west, p, 0)),
                        shift_north(value, row, high),
                        shift_south(value, row, low),
                    )
                if k > 0:
                    value = value - lower * previous[f]
                value = value * inverse
                previous[f] = value
                forward[f * sz.slab + at : f * sz.slab + at + sz.rows, :] = value
        for k in range(sz.lev - 1, -1, -1):
            at = k * sz.rows
            wet = lev > k
            for f in range(sz.nf):
                here = f * sz.slab + at
                if k < sz.lev - 1:
                    previous[f] = forward[here : here + sz.rows, :] - ratio[at : at + sz.rows, :] * previous[f]
                out[here : here + sz.rows, :] = keep(wet, previous[f])

    @pl.when(is_dynamics)
    def _():
        physics(True)

    @pl.when(jnp.logical_not(is_dynamics))
    def _():
        step = TIME_STEP / NSUB
        row_strips(step)
        column_strips(step)
        physics(False)
        transport(step)


def pair_of(index, count, odd):
    if not odd:
        return index ^ 1
    return (((index + 1) ^ 1) - 1) % count


def on_device(sizes_of, fields, levels):
    sz = Sizes(fields, levels)
    count_s, count_o, count_a = sizes_of
    flat = fields.reshape(sz.nf * sz.slab, sz.cols)
    axes = ("sect", "lon", "lat")

    def swap(value, odd):
        pairs = [(i, pair_of(i, count_a, odd)) for i in range(count_a)]
        return lax.ppermute(value, "lat", pairs)

    def from_dynamics(value, odd=None):
        mine = lax.axis_index("sect")
        got = None
        for hop in range(1, count_s):
            pairs = []
            for s in range(count_s):
                for o in range(count_o):
                    for a in range(count_a):
                        b = a if odd is None else pair_of(a, count_a, odd)
                        pairs.append(((s * count_o + o) * count_a + a, (((s + hop) % count_s) * count_o + o) * count_a + b))
            if odd is None:
                part = lax.ppermute(value, "sect", [(s, (s + hop) % count_s) for s in range(count_s)])
            else:
                part = lax.ppermute(value, axes, pairs)
            got = part if got is None else jnp.where(mine == hop, part, got)
        return got

    def around(value, step):
        return lax.ppermute(value, "lon", [(i, (i + step) % count_o) for i in range(count_o)])

    rows_shape = ((2 * sz.nf * sz.lev + 8), sz.cols)
    cross_shape = (5 * sz.lev, sz.cols)
    columns_shape = (3 * sz.rows + sz.lev, sz.cols)
    row_a, row_b, cross_a, cross_b, bulk = call_kernel(
        functools.partial(pack_rows, sz),
        [rows_shape, rows_shape, cross_shape, cross_shape, (2 * sz.slab + sz.rows, sz.cols)],
        [flat, levels],
    )
    bulk = from_dynamics(bulk)
    cross_b = from_dynamics(cross_b, True)
    row_b = swap(row_b, True)
    cross_a = from_dynamics(cross_a, False)
    row_a = swap(row_a, False)
    to_east, to_west, south, north, cross_south, cross_north, bulk_two = call_kernel(
        functools.partial(pack_columns, sz),
        [columns_shape] * 2 + [rows_shape] * 2 + [cross_shape] * 2 + [(3 * sz.slab, sz.cols)],
        [flat, levels, row_a, row_b, cross_a, cross_b, bulk],
    )
    bulk_two = from_dynamics(bulk_two)
    from_east = around(to_west, -1)
    from_west = around(to_east, 1)
    slab = (sz.slab, sz.cols)
    (out,) = call_kernel(
        functools.partial(finish, sz),
        [flat.shape],
        [flat, levels, south, north, cross_south, cross_north, bulk, bulk_two, to_east, to_west, from_west, from_east],
        [slab, slab, slab, (sz.nf * sz.lev, sz.cols), (sz.nf * sz.lev, sz.cols), (2 * sz.rows, sz.cols), slab, flat.shape],
    )
    return out.reshape(fields.shape)


def solution(mesh):
    sizes_of = (mesh.shape["sect"], mesh.shape["lon"], mesh.shape["lat"])
    return jax.shard_map(
        functools.partial(on_device, sizes_of),
        mesh=mesh,
        in_specs=(P("sect", None, None, "lat", "lon"), P("lat", "lon")),
        out_specs=P("sect", None, None, "lat", "lon"),
        check_vma=False,
    )
```

```python
import functools
import jax
import jax.numpy as jnp
from jax import lax
from jax.experimental import pallas as pl
from jax.experimental.pallas import tpu as pltpu
from jax.sharding import PartitionSpec as P

NSUB = 2
TIME_STEP = 1.0
CORIOLIS = 0.3
THERMAL = 0.2
HALINE = 0.15
GRAVITY_SCALE = 0.05
MIX_BOOST = 4.0
RICHARDSON = 1.0

VMEM_LIMIT = 8 * 1024 * 1024

ZONAL_ROW, MERID_ROW, MERID_ROW2, TEMPER_ROW, VISC_ROW, LEVEL_ROW = range(6)


def call_kernel(body, outputs, inputs, scratch=()):
    in_vmem = pl.BlockSpec(memory_space=pltpu.VMEM)
    return pl.pallas_call(
        body,
        out_shape=[jax.ShapeDtypeStruct(shape, jnp.float32) for shape in outputs],
        in_specs=[in_vmem] * len(inputs),
        out_specs=[in_vmem] * len(outputs),
        scratch_shapes=[pltpu.VMEM(shape, jnp.float32) for shape in scratch],
        compiler_params=pltpu.CompilerParams(vmem_limit_bytes=VMEM_LIMIT),
    )(*inputs)


class Sizes:
    def __init__(self, fields, levels):
        self.nf, self.lev = fields.shape[1], fields.shape[2]
        self.rows, self.cols = levels.shape
        self.slab = self.lev * self.rows


def lane_ids(shape):
    return lax.broadcasted_iota(jnp.int32, shape, 1)


def row_ids(shape):
    return lax.broadcasted_iota(jnp.int32, shape, 0)


def turn(value, shift, axis):
    size = value.shape[axis]
    shift = shift % size
    return value if shift == 0 else pltpu.roll(value, shift, axis)


def to_lane(value, source, target):
    return turn(value, target - source, 1)


def level_rows(ref, first, row, sz):
    return ref[pl.ds(first + row, sz.lev, stride=sz.rows), :]


def send_north_first(sz, fill):
    even = lax.axis_index("lat") % 2 == 0
    top, second = sz.rows - 1, sz.rows - 2

    @pl.when(even)
    def _():
        fill(0, top, second)
        fill(1, 0, 1)

    @pl.when(jnp.logical_not(even))
    def _():
        fill(0, 0, 1)
        fill(1, top, second)


def pack_edges(sz, fields, row_a, row_b, side):
    def fill(which, near, far):
        message = (row_a, row_b)[which]
        for f in range(sz.nf):
            for r, row in enumerate((near, far)):
                at = (2 * f + r) * sz.lev
                message[at : at + sz.lev, :] = level_rows(fields, f * sz.slab, row, sz)

    send_north_first(sz, fill)
    for place, column in enumerate(edge_columns(sz, fields, sz.nf, 0)):
        side[place * sz.rows : (place + 1) * sz.rows, :] = column


def pack_cross(sz, fields, levels, cross_a, cross_b):
    lev = levels[...].astype(jnp.float32)

    def fill(which, near, far):
        cross = (cross_a, cross_b)[which]
        for at, (f, row) in enumerate(((0, near), (1, near), (1, far), (2, near), (4, near))):
            cross[at * sz.lev : (at + 1) * sz.lev, :] = level_rows(fields, f * sz.slab, row, sz)
        at = LEVEL_ROW * sz.lev
        cross[at : at + 1, :] = lev[near : near + 1, :]
        cross[at + 1 : at + 2, :] = lev[far : far + 1, :]
        cross[at + 2 : at + 8, :] = jnp.zeros((6, sz.cols), jnp.float32)

    send_north_first(sz, fill)


def edge_columns(sz, ref, count, first):
    tile = (sz.rows, sz.cols)
    lane = lane_ids(tile)
    zero = jnp.zeros(tile, jnp.float32)
    last = sz.cols - 1
    east_one, west_one, east_two, west_two = zero, zero, zero, zero
    for f in range(count):
        for k in range(sz.lev):
            at = f * sz.slab + k * sz.rows
            p = (first + f) * sz.lev + k
            moved = to_lane(ref[at : at + sz.rows, :], last, p)
            east_one = jnp.where(lane == p, moved, east_one)
            west_one = jnp.where(lane == (p + 1) % sz.cols, moved, west_one)
            west_two = jnp.where(lane == (p + 2) % sz.cols, moved, west_two)
            east_two = jnp.where(lane == (p - 1) % sz.cols, moved, east_two)
    return east_one, turn(west_one, -1, 1), turn(east_two, 1, 1), turn(west_two, -2, 1)


def pack_columns(
    sz, fields, levels, row_a, row_b, cross_a, cross_b, own_side, side,
    to_east, to_west, south, north, cross_south, cross_north, bulk,
):
    position = lax.axis_index("lat")
    even = position % 2 == 0
    has_south = position > 0
    has_north = position < lax.axis_size("lat") - 1
    for low, high, from_a, from_b in ((south, north, row_a, row_b), (cross_south, cross_north, cross_a, cross_b)):
        first, other = from_a[...], from_b[...]
        low[...] = jnp.where(has_south, jnp.where(even, other, first), 0.0)
        high[...] = jnp.where(has_north, jnp.where(even, first, other), 0.0)

    tile = (sz.rows, sz.cols)
    lane = lane_ids(tile)
    last = sz.cols - 1
    bulk[0 : 2 * sz.slab, :] = fields[0 : 2 * sz.slab, :]
    tracer_lanes = lane < sz.nf * sz.lev
    for place, (message, at) in enumerate(((to_east, 0), (to_west, 0), (to_east, sz.rows), (to_west, sz.rows))):
        own = own_side[place * sz.rows : (place + 1) * sz.rows, :]
        dynamics = side[place * sz.rows : (place + 1) * sz.rows, :]
        message[at : at + sz.rows, :] = jnp.where(tracer_lanes, own, turn(dynamics, sz.nf * sz.lev, 1))

    lev = levels[...].astype(jnp.float32)
    level_row = LEVEL_ROW * sz.lev
    south_lev = cross_south[level_row : level_row + 1, :]
    north_lev = cross_north[level_row : level_row + 1, :]
    base = 2 * sz.lev
    for place, (message, near, far) in enumerate(((to_east, last, last - 1), (to_west, 0, 1))):
        part = side[place * sz.rows : (place + 1) * sz.rows, :]
        part = jnp.where(lane < sz.lev, turn(part, -2 * sz.lev, 1), turn(part, -3 * sz.lev, 1))
        part = jnp.where(lane == base, to_lane(lev, near, base), part)
        part = jnp.where(lane == base + 1, to_lane(lev, far, base + 1), part)
        low = jnp.broadcast_to(to_lane(south_lev, near, base + 2), tile)
        high = jnp.broadcast_to(to_lane(north_lev, near, base + 3), tile)
        part = jnp.where(lane == base + 2, low, part)
        part = jnp.where(lane == base + 3, high, part)
        message[2 * sz.rows : 3 * sz.rows, :] = part

    tall = (sz.lev, sz.cols)
    tall_lane = lane_ids(tall)
    east_corner = jnp.zeros(tall, jnp.float32)
    west_corner = east_corner
    for r, (rows, cross) in enumerate(((south, cross_south), (north, cross_north))):
        for f in range(sz.nf + 2):
            if f < sz.nf:
                values = rows[2 * f * sz.lev : (2 * f + 1) * sz.lev, :]
            else:
                at = (ZONAL_ROW, MERID_ROW)[f - sz.nf] * sz.lev
                values = cross[at : at + sz.lev, :]
            p = r * (sz.nf + 2) + f
            moved = to_lane(values, last, p)
            east_corner = jnp.where(tall_lane == p, moved, east_corner)
            west_corner = jnp.where(tall_lane == p + 1, moved, west_corner)
    to_east[3 * sz.rows : 3 * sz.rows + sz.lev, :] = east_corner
    to_west[3 * sz.rows : 3 * sz.rows + sz.lev, :] = turn(west_corner, -1, 1)

    @pl.when(lax.axis_index("sect") == 0)
    def _():
        row = row_ids(tile)
        lev_e, lev_w = turn(lev, -1, 1), turn(lev, 1, 1)
        lev_n, lev_s = shift_north(lev, row, north_lev), shift_south(lev, row, south_lev)
        warm_above = None
        for k in range(sz.lev):
            at = k * sz.rows

            def around(f):
                value = fields[f * sz.slab + at : f * sz.slab + at + sz.rows, :]
                beyond = 2 * f * sz.lev + k
                return (
                    value, turn(value, -1, 1), turn(value, 1, 1),
                    shift_north(value, row, north[beyond : beyond + 1, :]),
                    shift_south(value, row, south[beyond : beyond + 1, :]),
                )

            wet = lev > k
            masks = wet, wet & (lev_e > k), wet & (lev_w > k), wet & (lev_n > k), wet & (lev_s > k)
            warm = diffused(around(2), around(4), masks)
            background = fields[5 * sz.slab + at : 5 * sz.slab + at + sz.rows, :]
            mixing = jnp.zeros(tile, jnp.float32) if k == 0 else mixed(warm_above, warm, background, wet)
            warm_above = warm
            bulk[2 * sz.slab + at : 2 * sz.slab + at + sz.rows, :] = mixing


def keep(mask, value):
    return jnp.where(mask, value, 0.0)


def diffused(quantity, viscosity, masks):
    mid, e, w, n, s = quantity
    visc, visc_e, visc_w, visc_n, visc_s = viscosity
    _, wet_e, wet_w, wet_n, wet_s = masks
    change = (
        keep(wet_e, 0.5 * (visc + visc_e)) * (e - mid)
        - keep(wet_w, 0.5 * (visc_w + visc)) * (mid - w)
        + keep(wet_n, 0.5 * (visc + visc_n)) * (n - mid)
        - keep(wet_s, 0.5 * (visc_s + visc)) * (mid - s)
    )
    return mid + TIME_STEP * change


def mixed(warm_above, warm, background, wet):
    jump = THERMAL * (warm_above - warm)
    return keep(wet, background * (1.0 + MIX_BOOST / (1.0 + RICHARDSON * jump * jump)))


def shift_west(value, lane, edge):
    return jnp.where(lane == 0, edge, turn(value, 1, 1))


def shift_east(value, lane, edge):
    return jnp.where(lane == value.shape[1] - 1, edge, turn(value, -1, 1))


def shift_south(value, row, edge):
    return jnp.where(row == 0, edge, turn(value, 1, 0))


def shift_north(value, row, edge):
    return jnp.where(row == value.shape[0] - 1, edge, turn(value, -1, 0))


class Weights:
    def __init__(self, east, west, north, south, step):
        self.own = 1.0 - step * (
            jnp.maximum(east, 0.0) - jnp.minimum(west, 0.0) + (jnp.maximum(north, 0.0) - jnp.minimum(south, 0.0))
        )
        self.east = -step * jnp.minimum(east, 0.0)
        self.west = step * jnp.maximum(west, 0.0)
        self.north = -step * jnp.minimum(north, 0.0)
        self.south = step * jnp.maximum(south, 0.0)

    def parts(self):
        return self.own, self.east, self.west, self.north, self.south

    @classmethod
    def of(cls, own, east, west, north, south):
        weights = cls.__new__(cls)
        weights.own, weights.east, weights.west, weights.north, weights.south = own, east, west, north, south
        return weights

    def apply(self, own, east, west, north, south):
        return self.own * own + self.east * east + self.west * west + (self.north * north + self.south * south)


def finish(
    sz, fields, levels, south, north, cross_south, cross_north, bulk,
    own_east, own_west, side, from_west, from_east,
    out, div, mix, vert, low_strip, high_strip, side_strips, ratio, forward, inv_ref, wref, pull, moved,
):
    tile = (sz.rows, sz.cols)
    lane, row = lane_ids(tile), row_ids(tile)
    last_lane, last_row = sz.cols - 1, sz.rows - 1
    lev = levels[...].astype(jnp.float32)
    level_row = LEVEL_ROW * sz.lev
    side_base = 2 * sz.lev
    west_side = from_west[2 * sz.rows : 3 * sz.rows, :]
    east_side = from_east[2 * sz.rows : 3 * sz.rows, :]
    lev_w = shift_west(lev, lane, to_lane(west_side, side_base, 0))
    lev_e = shift_east(lev, lane, to_lane(east_side, side_base, last_lane))
    south_lev, north_lev = cross_south[level_row : level_row + 1, :], cross_north[level_row : level_row + 1, :]
    lev_s = shift_south(lev, row, south_lev)
    lev_n = shift_north(lev, row, north_lev)

    def masks(k):
        wet = lev > k
        return wet, wet & (lev_e > k), wet & (lev_w > k), wet & (lev_n > k), wet & (lev_s > k)

    is_dynamics = lax.axis_index("sect") == 0

    def physics():
        def around(f, k):
            at = f * sz.slab + k * sz.rows
            value = fields[at : at + sz.rows, :]
            lane_at, beyond = f * sz.lev + k, 2 * f * sz.lev + k
            return (
                value,
                shift_east(value, lane, to_lane(from_east[0 : sz.rows, :], lane_at, last_lane)),
                shift_west(value, lane, to_lane(from_west[0 : sz.rows, :], lane_at, 0)),
                shift_north(value, row, north[beyond : beyond + 1, :]),
                shift_south(value, row, south[beyond : beyond + 1, :]),
            )

        press = jnp.zeros(tile, jnp.float32)
        press_e, press_n, warm_above = press, press, press
        for k in range(sz.lev):
            at = k * sz.rows
            mask = masks(k)
            wet, wet_e, wet_w, wet_n, wet_s = mask
            zonal, merid, temper, saline, visc = (around(f, k) for f in range(5))
            flow_east, flow_west = keep(wet_e, zonal[0]), keep(wet_w, zonal[2])
            flow_north, flow_south = keep(wet_n, merid[0]), keep(wet_s, merid[4])
            div[at : at + sz.rows, :] = flow_east - flow_west + (flow_north - flow_south)
            warm = diffused(temper, visc, mask)
            mixing = jnp.zeros(tile, jnp.float32)
            if k > 0:
                background = fields[5 * sz.slab + at : 5 * sz.slab + at + sz.rows, :]
                mixing = mixed(warm_above, warm, background, wet)
            warm_above = warm

            def weight(place, wet_there):
                return keep(wet_there, HALINE * saline[place] - THERMAL * temper[place])

            press = press + GRAVITY_SCALE * weight(0, wet)
            press_e = press_e + GRAVITY_SCALE * weight(1, lev_e > k)
            press_n = press_n + GRAVITY_SCALE * weight(3, lev_n > k)
            zonal_new = diffused(zonal, visc, mask) + TIME_STEP * (CORIOLIS * merid[0] - (press_e - press))
            merid_new = diffused(merid, visc, mask) - TIME_STEP * (CORIOLIS * zonal[0] + (press_n - press))
            saline_new = diffused(saline, visc, mask)
            parts = (keep(wet_e, zonal_new), keep(wet_n, merid_new), warm, saline_new, None, mixing)
            for f, part in enumerate(parts):
                if part is not None:
                    out[f * sz.slab + at : f * sz.slab + at + sz.rows, :] = part
        total = jnp.zeros(tile, jnp.float32)
        for k in range(sz.lev - 1, -1, -1):
            at = k * sz.rows
            total = total + div[at : at + sz.rows, :]
            out[4 * sz.slab + at : 4 * sz.slab + at + sz.rows, :] = -total if k > 0 else jnp.zeros(tile, jnp.float32)

    def column(value, at):
        return jnp.broadcast_to(value[:, at : at + 1], value.shape)

    def both(west, east):
        return jnp.concatenate([west, east], axis=0)

    tall = (sz.lev, sz.cols)
    pair_row = row_ids((2 * sz.rows, sz.cols)) % sz.rows
    pair_lane = lane_ids((2 * sz.rows, sz.cols))

    def pair_south(value, edge):
        return jnp.where(pair_row == 0, edge, turn(value, 1, 0))

    def pair_north(value, edge):
        return jnp.where(pair_row == last_row, edge, turn(value, -1, 0))

    def edge_mixing():
        diagonal = lane_ids(tall) == row_ids(tall)

        def levels_in_lanes(rows, at):
            return jnp.broadcast_to(jnp.sum(keep(diagonal, column(rows, at)), axis=0, keepdims=True), tile)

        def place(index):
            return side[index * sz.rows : (index + 1) * sz.rows, :]

        own_pair, inner_w, inner_e = both(place(1), place(0)), place(3), place(2)

        def around(f, message_lane, cross_row):
            shift = -f * sz.lev
            outer_w, outer_e = turn(west_side, -message_lane, 1), turn(east_side, -message_lane, 1)
            own = turn(own_pair, shift, 1)
            low, high = (
                cross[cross_row * sz.lev : (cross_row + 1) * sz.lev, :] for cross in (cross_south, cross_north)
            )
            return (
                own,
                both(turn(inner_w, shift, 1), outer_e),
                both(outer_w, turn(inner_e, shift, 1)),
                pair_north(own, both(levels_in_lanes(high, 0), levels_in_lanes(high, last_lane))),
                pair_south(own, both(levels_in_lanes(low, 0), levels_in_lanes(low, last_lane))),
            )

        depth = pair_lane.astype(jnp.float32)

        def wet(value):
            return both(column(value, 0), column(value, last_lane)) > depth

        mid = wet(lev)
        mask = mid, mid & wet(lev_e), mid & wet(lev_w), mid & wet(lev_n), mid & wet(lev_s)
        warm = diffused(around(2, 0, TEMPER_ROW), around(4, sz.lev, VISC_ROW), mask)
        background = turn(own_pair, -5 * sz.lev, 1)
        return jnp.where(pair_lane == 0, 0.0, mixed(turn(warm, 1, 1), warm, background, mid))

    def row_strips(step):
        lane16, depth = lane_ids(tall), row_ids(tall).astype(jnp.float32)

        def wet(levels_row):
            return levels_row > depth

        west_corner = from_west[3 * sz.rows : 3 * sz.rows + sz.lev, :]
        east_corner = from_east[3 * sz.rows : 3 * sz.rows + sz.lev, :]
        lane1 = lane_ids((1, sz.cols))
        for r in range(2):
            rows, cross = (south, cross_south) if r == 0 else (north, cross_north)
            strip = low_strip if r == 0 else high_strip
            edge = 0 if r == 0 else last_row
            near_lev = cross[level_row : level_row + 1, :]
            far_lev = cross[level_row + 1 : level_row + 2, :]
            own_lev = lev[edge : edge + 1, :]
            corner_lane = side_base + 2 + r
            lev_at_w = shift_west(near_lev, lane1, to_lane(west_side[0:1, :], corner_lane, 0))
            lev_at_e = shift_east(near_lev, lane1, to_lane(east_side[0:1, :], corner_lane, last_lane))
            wet_near = wet(near_lev)
            zonal = cross[ZONAL_ROW * sz.lev : (ZONAL_ROW + 1) * sz.lev, :]
            p = r * (sz.nf + 2)
            zonal_w = shift_west(zonal, lane16, to_lane(west_corner, p + sz.nf, 0))
            flow_e = keep(wet_near & wet(lev_at_e), zonal)
            flow_w = keep(wet_near & wet(lev_at_w), zonal_w)
            merid = cross[MERID_ROW * sz.lev : (MERID_ROW + 1) * sz.lev, :]
            if r == 0:
                merid_far = cross[MERID_ROW2 * sz.lev : (MERID_ROW2 + 1) * sz.lev, :]
                flow_n = keep(wet_near & wet(own_lev), merid)
                flow_s = keep(wet_near & wet(far_lev), merid_far)
            else:
                flow_n = keep(wet_near & wet(far_lev), merid)
                flow_s = keep(wet_near & wet(own_lev), level_rows(bulk, sz.slab, last_row, sz))
            weights = Weights(flow_e, flow_w, flow_n, flow_s, step)
            for f in range(sz.nf):
                at = 2 * f * sz.lev
                near, far = rows[at : at + sz.lev, :], rows[at + sz.lev : at + 2 * sz.lev, :]
                inside = level_rows(fields, f * sz.slab, edge, sz)
                at_w = shift_west(near, lane16, to_lane(west_corner, p + f, 0))
                at_e = shift_east(near, lane16, to_lane(east_corner, p + f, last_lane))
                up, down = (inside, far) if r == 0 else (far, inside)
                strip[f * sz.lev : (f + 1) * sz.lev, :] = weights.apply(near, at_e, at_w, up, down)

    def column_strips(step):
        lane16, depth16 = lane_ids(tall), row_ids(tall)

        def all_fields(value, first):
            at = lane_ids(value.shape)
            value = jnp.where((at >= first) & (at < first + sz.lev), value, 0.0)
            width = sz.lev
            while width < sz.cols:
                value = value + turn(value, width, 1)
                width *= 2
            return value

        def corner_rows(message, r):
            items = message[3 * sz.rows : 3 * sz.rows + sz.lev, :]
            p = r * (sz.nf + 2)
            tracers = jnp.zeros(tall, jnp.float32)
            for f in range(sz.nf):
                spread = jnp.broadcast_to(items[:, p + f : p + f + 1], tall)
                tracers = jnp.where(lane16 == f * sz.lev + depth16, spread, tracers)
            spread = jnp.broadcast_to(items[:, p + sz.nf + 1 : p + sz.nf + 2], tall)
            velocity = jnp.where(lane16 % sz.lev == depth16, spread, 0.0)
            return jnp.sum(tracers, axis=0, keepdims=True), jnp.sum(velocity, axis=0, keepdims=True)

        inside_w, inside_e = own_west[0 : sz.rows, :], own_east[0 : sz.rows, :]
        near = both(from_west[0 : sz.rows, :], from_east[0 : sz.rows, :])
        far_w, far_e = from_west[sz.rows : 2 * sz.rows, :], from_east[sz.rows : 2 * sz.rows, :]
        corners = [corner_rows(message, r) for message in (from_west, from_east) for r in range(2)]
        low_tracers, high_tracers, low_merid = (
            both(jnp.broadcast_to(corners[i][part], tile), jnp.broadcast_to(corners[i + 2][part], tile))
            for i, part in ((0, 0), (1, 0), (0, 1))
        )

        def side_levels(at):
            return column(west_side, at), column(east_side, at)

        near_lev = both(*side_levels(side_base))
        far_lev_w, far_lev_e = side_levels(side_base + 1)
        own_lev_w, own_lev_e = column(lev, 0), column(lev, last_lane)
        lev_at_s = pair_south(near_lev, both(*side_levels(side_base + 2)))
        lev_at_n = pair_north(near_lev, both(*side_levels(side_base + 3)))
        depth = (lane_ids(near.shape) % sz.lev).astype(jnp.float32)
        wet_near = near_lev > depth
        zonal_first = sz.nf * sz.lev
        west, east = both(far_w, inside_e), both(inside_w, far_e)
        flow_e = keep(wet_near & (both(own_lev_w, far_lev_e) > depth), all_fields(near, zonal_first))
        flow_w = keep(wet_near & (both(far_lev_w, own_lev_e) > depth), all_fields(west, zonal_first))
        merid = all_fields(near, zonal_first + sz.lev)
        flow_n = keep(wet_near & (lev_at_n > depth), merid)
        flow_s = keep(wet_near & (lev_at_s > depth), pair_south(merid, low_merid))
        weights = Weights(flow_e, flow_w, flow_n, flow_s, step)
        side_strips[...] = weights.apply(near, east, west, pair_north(near, high_tracers), pair_south(near, low_tracers))

    def transport(step):
        west_old, east_old = from_west[0 : sz.rows, :], from_east[0 : sz.rows, :]
        zero = jnp.zeros(tile, jnp.float32)

        def faces(k):
            if k == sz.lev:
                return zero, zero
            at = k * sz.rows
            speed, mixing = vert[at : at + sz.rows, :], mix[at : at + sz.rows, :]
            return jnp.maximum(speed, 0.0) + mixing, jnp.minimum(speed, 0.0) - mixing

        every = range(sz.nf)

        def stored_weights(k):
            at = k * sz.rows
            return Weights.of(*(wref[i * sz.slab + at : i * sz.slab + at + sz.rows, :] for i in range(5)))

        def substep(weights, values, k, west, east, lows, highs):
            to_e = [turn(value, -1, 1) for value in values]
            to_w = [turn(value, 1, 1) for value in values]
            edge_e = [to_lane(east, f * sz.lev + k, last_lane) for f in every]
            edge_w = [to_lane(west, f * sz.lev + k, 0) for f in every]
            return [
                weights.apply(
                    values[f],
                    jnp.where(lane == last_lane, edge_e[f], to_e[f]),
                    jnp.where(lane == 0, edge_w[f], to_w[f]),
                    shift_north(values[f], row, highs[f]),
                    shift_south(values[f], row, lows[f]),
                )
                for f in every
            ]

        for k in range(sz.lev):
            at = k * sz.rows
            wet, wet_e, wet_w, wet_n, wet_s = masks(k)
            zonal, merid = bulk[at : at + sz.rows, :], bulk[sz.slab + at : sz.slab + at + sz.rows, :]
            zonal_first = sz.nf * sz.lev
            zonal_west = shift_west(zonal, lane, to_lane(west_old, zonal_first + k, 0))
            beyond = MERID_ROW * sz.lev + k
            merid_south = shift_south(merid, row, cross_south[beyond : beyond + 1, :])
            flow_e, flow_w, flow_n, flow_s = (
                keep(wet_e, zonal), keep(wet_w, zonal_west), keep(wet_n, merid), keep(wet_s, merid_south)
            )
            div[at : at + sz.rows, :] = flow_e - flow_w + (flow_n - flow_s)
            weights = Weights(flow_e, flow_w, flow_n, flow_s, step)
            for i, part in enumerate(weights.parts()):
                wref[i * sz.slab + at : i * sz.slab + at + sz.rows, :] = part
        column_strips(step)
        row_strips(step)
        west_new, east_new = side_strips[0 : sz.rows, :], side_strips[sz.rows : 2 * sz.rows, :]
        for k in range(sz.lev):
            at = k * sz.rows
            weights = stored_weights(k)
            values = [fields[f * sz.slab + at : f * sz.slab + at + sz.rows, :] for f in every]
            lows = [south[2 * f * sz.lev + k : 2 * f * sz.lev + k + 1, :] for f in every]
            highs = [north[2 * f * sz.lev + k : 2 * f * sz.lev + k + 1, :] for f in every]
            values = substep(weights, values, k, west_old, east_old, lows, highs)
            for f in every:
                forward[f * sz.slab + at : f * sz.slab + at + sz.rows, :] = values[f]
        edges = edge_mixing()
        edge_w, edge_e = edges[0 : sz.rows, :], edges[sz.rows : 2 * sz.rows, :]
        total = zero
        for k in range(sz.lev - 1, -1, -1):
            at = k * sz.rows
            total = total + div[at : at + sz.rows, :]
            vert[at : at + sz.rows, :] = -total if k > 0 else zero
            mixing = bulk[2 * sz.slab + at : 2 * sz.slab + at + sz.rows, :]
            mixing = jnp.where(lane == 0, to_lane(edge_w, k, 0), mixing)
            mix[at : at + sz.rows, :] = jnp.where(lane == last_lane, to_lane(edge_e, k, last_lane), mixing)
        last_ratio = None
        up, down = faces(0)
        lower, inverse = [], []
        for k in range(sz.lev):
            at = k * sz.rows
            up_next, down_next = faces(k + 1)
            pivot = 1.0 + TIME_STEP * (up - down_next)
            lower.append(TIME_STEP * down)
            if k > 0:
                pivot = pivot - lower[k] * last_ratio
            inverse.append(1.0 / pivot)
            last_ratio = -TIME_STEP * up_next * inverse[k]
            ratio[at : at + sz.rows, :] = last_ratio
            inv_ref[at : at + sz.rows, :] = inverse[k]
            pull[at : at + sz.rows, :] = lower[k] * inverse[k]
            up, down = up_next, down_next
        previous = [None] * sz.nf
        for k in range(sz.lev):
            at = k * sz.rows
            weights = stored_weights(k)
            values = [forward[f * sz.slab + at : f * sz.slab + at + sz.rows, :] for f in every]
            lows = [low_strip[f * sz.lev + k : f * sz.lev + k + 1, :] for f in every]
            highs = [high_strip[f * sz.lev + k : f * sz.lev + k + 1, :] for f in every]
            values = substep(weights, values, k, west_new, east_new, lows, highs)
            for f in every:
                moved[f * sz.slab + at : f * sz.slab + at + sz.rows, :] = values[f] * inv_ref[at : at + sz.rows, :]
        for k in range(sz.lev):
            at = k * sz.rows
            for f in every:
                here = f * sz.slab + at
                value = moved[here : here + sz.rows, :]
                if k > 0:
                    value = value - pull[at : at + sz.rows, :] * previous[f]
                forward[here : here + sz.rows, :] = value
                previous[f] = value
        for k in range(sz.lev - 1, -1, -1):
            at = k * sz.rows
            wet = lev > k
            for f in range(sz.nf):
                here = f * sz.slab + at
                if k < sz.lev - 1:
                    previous[f] = forward[here : here + sz.rows, :] - ratio[at : at + sz.rows, :] * previous[f]
                out[here : here + sz.rows, :] = keep(wet, previous[f])

    @pl.when(is_dynamics)
    def _():
        physics()

    @pl.when(jnp.logical_not(is_dynamics))
    def _():
        transport(TIME_STEP / NSUB)


def pair_of(index, count, odd):
    if not odd:
        return index ^ 1
    return (((index + 1) ^ 1) - 1) % count


def on_device(sizes_of, fields, levels):
    sz = Sizes(fields, levels)
    count_s, count_o, count_a = sizes_of
    flat = fields.reshape(sz.nf * sz.slab, sz.cols)
    axes = ("sect", "lon", "lat")

    def swap(value, odd):
        pairs = [(i, pair_of(i, count_a, odd)) for i in range(count_a)]
        return lax.ppermute(value, "lat", pairs)

    def from_dynamics(value, odd=None):
        mine = lax.axis_index("sect")
        got = None
        for hop in range(1, count_s):
            pairs = []
            for s in range(count_s):
                for o in range(count_o):
                    for a in range(count_a):
                        b = a if odd is None else pair_of(a, count_a, odd)
                        pairs.append(((s * count_o + o) * count_a + a, (((s + hop) % count_s) * count_o + o) * count_a + b))
            if odd is None:
                part = lax.ppermute(value, "sect", [(s, (s + hop) % count_s) for s in range(count_s)])
            else:
                part = lax.ppermute(value, axes, pairs)
            got = part if got is None else jnp.where(mine == hop, part, got)
        return got

    def around(value, step):
        return lax.ppermute(value, "lon", [(i, (i + step) % count_o) for i in range(count_o)])

    rows_shape = (2 * sz.nf * sz.lev, sz.cols)
    cross_shape = (LEVEL_ROW * sz.lev + 8, sz.cols)
    columns_shape = (3 * sz.rows + sz.lev, sz.cols)
    side_shape = (4 * sz.rows, sz.cols)
    row_a, row_b, own_side = call_kernel(functools.partial(pack_edges, sz), [rows_shape, rows_shape, side_shape], [flat])
    cross_a, cross_b = call_kernel(functools.partial(pack_cross, sz), [cross_shape, cross_shape], [flat, levels])
    side = from_dynamics(own_side)
    cross_b = from_dynamics(cross_b, True)
    row_b = swap(row_b, True)
    cross_a = from_dynamics(cross_a, False)
    row_a = swap(row_a, False)
    to_east, to_west, south, north, cross_south, cross_north, bulk = call_kernel(
        functools.partial(pack_columns, sz),
        [columns_shape] * 2 + [rows_shape] * 2 + [cross_shape] * 2 + [(3 * sz.slab, sz.cols)],
        [flat, levels, row_a, row_b, cross_a, cross_b, own_side, side],
    )
    bulk = from_dynamics(bulk)
    from_east = around(to_west, -1)
    from_west = around(to_east, 1)
    slab = (sz.slab, sz.cols)
    (out,) = call_kernel(
        functools.partial(finish, sz),
        [flat.shape],
        [flat, levels, south, north, cross_south, cross_north, bulk, to_east, to_west, side, from_west, from_east],
        [slab, slab, slab, (sz.nf * sz.lev, sz.cols), (sz.nf * sz.lev, sz.cols), (2 * sz.rows, sz.cols), slab, flat.shape, slab, (5 * sz.slab, sz.cols), slab, flat.shape],
    )
    return out.reshape(fields.shape)


def solution(mesh):
    sizes_of = (mesh.shape["sect"], mesh.shape["lon"], mesh.shape["lat"])
    return jax.shard_map(
        functools.partial(on_device, sizes_of),
        mesh=mesh,
        in_specs=(P("sect", None, None, "lat", "lon"), P("lat", "lon")),
        out_specs=P("sect", None, None, "lat", "lon"),
        check_vma=False,
    )
```

```python
import functools
import jax
import jax.numpy as jnp
from jax import lax
from jax.experimental import pallas as pl
from jax.experimental.pallas import tpu as pltpu
from jax.sharding import PartitionSpec as P

NSUB = 2
TIME_STEP = 1.0
CORIOLIS = 0.3
THERMAL = 0.2
HALINE = 0.15
GRAVITY_SCALE = 0.05
MIX_BOOST = 4.0
RICHARDSON = 1.0

VMEM_LIMIT = 8 * 1024 * 1024

ZONAL_ROW, MERID_ROW, MERID_ROW2, TEMPER_ROW, VISC_ROW, LEVEL_ROW = range(6)


def call_kernel(body, outputs, inputs, scratch=()):
    in_vmem = pl.BlockSpec(memory_space=pltpu.VMEM)
    return pl.pallas_call(
        body,
        out_shape=[jax.ShapeDtypeStruct(shape, jnp.float32) for shape in outputs],
        in_specs=[in_vmem] * len(inputs),
        out_specs=[in_vmem] * len(outputs),
        scratch_shapes=[pltpu.VMEM(shape, jnp.float32) for shape in scratch],
        compiler_params=pltpu.CompilerParams(vmem_limit_bytes=VMEM_LIMIT),
    )(*inputs)


class Sizes:
    def __init__(self, fields, levels):
        self.nf, self.lev = fields.shape[1], fields.shape[2]
        self.rows, self.cols = levels.shape
        self.slab = self.lev * self.rows


def lane_ids(shape):
    return lax.broadcasted_iota(jnp.int32, shape, 1)


def row_ids(shape):
    return lax.broadcasted_iota(jnp.int32, shape, 0)


def turn(value, shift, axis):
    size = value.shape[axis]
    shift = shift % size
    return value if shift == 0 else pltpu.roll(value, shift, axis)


def to_lane(value, source, target):
    return turn(value, target - source, 1)


def level_rows(ref, first, row, sz):
    return ref[pl.ds(first + row, sz.lev, stride=sz.rows), :]


def send_north_first(sz, fill):
    even = lax.axis_index("lat") % 2 == 0
    top, second = sz.rows - 1, sz.rows - 2

    @pl.when(even)
    def _():
        fill(0, top, second)
        fill(1, 0, 1)

    @pl.when(jnp.logical_not(even))
    def _():
        fill(0, 0, 1)
        fill(1, top, second)


def pack_edges(sz, fields, row_a, row_b, side):
    def fill(which, near, far):
        message = (row_a, row_b)[which]
        for f in range(sz.nf):
            for r, row in enumerate((near, far)):
                at = (2 * f + r) * sz.lev
                message[at : at + sz.lev, :] = level_rows(fields, f * sz.slab, row, sz)

    send_north_first(sz, fill)
    for place, column in enumerate(edge_columns(sz, fields, sz.nf, 0)):
        side[place * sz.rows : (place + 1) * sz.rows, :] = column


def pack_cross(sz, fields, levels, cross):
    lev = levels[...].astype(jnp.float32)

    def fill(which, near, far):
        if which == 0:
            return
        for at, (f, row) in enumerate(((0, near), (1, near), (1, far), (2, near), (4, near))):
            cross[at * sz.lev : (at + 1) * sz.lev, :] = level_rows(fields, f * sz.slab, row, sz)
        at = LEVEL_ROW * sz.lev
        cross[at : at + 1, :] = lev[near : near + 1, :]
        cross[at + 1 : at + 2, :] = lev[far : far + 1, :]
        cross[at + 2 : at + 8, :] = jnp.zeros((6, sz.cols), jnp.float32)

    send_north_first(sz, fill)


def pack_twin(sz, fields, own_side, row_a, twin):
    base = 4 * sz.rows
    twin[0:base, :] = own_side[...]
    for at, (f, r) in enumerate(((0, 0), (1, 0), (1, 1), (2, 0), (4, 0))):
        first = (2 * f + r) * sz.lev
        twin[base + at * sz.lev : base + (at + 1) * sz.lev, :] = row_a[first : first + sz.lev, :]
    twin[zonal_place(sz) : zonal_place(sz) + early(sz), :] = fields[0 : early(sz), :]


def early(sz):
    return sz.lev // 2 * sz.rows


def zonal_place(sz):
    return 4 * sz.rows + LEVEL_ROW * sz.lev


def edge_columns(sz, ref, count, first):
    tile = (sz.rows, sz.cols)
    lane = lane_ids(tile)
    zero = jnp.zeros(tile, jnp.float32)
    last = sz.cols - 1
    east_one, west_one, east_two, west_two = zero, zero, zero, zero
    for f in range(count):
        for k in range(sz.lev):
            at = f * sz.slab + k * sz.rows
            p = (first + f) * sz.lev + k
            moved = to_lane(ref[at : at + sz.rows, :], last, p)
            east_one = jnp.where(lane == p, moved, east_one)
            west_one = jnp.where(lane == (p + 1) % sz.cols, moved, west_one)
            west_two = jnp.where(lane == (p + 2) % sz.cols, moved, west_two)
            east_two = jnp.where(lane == (p - 1) % sz.cols, moved, east_two)
    return east_one, turn(west_one, -1, 1), turn(east_two, 1, 1), turn(west_two, -2, 1)


def pack_columns(
    sz, fields, levels, levels_a, row_a, row_b, twin, cross_b, own_side,
    to_east, to_west, south, north, cross_south, cross_north, bulk,
):
    position = lax.axis_index("lat")
    even = position % 2 == 0
    has_south = position > 0
    has_north = position < lax.axis_size("lat") - 1
    tile = (sz.rows, sz.cols)
    lane = lane_ids(tile)
    last = sz.cols - 1
    side = twin
    level_row = LEVEL_ROW * sz.lev
    near_a = levels_a[...].astype(jnp.float32)
    top, second = sz.rows - 1, sz.rows - 2
    near_a, far_a = (
        jnp.where(even, near_a[low : low + 1, :], near_a[high : high + 1, :]) for low, high in ((0, top), (1, second))
    )
    near_b, far_b = (cross_b[level_row + i : level_row + i + 1, :] for i in range(2))
    pairs = (
        (south, north, slice(None), row_a[...], row_b[...]),
        (cross_south, cross_north, slice(0, level_row), twin[4 * sz.rows : 4 * sz.rows + level_row, :], cross_b[0:level_row, :]),
        (cross_south, cross_north, slice(level_row, level_row + 1), near_a, near_b),
        (cross_south, cross_north, slice(level_row + 1, level_row + 2), far_a, far_b),
    )
    for low, high, at, first, other in pairs:
        low[at, :] = jnp.where(has_south, jnp.where(even, other, first), 0.0)
        high[at, :] = jnp.where(has_north, jnp.where(even, first, other), 0.0)
    for ref in (cross_south, cross_north):
        ref[level_row + 2 : level_row + 8, :] = jnp.zeros((6, sz.cols), jnp.float32)

    bulk[0 : sz.slab, :] = fields[sz.slab : 2 * sz.slab, :]
    bulk[2 * sz.slab : 3 * sz.slab - early(sz), :] = fields[early(sz) : sz.slab, :]
    tracer_lanes = lane < sz.nf * sz.lev
    for place, (message, at) in enumerate(((to_east, 0), (to_west, 0), (to_east, sz.rows), (to_west, sz.rows))):
        own = own_side[place * sz.rows : (place + 1) * sz.rows, :]
        dynamics = side[place * sz.rows : (place + 1) * sz.rows, :]
        message[at : at + sz.rows, :] = jnp.where(tracer_lanes, own, turn(dynamics, sz.nf * sz.lev, 1))

    lev = levels[...].astype(jnp.float32)
    south_lev = cross_south[level_row : level_row + 1, :]
    north_lev = cross_north[level_row : level_row + 1, :]
    base = 2 * sz.lev
    for place, (message, near, far) in enumerate(((to_east, last, last - 1), (to_west, 0, 1))):
        part = side[place * sz.rows : (place + 1) * sz.rows, :]
        part = jnp.where(lane < sz.lev, turn(part, -2 * sz.lev, 1), turn(part, -3 * sz.lev, 1))
        part = jnp.where(lane == base, to_lane(lev, near, base), part)
        part = jnp.where(lane == base + 1, to_lane(lev, far, base + 1), part)
        low = jnp.broadcast_to(to_lane(south_lev, near, base + 2), tile)
        high = jnp.broadcast_to(to_lane(north_lev, near, base + 3), tile)
        part = jnp.where(lane == base + 2, low, part)
        part = jnp.where(lane == base + 3, high, part)
        message[2 * sz.rows : 3 * sz.rows, :] = part

    tall = (sz.lev, sz.cols)
    tall_lane = lane_ids(tall)
    east_corner = jnp.zeros(tall, jnp.float32)
    west_corner = east_corner
    for r, (rows, cross) in enumerate(((south, cross_south), (north, cross_north))):
        for f in range(sz.nf + 2):
            if f < sz.nf:
                values = rows[2 * f * sz.lev : (2 * f + 1) * sz.lev, :]
            else:
                at = (ZONAL_ROW, MERID_ROW)[f - sz.nf] * sz.lev
                values = cross[at : at + sz.lev, :]
            p = r * (sz.nf + 2) + f
            moved = to_lane(values, last, p)
            east_corner = jnp.where(tall_lane == p, moved, east_corner)
            west_corner = jnp.where(tall_lane == p + 1, moved, west_corner)
    to_east[3 * sz.rows : 3 * sz.rows + sz.lev, :] = east_corner
    to_west[3 * sz.rows : 3 * sz.rows + sz.lev, :] = turn(west_corner, -1, 1)

    @pl.when(lax.axis_index("sect") == 0)
    def _():
        row = row_ids(tile)
        lev_e, lev_w = turn(lev, -1, 1), turn(lev, 1, 1)
        lev_n, lev_s = shift_north(lev, row, north_lev), shift_south(lev, row, south_lev)
        warm_above = None
        for k in range(sz.lev):
            at = k * sz.rows

            def around(f):
                value = fields[f * sz.slab + at : f * sz.slab + at + sz.rows, :]
                beyond = 2 * f * sz.lev + k
                return (
                    value, turn(value, -1, 1), turn(value, 1, 1),
                    shift_north(value, row, north[beyond : beyond + 1, :]),
                    shift_south(value, row, south[beyond : beyond + 1, :]),
                )

            wet = lev > k
            masks = wet, wet & (lev_e > k), wet & (lev_w > k), wet & (lev_n > k), wet & (lev_s > k)
            warm = diffused(around(2), around(4), masks)
            background = fields[5 * sz.slab + at : 5 * sz.slab + at + sz.rows, :]
            mixing = jnp.zeros(tile, jnp.float32) if k == 0 else mixed(warm_above, warm, background, wet)
            warm_above = warm
            bulk[sz.slab + at : sz.slab + at + sz.rows, :] = mixing


def keep(mask, value):
    return jnp.where(mask, value, 0.0)


def diffused(quantity, viscosity, masks):
    mid, e, w, n, s = quantity
    visc, visc_e, visc_w, visc_n, visc_s = viscosity
    _, wet_e, wet_w, wet_n, wet_s = masks
    change = (
        keep(wet_e, 0.5 * (visc + visc_e)) * (e - mid)
        - keep(wet_w, 0.5 * (visc_w + visc)) * (mid - w)
        + keep(wet_n, 0.5 * (visc + visc_n)) * (n - mid)
        - keep(wet_s, 0.5 * (visc_s + visc)) * (mid - s)
    )
    return mid + TIME_STEP * change


def mixed(warm_above, warm, background, wet):
    jump = THERMAL * (warm_above - warm)
    return keep(wet, background * (1.0 + MIX_BOOST / (1.0 + RICHARDSON * jump * jump)))


def shift_west(value, lane, edge):
    return jnp.where(lane == 0, edge, turn(value, 1, 1))


def shift_east(value, lane, edge):
    return jnp.where(lane == value.shape[1] - 1, edge, turn(value, -1, 1))


def shift_south(value, row, edge):
    return jnp.where(row == 0, edge, turn(value, 1, 0))


def shift_north(value, row, edge):
    return jnp.where(row == value.shape[0] - 1, edge, turn(value, -1, 0))


class Weights:
    def __init__(self, east, west, north, south, step):
        self.own = 1.0 - step * (
            jnp.maximum(east, 0.0) - jnp.minimum(west, 0.0) + (jnp.maximum(north, 0.0) - jnp.minimum(south, 0.0))
        )
        self.east = -step * jnp.minimum(east, 0.0)
        self.west = step * jnp.maximum(west, 0.0)
        self.north = -step * jnp.minimum(north, 0.0)
        self.south = step * jnp.maximum(south, 0.0)

    def parts(self):
        return self.own, self.east, self.west, self.north, self.south

    @classmethod
    def of(cls, own, east, west, north, south):
        weights = cls.__new__(cls)
        weights.own, weights.east, weights.west, weights.north, weights.south = own, east, west, north, south
        return weights

    def apply(self, own, east, west, north, south):
        return self.own * own + self.east * east + self.west * west + (self.north * north + self.south * south)


def finish(
    sz, fields, levels, south, north, cross_south, cross_north, bulk,
    own_east, own_west, side, from_west, from_east,
    out, div, mix, vert, low_strip, high_strip, side_strips, ratio, forward, inv_ref, wref, pull, moved,
):
    tile = (sz.rows, sz.cols)
    lane, row = lane_ids(tile), row_ids(tile)
    last_lane, last_row = sz.cols - 1, sz.rows - 1
    lev = levels[...].astype(jnp.float32)
    level_row = LEVEL_ROW * sz.lev
    side_base = 2 * sz.lev
    west_side = from_west[2 * sz.rows : 3 * sz.rows, :]
    east_side = from_east[2 * sz.rows : 3 * sz.rows, :]
    lev_w = shift_west(lev, lane, to_lane(west_side, side_base, 0))
    lev_e = shift_east(lev, lane, to_lane(east_side, side_base, last_lane))
    south_lev, north_lev = cross_south[level_row : level_row + 1, :], cross_north[level_row : level_row + 1, :]
    lev_s = shift_south(lev, row, south_lev)
    lev_n = shift_north(lev, row, north_lev)

    def masks(k):
        wet = lev > k
        return wet, wet & (lev_e > k), wet & (lev_w > k), wet & (lev_n > k), wet & (lev_s > k)

    is_dynamics = lax.axis_index("sect") == 0

    def physics():
        def around(f, k):
            at = f * sz.slab + k * sz.rows
            value = fields[at : at + sz.rows, :]
            lane_at, beyond = f * sz.lev + k, 2 * f * sz.lev + k
            return (
                value,
                shift_east(value, lane, to_lane(from_east[0 : sz.rows, :], lane_at, last_lane)),
                shift_west(value, lane, to_lane(from_west[0 : sz.rows, :], lane_at, 0)),
                shift_north(value, row, north[beyond : beyond + 1, :]),
                shift_south(value, row, south[beyond : beyond + 1, :]),
            )

        press = jnp.zeros(tile, jnp.float32)
        press_e, press_n, warm_above = press, press, press
        for k in range(sz.lev):
            at = k * sz.rows
            mask = masks(k)
            wet, wet_e, wet_w, wet_n, wet_s = mask
            zonal, merid, temper, saline, visc = (around(f, k) for f in range(5))
            flow_east, flow_west = keep(wet_e, zonal[0]), keep(wet_w, zonal[2])
            flow_north, flow_south = keep(wet_n, merid[0]), keep(wet_s, merid[4])
            div[at : at + sz.rows, :] = flow_east - flow_west + (flow_north - flow_south)
            warm = diffused(temper, visc, mask)
            mixing = jnp.zeros(tile, jnp.float32)
            if k > 0:
                background = fields[5 * sz.slab + at : 5 * sz.slab + at + sz.rows, :]
                mixing = mixed(warm_above, warm, background, wet)
            warm_above = warm

            def weight(place, wet_there):
                return keep(wet_there, HALINE * saline[place] - THERMAL * temper[place])

            press = press + GRAVITY_SCALE * weight(0, wet)
            press_e = press_e + GRAVITY_SCALE * weight(1, lev_e > k)
            press_n = press_n + GRAVITY_SCALE * weight(3, lev_n > k)
            zonal_new = diffused(zonal, visc, mask) + TIME_STEP * (CORIOLIS * merid[0] - (press_e - press))
            merid_new = diffused(merid, visc, mask) - TIME_STEP * (CORIOLIS * zonal[0] + (press_n - press))
            saline_new = diffused(saline, visc, mask)
            parts = (keep(wet_e, zonal_new), keep(wet_n, merid_new), warm, saline_new, None, mixing)
            for f, part in enumerate(parts):
                if part is not None:
                    out[f * sz.slab + at : f * sz.slab + at + sz.rows, :] = part
        total = jnp.zeros(tile, jnp.float32)
        for k in range(sz.lev - 1, -1, -1):
            at = k * sz.rows
            total = total + div[at : at + sz.rows, :]
            out[4 * sz.slab + at : 4 * sz.slab + at + sz.rows, :] = -total if k > 0 else jnp.zeros(tile, jnp.float32)

    def column(value, at):
        return jnp.broadcast_to(value[:, at : at + 1], value.shape)

    def both(west, east):
        return jnp.concatenate([west, east], axis=0)

    tall = (sz.lev, sz.cols)
    pair_row = row_ids((2 * sz.rows, sz.cols)) % sz.rows
    pair_lane = lane_ids((2 * sz.rows, sz.cols))

    def pair_south(value, edge):
        return jnp.where(pair_row == 0, edge, turn(value, 1, 0))

    def pair_north(value, edge):
        return jnp.where(pair_row == last_row, edge, turn(value, -1, 0))

    def edge_mixing():
        diagonal = lane_ids(tall) == row_ids(tall)

        def levels_in_lanes(rows, at):
            return jnp.broadcast_to(jnp.sum(keep(diagonal, column(rows, at)), axis=0, keepdims=True), tile)

        def place(index):
            return side[index * sz.rows : (index + 1) * sz.rows, :]

        own_pair, inner_w, inner_e = both(place(1), place(0)), place(3), place(2)

        def around(f, message_lane, cross_row):
            shift = -f * sz.lev
            outer_w, outer_e = turn(west_side, -message_lane, 1), turn(east_side, -message_lane, 1)
            own = turn(own_pair, shift, 1)
            low, high = (
                cross[cross_row * sz.lev : (cross_row + 1) * sz.lev, :] for cross in (cross_south, cross_north)
            )
            return (
                own,
                both(turn(inner_w, shift, 1), outer_e),
                both(outer_w, turn(inner_e, shift, 1)),
                pair_north(own, both(levels_in_lanes(high, 0), levels_in_lanes(high, last_lane))),
                pair_south(own, both(levels_in_lanes(low, 0), levels_in_lanes(low, last_lane))),
            )

        depth = pair_lane.astype(jnp.float32)

        def wet(value):
            return both(column(value, 0), column(value, last_lane)) > depth

        mid = wet(lev)
        mask = mid, mid & wet(lev_e), mid & wet(lev_w), mid & wet(lev_n), mid & wet(lev_s)
        warm = diffused(around(2, 0, TEMPER_ROW), around(4, sz.lev, VISC_ROW), mask)
        background = turn(own_pair, -5 * sz.lev, 1)
        return jnp.where(pair_lane == 0, 0.0, mixed(turn(warm, 1, 1), warm, background, mid))

    def row_strips(step):
        lane16, depth = lane_ids(tall), row_ids(tall).astype(jnp.float32)

        def wet(levels_row):
            return levels_row > depth

        west_corner = from_west[3 * sz.rows : 3 * sz.rows + sz.lev, :]
        east_corner = from_east[3 * sz.rows : 3 * sz.rows + sz.lev, :]
        lane1 = lane_ids((1, sz.cols))
        for r in range(2):
            rows, cross = (south, cross_south) if r == 0 else (north, cross_north)
            strip = low_strip if r == 0 else high_strip
            edge = 0 if r == 0 else last_row
            near_lev = cross[level_row : level_row + 1, :]
            far_lev = cross[level_row + 1 : level_row + 2, :]
            own_lev = lev[edge : edge + 1, :]
            corner_lane = side_base + 2 + r
            lev_at_w = shift_west(near_lev, lane1, to_lane(west_side[0:1, :], corner_lane, 0))
            lev_at_e = shift_east(near_lev, lane1, to_lane(east_side[0:1, :], corner_lane, last_lane))
            wet_near = wet(near_lev)
            zonal = cross[ZONAL_ROW * sz.lev : (ZONAL_ROW + 1) * sz.lev, :]
            p = r * (sz.nf + 2)
            zonal_w = shift_west(zonal, lane16, to_lane(west_corner, p + sz.nf, 0))
            flow_e = keep(wet_near & wet(lev_at_e), zonal)
            flow_w = keep(wet_near & wet(lev_at_w), zonal_w)
            merid = cross[MERID_ROW * sz.lev : (MERID_ROW + 1) * sz.lev, :]
            if r == 0:
                merid_far = cross[MERID_ROW2 * sz.lev : (MERID_ROW2 + 1) * sz.lev, :]
                flow_n = keep(wet_near & wet(own_lev), merid)
                flow_s = keep(wet_near & wet(far_lev), merid_far)
            else:
                flow_n = keep(wet_near & wet(far_lev), merid)
                flow_s = keep(wet_near & wet(own_lev), level_rows(bulk, 0, last_row, sz))
            weights = Weights(flow_e, flow_w, flow_n, flow_s, step)
            for f in range(sz.nf):
                at = 2 * f * sz.lev
                near, far = rows[at : at + sz.lev, :], rows[at + sz.lev : at + 2 * sz.lev, :]
                inside = level_rows(fields, f * sz.slab, edge, sz)
                at_w = shift_west(near, lane16, to_lane(west_corner, p + f, 0))
                at_e = shift_east(near, lane16, to_lane(east_corner, p + f, last_lane))
                up, down = (inside, far) if r == 0 else (far, inside)
                strip[f * sz.lev : (f + 1) * sz.lev, :] = weights.apply(near, at_e, at_w, up, down)

    def column_strips(step):
        lane16, depth16 = lane_ids(tall), row_ids(tall)

        def all_fields(value, first):
            at = lane_ids(value.shape)
            value = jnp.where((at >= first) & (at < first + sz.lev), value, 0.0)
            width = sz.lev
            while width < sz.cols:
                value = value + turn(value, width, 1)
                width *= 2
            return value

        def corner_rows(message, r):
            items = message[3 * sz.rows : 3 * sz.rows + sz.lev, :]
            p = r * (sz.nf + 2)
            tracers = jnp.zeros(tall, jnp.float32)
            for f in range(sz.nf):
                spread = jnp.broadcast_to(items[:, p + f : p + f + 1], tall)
                tracers = jnp.where(lane16 == f * sz.lev + depth16, spread, tracers)
            spread = jnp.broadcast_to(items[:, p + sz.nf + 1 : p + sz.nf + 2], tall)
            velocity = jnp.where(lane16 % sz.lev == depth16, spread, 0.0)
            return jnp.sum(tracers, axis=0, keepdims=True), jnp.sum(velocity, axis=0, keepdims=True)

        inside_w, inside_e = own_west[0 : sz.rows, :], own_east[0 : sz.rows, :]
        near = both(from_west[0 : sz.rows, :], from_east[0 : sz.rows, :])
        far_w, far_e = from_west[sz.rows : 2 * sz.rows, :], from_east[sz.rows : 2 * sz.rows, :]
        corners = [corner_rows(message, r) for message in (from_west, from_east) for r in range(2)]
        low_tracers, high_tracers, low_merid = (
            both(jnp.broadcast_to(corners[i][part], tile), jnp.broadcast_to(corners[i + 2][part], tile))
            for i, part in ((0, 0), (1, 0), (0, 1))
        )

        def side_levels(at):
            return column(west_side, at), column(east_side, at)

        near_lev = both(*side_levels(side_base))
        far_lev_w, far_lev_e = side_levels(side_base + 1)
        own_lev_w, own_lev_e = column(lev, 0), column(lev, last_lane)
        lev_at_s = pair_south(near_lev, both(*side_levels(side_base + 2)))
        lev_at_n = pair_north(near_lev, both(*side_levels(side_base + 3)))
        depth = (lane_ids(near.shape) % sz.lev).astype(jnp.float32)
        wet_near = near_lev > depth
        zonal_first = sz.nf * sz.lev
        west, east = both(far_w, inside_e), both(inside_w, far_e)
        flow_e = keep(wet_near & (both(own_lev_w, far_lev_e) > depth), all_fields(near, zonal_first))
        flow_w = keep(wet_near & (both(far_lev_w, own_lev_e) > depth), all_fields(west, zonal_first))
        merid = all_fields(near, zonal_first + sz.lev)
        flow_n = keep(wet_near & (lev_at_n > depth), merid)
        flow_s = keep(wet_near & (lev_at_s > depth), pair_south(merid, low_merid))
        weights = Weights(flow_e, flow_w, flow_n, flow_s, step)
        side_strips[...] = weights.apply(near, east, west, pair_north(near, high_tracers), pair_south(near, low_tracers))

    def transport(step):
        west_old, east_old = from_west[0 : sz.rows, :], from_east[0 : sz.rows, :]
        zero = jnp.zeros(tile, jnp.float32)

        def faces(k):
            if k == sz.lev:
                return zero, zero
            at = k * sz.rows
            speed, mixing = vert[at : at + sz.rows, :], mix[at : at + sz.rows, :]
            return jnp.maximum(speed, 0.0) + mixing, jnp.minimum(speed, 0.0) - mixing

        every = range(sz.nf)

        def stored_weights(k):
            at = k * sz.rows
            return Weights.of(*(wref[i * sz.slab + at : i * sz.slab + at + sz.rows, :] for i in range(5)))

        def substep(weights, values, k, west, east, lows, highs):
            to_e = [turn(value, -1, 1) for value in values]
            to_w = [turn(value, 1, 1) for value in values]
            edge_e = [to_lane(east, f * sz.lev + k, last_lane) for f in every]
            edge_w = [to_lane(west, f * sz.lev + k, 0) for f in every]
            return [
                weights.apply(
                    values[f],
                    jnp.where(lane == last_lane, edge_e[f], to_e[f]),
                    jnp.where(lane == 0, edge_w[f], to_w[f]),
                    shift_north(values[f], row, highs[f]),
                    shift_south(values[f], row, lows[f]),
                )
                for f in every
            ]

        for k in range(sz.lev):
            at = k * sz.rows
            wet, wet_e, wet_w, wet_n, wet_s = masks(k)
            zonal_at = zonal_place(sz) + at if at < early(sz) else 2 * sz.slab + at - early(sz)
            zonal = (side if at < early(sz) else bulk)[zonal_at : zonal_at + sz.rows, :]
            merid = bulk[at : at + sz.rows, :]
            zonal_first = sz.nf * sz.lev
            zonal_west = shift_west(zonal, lane, to_lane(west_old, zonal_first + k, 0))
            beyond = MERID_ROW * sz.lev + k
            merid_south = shift_south(merid, row, cross_south[beyond : beyond + 1, :])
            flow_e, flow_w, flow_n, flow_s = (
                keep(wet_e, zonal), keep(wet_w, zonal_west), keep(wet_n, merid), keep(wet_s, merid_south)
            )
            div[at : at + sz.rows, :] = flow_e - flow_w + (flow_n - flow_s)
            weights = Weights(flow_e, flow_w, flow_n, flow_s, step)
            for i, part in enumerate(weights.parts()):
                wref[i * sz.slab + at : i * sz.slab + at + sz.rows, :] = part
        column_strips(step)
        row_strips(step)
        west_new, east_new = side_strips[0 : sz.rows, :], side_strips[sz.rows : 2 * sz.rows, :]
        for k in range(sz.lev):
            at = k * sz.rows
            weights = stored_weights(k)
            values = [fields[f * sz.slab + at : f * sz.slab + at + sz.rows, :] for f in every]
            lows = [south[2 * f * sz.lev + k : 2 * f * sz.lev + k + 1, :] for f in every]
            highs = [north[2 * f * sz.lev + k : 2 * f * sz.lev + k + 1, :] for f in every]
            values = substep(weights, values, k, west_old, east_old, lows, highs)
            for f in every:
                forward[f * sz.slab + at : f * sz.slab + at + sz.rows, :] = values[f]
        edges = edge_mixing()
        edge_w, edge_e = edges[0 : sz.rows, :], edges[sz.rows : 2 * sz.rows, :]
        total = zero
        for k in range(sz.lev - 1, -1, -1):
            at = k * sz.rows
            total = total + div[at : at + sz.rows, :]
            vert[at : at + sz.rows, :] = -total if k > 0 else zero
            mixing = bulk[sz.slab + at : sz.slab + at + sz.rows, :]
            mixing = jnp.where(lane == 0, to_lane(edge_w, k, 0), mixing)
            mix[at : at + sz.rows, :] = jnp.where(lane == last_lane, to_lane(edge_e, k, last_lane), mixing)
        last_ratio = None
        up, down = faces(0)
        lower, inverse = [], []
        for k in range(sz.lev):
            at = k * sz.rows
            up_next, down_next = faces(k + 1)
            pivot = 1.0 + TIME_STEP * (up - down_next)
            lower.append(TIME_STEP * down)
            if k > 0:
                pivot = pivot - lower[k] * last_ratio
            inverse.append(1.0 / pivot)
            last_ratio = -TIME_STEP * up_next * inverse[k]
            ratio[at : at + sz.rows, :] = last_ratio
            inv_ref[at : at + sz.rows, :] = inverse[k]
            pull[at : at + sz.rows, :] = lower[k] * inverse[k]
            up, down = up_next, down_next
        previous = [None] * sz.nf
        for k in range(sz.lev):
            at = k * sz.rows
            weights = stored_weights(k)
            values = [forward[f * sz.slab + at : f * sz.slab + at + sz.rows, :] for f in every]
            lows = [low_strip[f * sz.lev + k : f * sz.lev + k + 1, :] for f in every]
            highs = [high_strip[f * sz.lev + k : f * sz.lev + k + 1, :] for f in every]
            values = substep(weights, values, k, west_new, east_new, lows, highs)
            for f in every:
                moved[f * sz.slab + at : f * sz.slab + at + sz.rows, :] = values[f] * inv_ref[at : at + sz.rows, :]
        for k in range(sz.lev):
            at = k * sz.rows
            for f in every:
                here = f * sz.slab + at
                value = moved[here : here + sz.rows, :]
                if k > 0:
                    value = value - pull[at : at + sz.rows, :] * previous[f]
                forward[here : here + sz.rows, :] = value
                previous[f] = value
        for k in range(sz.lev - 1, -1, -1):
            at = k * sz.rows
            wet = lev > k
            for f in range(sz.nf):
                here = f * sz.slab + at
                if k < sz.lev - 1:
                    previous[f] = forward[here : here + sz.rows, :] - ratio[at : at + sz.rows, :] * previous[f]
                out[here : here + sz.rows, :] = keep(wet, previous[f])

    @pl.when(is_dynamics)
    def _():
        physics()

    @pl.when(jnp.logical_not(is_dynamics))
    def _():
        transport(TIME_STEP / NSUB)


def pair_of(index, count, odd):
    if not odd:
        return index ^ 1
    return (((index + 1) ^ 1) - 1) % count


def on_device(sizes_of, fields, levels):
    sz = Sizes(fields, levels)
    count_s, count_o, count_a = sizes_of
    flat = fields.reshape(sz.nf * sz.slab, sz.cols)

    def place(s, o, a):
        return (s * count_o + o) * count_a + a

    def partner(s, o, a, odd, hop):
        b = pair_of(a, count_a, odd)
        if abs(a - b) > 1 and count_o % 2 == 0:
            return place(s, o ^ 1, a)
        return place((s + hop) % count_s, o, b)

    def swap(value, odd, hop=0):
        pairs = [
            (place(s, o, a), partner(s, o, a, odd, hop))
            for s in range(count_s)
            for o in range(count_o)
            for a in range(count_a)
        ]
        return lax.ppermute(value, ("sect", "lon", "lat"), pairs)

    def from_dynamics(value, odd=None):
        mine = lax.axis_index("sect")
        got = None
        for hop in range(1, count_s):
            if odd is None:
                part = lax.ppermute(value, "sect", [(s, (s + hop) % count_s) for s in range(count_s)])
            else:
                part = swap(value, odd, hop)
            got = part if got is None else jnp.where(mine == hop, part, got)
        return got

    def around(value, step):
        return lax.ppermute(value, "lon", [(i, (i + step) % count_o) for i in range(count_o)])

    rows_shape = (2 * sz.nf * sz.lev, sz.cols)
    cross_shape = (LEVEL_ROW * sz.lev + 8, sz.cols)
    columns_shape = (3 * sz.rows + sz.lev, sz.cols)
    side_shape = (4 * sz.rows, sz.cols)
    row_a, row_b, own_side = call_kernel(functools.partial(pack_edges, sz), [rows_shape, rows_shape, side_shape], [flat])
    (cross_b,) = call_kernel(functools.partial(pack_cross, sz), [cross_shape], [flat, levels])
    row_a = swap(row_a, False)
    levels_a = swap(levels, False)
    row_b = swap(row_b, True)
    (twin,) = call_kernel(
        functools.partial(pack_twin, sz), [(zonal_place(sz) + early(sz), sz.cols)], [flat, own_side, row_a]
    )
    twin = from_dynamics(twin)
    cross_b = from_dynamics(cross_b, True)
    to_east, to_west, south, north, cross_south, cross_north, bulk = call_kernel(
        functools.partial(pack_columns, sz),
        [columns_shape] * 2 + [rows_shape] * 2 + [cross_shape] * 2 + [(3 * sz.slab - early(sz), sz.cols)],
        [flat, levels, levels_a, row_a, row_b, twin, cross_b, own_side],
    )
    bulk = from_dynamics(bulk)
    from_east = around(to_west, -1)
    from_west = around(to_east, 1)
    slab = (sz.slab, sz.cols)
    (out,) = call_kernel(
        functools.partial(finish, sz),
        [flat.shape],
        [flat, levels, south, north, cross_south, cross_north, bulk, to_east, to_west, twin, from_west, from_east],
        [slab, slab, slab, (sz.nf * sz.lev, sz.cols), (sz.nf * sz.lev, sz.cols), (2 * sz.rows, sz.cols), slab, flat.shape, slab, (5 * sz.slab, sz.cols), slab, flat.shape],
    )
    return out.reshape(fields.shape)


def solution(mesh):
    sizes_of = (mesh.shape["sect"], mesh.shape["lon"], mesh.shape["lat"])
    return jax.shard_map(
        functools.partial(on_device, sizes_of),
        mesh=mesh,
        in_specs=(P("sect", None, None, "lat", "lon"), P("lat", "lon")),
        out_specs=P("sect", None, None, "lat", "lon"),
        check_vma=False,
    )
```

```python
import functools
import jax
import jax.numpy as jnp
from jax import lax
from jax.experimental import pallas as pl
from jax.experimental.pallas import tpu as pltpu
from jax.sharding import PartitionSpec as P

NSUB = 2
TIME_STEP = 1.0
CORIOLIS = 0.3
THERMAL = 0.2
HALINE = 0.15
GRAVITY_SCALE = 0.05
MIX_BOOST = 4.0
RICHARDSON = 1.0

VMEM_LIMIT = 8 * 1024 * 1024
CHUNKS = 4
EARLY_LEVELS = 0

ZONAL_ROW, MERID_ROW, MERID_ROW2, TEMPER_ROW, VISC_ROW, LEVEL_ROW = range(6)


def call_kernel(body, outputs, inputs, scratch=(), copies=0):
    in_vmem = pl.BlockSpec(memory_space=pltpu.VMEM)
    scratch = [pltpu.VMEM(shape, jnp.float32) for shape in scratch]
    if copies:
        scratch.append(pltpu.SemaphoreType.DMA((copies,)))
    return pl.pallas_call(
        body,
        out_shape=[jax.ShapeDtypeStruct(shape, jnp.float32) for shape in outputs],
        in_specs=[in_vmem] * len(inputs),
        out_specs=[pl.BlockSpec(memory_space=pl.ANY) if copies else in_vmem] * len(outputs),
        scratch_shapes=scratch,
        compiler_params=pltpu.CompilerParams(vmem_limit_bytes=VMEM_LIMIT),
    )(*inputs)


class Sizes:
    def __init__(self, fields, levels):
        self.nf, self.lev = fields.shape[1], fields.shape[2]
        self.rows, self.cols = levels.shape
        self.slab = self.lev * self.rows


def lane_ids(shape):
    return lax.broadcasted_iota(jnp.int32, shape, 1)


def row_ids(shape):
    return lax.broadcasted_iota(jnp.int32, shape, 0)


def turn(value, shift, axis):
    size = value.shape[axis]
    shift = shift % size
    return value if shift == 0 else pltpu.roll(value, shift, axis)


def to_lane(value, source, target):
    return turn(value, target - source, 1)


def level_rows(ref, first, row, sz):
    return ref[pl.ds(first + row, sz.lev, stride=sz.rows), :]


def send_north_first(sz, fill):
    even = lax.axis_index("lat") % 2 == 0
    top, second = sz.rows - 1, sz.rows - 2

    @pl.when(even)
    def _():
        fill(0, top, second)
        fill(1, 0, 1)

    @pl.when(jnp.logical_not(even))
    def _():
        fill(0, 0, 1)
        fill(1, top, second)


def pack_edges(sz, fields, row_a, row_b, side):
    def fill(which, near, far):
        message = (row_a, row_b)[which]
        for f in range(sz.nf):
            for r, row in enumerate((near, far)):
                at = (2 * f + r) * sz.lev
                message[at : at + sz.lev, :] = level_rows(fields, f * sz.slab, row, sz)

    send_north_first(sz, fill)
    for place, column in enumerate(edge_columns(sz, fields, sz.nf, 0)):
        side[place * sz.rows : (place + 1) * sz.rows, :] = column


def pack_cross(sz, fields, levels, cross):
    lev = levels[...].astype(jnp.float32)

    def fill(which, near, far):
        if which == 0:
            return
        for at, (f, row) in enumerate(((0, near), (1, near), (1, far), (2, near), (4, near))):
            cross[at * sz.lev : (at + 1) * sz.lev, :] = level_rows(fields, f * sz.slab, row, sz)
        at = LEVEL_ROW * sz.lev
        cross[at : at + 1, :] = lev[near : near + 1, :]
        cross[at + 1 : at + 2, :] = lev[far : far + 1, :]
        cross[at + 2 :, :] = jnp.zeros((cross.shape[0] - at - 2, sz.cols), jnp.float32)

    send_north_first(sz, fill)


def pack_twin(sz, fields, own_side, row_a, twin):
    base = 4 * sz.rows
    twin[0:base, :] = own_side[...]
    for at, (f, r) in enumerate(((0, 0), (1, 0), (1, 1), (2, 0), (4, 0))):
        first = (2 * f + r) * sz.lev
        twin[base + at * sz.lev : base + (at + 1) * sz.lev, :] = row_a[first : first + sz.lev, :]
    if early(sz):
        twin[zonal_place(sz) : zonal_place(sz) + early(sz), :] = fields[0 : early(sz), :]


def early(sz):
    return EARLY_LEVELS * sz.rows


def zonal_place(sz):
    return 4 * sz.rows + LEVEL_ROW * sz.lev


def edge_columns(sz, ref, count, first):
    tile = (sz.rows, sz.cols)
    lane = lane_ids(tile)
    zero = jnp.zeros(tile, jnp.float32)
    last = sz.cols - 1
    east_one, west_one, east_two, west_two = zero, zero, zero, zero
    for f in range(count):
        for k in range(sz.lev):
            at = f * sz.slab + k * sz.rows
            p = (first + f) * sz.lev + k
            moved = to_lane(ref[at : at + sz.rows, :], last, p)
            east_one = jnp.where(lane == p, moved, east_one)
            west_one = jnp.where(lane == (p + 1) % sz.cols, moved, west_one)
            west_two = jnp.where(lane == (p + 2) % sz.cols, moved, west_two)
            east_two = jnp.where(lane == (p - 1) % sz.cols, moved, east_two)
    return east_one, turn(west_one, -1, 1), turn(east_two, 1, 1), turn(west_two, -2, 1)


def place_rows(sz, row_a, row_b, south, north, corners):
    position = lax.axis_index("lat")
    even = position % 2 == 0
    first, other = row_a[...], row_b[...]
    tall = (sz.lev, sz.cols)
    lane, depth = lane_ids(tall), row_ids(tall)
    low = jnp.where(position > 0, jnp.where(even, other, first), 0.0)
    high = jnp.where(position < lax.axis_size("lat") - 1, jnp.where(even, first, other), 0.0)
    south[...] = low
    north[...] = high
    ends = []
    for column in (sz.cols - 1, 0):
        for rows in (low, high):
            total = jnp.zeros(tall, jnp.float32)
            for f in range(sz.nf):
                near = rows[2 * f * sz.lev : (2 * f + 1) * sz.lev, :]
                spread = jnp.broadcast_to(near[:, column : column + 1], tall)
                total = jnp.where(lane == f * sz.lev + depth, spread, total)
            ends.append(jnp.sum(total, axis=0, keepdims=True))
    for i, end in enumerate(ends):
        corners[i : i + 1, :] = end
    corners[len(ends) :, :] = jnp.zeros((sz.rows - len(ends), sz.cols), jnp.float32)


def pack_columns(
    sz, fields, levels, levels_a, south, north, corners, twin, cross_b, own_side,
    to_east, to_west, cross_south, cross_north, bulk,
):
    position = lax.axis_index("lat")
    even = position % 2 == 0
    has_south = position > 0
    has_north = position < lax.axis_size("lat") - 1
    tile = (sz.rows, sz.cols)
    lane = lane_ids(tile)
    last = sz.cols - 1
    side = twin
    level_row = LEVEL_ROW * sz.lev
    near_a = levels_a[...].astype(jnp.float32)
    top, second = sz.rows - 1, sz.rows - 2
    near_a, far_a = (
        jnp.where(even, near_a[low : low + 1, :], near_a[high : high + 1, :]) for low, high in ((0, top), (1, second))
    )
    near_b, far_b = (cross_b[level_row + i : level_row + i + 1, :] for i in range(2))
    pairs = (
        (cross_south, cross_north, slice(0, level_row), twin[4 * sz.rows : 4 * sz.rows + level_row, :], cross_b[0:level_row, :]),
        (cross_south, cross_north, slice(level_row, level_row + 1), near_a, near_b),
        (cross_south, cross_north, slice(level_row + 1, level_row + 2), far_a, far_b),
    )
    for low, high, at, first, other in pairs:
        low[at, :] = jnp.where(has_south, jnp.where(even, other, first), 0.0)
        high[at, :] = jnp.where(has_north, jnp.where(even, first, other), 0.0)
    for ref in (cross_south, cross_north):
        ref[level_row + 2 : level_row + 8, :] = jnp.zeros((6, sz.cols), jnp.float32)

    bulk[0 : sz.slab, :] = fields[sz.slab : 2 * sz.slab, :]
    bulk[2 * sz.slab : 3 * sz.slab - early(sz), :] = fields[early(sz) : sz.slab, :]
    tracer_lanes = lane < sz.nf * sz.lev
    for place, (message, at) in enumerate(((to_east, 0), (to_west, 0), (to_east, sz.rows), (to_west, sz.rows))):
        own = own_side[place * sz.rows : (place + 1) * sz.rows, :]
        dynamics = side[place * sz.rows : (place + 1) * sz.rows, :]
        message[at : at + sz.rows, :] = jnp.where(tracer_lanes, own, turn(dynamics, sz.nf * sz.lev, 1))

    lev = levels[...].astype(jnp.float32)
    south_lev = cross_south[level_row : level_row + 1, :]
    north_lev = cross_north[level_row : level_row + 1, :]
    base = 2 * sz.lev
    for place, (message, near, far) in enumerate(((to_east, last, last - 1), (to_west, 0, 1))):
        part = side[place * sz.rows : (place + 1) * sz.rows, :]
        part = jnp.where(lane < sz.lev, turn(part, -2 * sz.lev, 1), turn(part, -3 * sz.lev, 1))
        part = jnp.where(lane == base, to_lane(lev, near, base), part)
        part = jnp.where(lane == base + 1, to_lane(lev, far, base + 1), part)
        low = jnp.broadcast_to(to_lane(south_lev, near, base + 2), tile)
        high = jnp.broadcast_to(to_lane(north_lev, near, base + 3), tile)
        part = jnp.where(lane == base + 2, low, part)
        part = jnp.where(lane == base + 3, high, part)
        message[2 * sz.rows : 3 * sz.rows, :] = part

    tall = (sz.lev, sz.cols)
    tall_lane = lane_ids(tall)
    east_corner = jnp.zeros(tall, jnp.float32)
    west_corner = east_corner
    for r, (rows, cross) in enumerate(((south, cross_south), (north, cross_north))):
        for f in range(sz.nf + 2):
            if f < sz.nf:
                values = rows[2 * f * sz.lev : (2 * f + 1) * sz.lev, :]
            else:
                at = (ZONAL_ROW, MERID_ROW)[f - sz.nf] * sz.lev
                values = cross[at : at + sz.lev, :]
            p = r * (sz.nf + 2) + f
            moved = to_lane(values, last, p)
            east_corner = jnp.where(tall_lane == p, moved, east_corner)
            west_corner = jnp.where(tall_lane == p + 1, moved, west_corner)
    to_east[3 * sz.rows : 3 * sz.rows + sz.lev, :] = east_corner
    to_west[3 * sz.rows : 3 * sz.rows + sz.lev, :] = turn(west_corner, -1, 1)
    ends = corners[...]
    to_east[3 * sz.rows + sz.lev :, :] = ends
    to_west[3 * sz.rows + sz.lev :, :] = turn(ends, -2, 0)

    @pl.when(lax.axis_index("sect") == 0)
    def _():
        row = row_ids(tile)
        lev_e, lev_w = turn(lev, -1, 1), turn(lev, 1, 1)
        lev_n, lev_s = shift_north(lev, row, north_lev), shift_south(lev, row, south_lev)
        warm_above = None
        for k in range(sz.lev):
            at = k * sz.rows

            def around(f):
                value = fields[f * sz.slab + at : f * sz.slab + at + sz.rows, :]
                beyond = 2 * f * sz.lev + k
                return (
                    value, turn(value, -1, 1), turn(value, 1, 1),
                    shift_north(value, row, north[beyond : beyond + 1, :]),
                    shift_south(value, row, south[beyond : beyond + 1, :]),
                )

            wet = lev > k
            masks = wet, wet & (lev_e > k), wet & (lev_w > k), wet & (lev_n > k), wet & (lev_s > k)
            warm = diffused(around(2), around(4), masks)
            background = fields[5 * sz.slab + at : 5 * sz.slab + at + sz.rows, :]
            mixing = jnp.zeros(tile, jnp.float32) if k == 0 else mixed(warm_above, warm, background, wet)
            warm_above = warm
            bulk[sz.slab + at : sz.slab + at + sz.rows, :] = mixing


def keep(mask, value):
    return jnp.where(mask, value, 0.0)


def diffused(quantity, viscosity, masks):
    mid, e, w, n, s = quantity
    visc, visc_e, visc_w, visc_n, visc_s = viscosity
    _, wet_e, wet_w, wet_n, wet_s = masks
    change = (
        keep(wet_e, 0.5 * (visc + visc_e)) * (e - mid)
        - keep(wet_w, 0.5 * (visc_w + visc)) * (mid - w)
        + keep(wet_n, 0.5 * (visc + visc_n)) * (n - mid)
        - keep(wet_s, 0.5 * (visc_s + visc)) * (mid - s)
    )
    return mid + TIME_STEP * change


def mixed(warm_above, warm, background, wet):
    jump = THERMAL * (warm_above - warm)
    return keep(wet, background * (1.0 + MIX_BOOST / (1.0 + RICHARDSON * jump * jump)))


def shift_west(value, lane, edge):
    return jnp.where(lane == 0, edge, turn(value, 1, 1))


def shift_east(value, lane, edge):
    return jnp.where(lane == value.shape[1] - 1, edge, turn(value, -1, 1))


def shift_south(value, row, edge):
    return jnp.where(row == 0, edge, turn(value, 1, 0))


def shift_north(value, row, edge):
    return jnp.where(row == value.shape[0] - 1, edge, turn(value, -1, 0))


class Weights:
    def __init__(self, east, west, north, south, step):
        self.own = 1.0 - step * (
            jnp.maximum(east, 0.0) - jnp.minimum(west, 0.0) + (jnp.maximum(north, 0.0) - jnp.minimum(south, 0.0))
        )
        self.east = -step * jnp.minimum(east, 0.0)
        self.west = step * jnp.maximum(west, 0.0)
        self.north = -step * jnp.minimum(north, 0.0)
        self.south = step * jnp.maximum(south, 0.0)

    def parts(self):
        return self.own, self.east, self.west, self.north, self.south

    @classmethod
    def of(cls, own, east, west, north, south):
        weights = cls.__new__(cls)
        weights.own, weights.east, weights.west, weights.north, weights.south = own, east, west, north, south
        return weights

    def apply(self, own, east, west, north, south):
        return self.own * own + self.east * east + self.west * west + (self.north * north + self.south * south)


def shift_fields(sz, fields, south, north, kept, moved_e, moved_w, moved_n, moved_s):
    kept[...] = fields[...]
    row = row_ids((sz.rows, sz.cols))
    for f in range(sz.nf):
        for k in range(sz.lev):
            at = f * sz.slab + k * sz.rows
            here = slice(at, at + sz.rows)
            value = fields[here, :]
            beyond = 2 * f * sz.lev + k
            moved_e[here, :] = turn(value, -1, 1)
            moved_w[here, :] = turn(value, 1, 1)
            moved_n[here, :] = shift_north(value, row, north[beyond : beyond + 1, :])
            moved_s[here, :] = shift_south(value, row, south[beyond : beyond + 1, :])


def column_edges(
    sz, levels, cross_south, cross_north, own_east, own_west, side, from_west, from_east, moved_e, moved_w,
    around_e, around_w, second, edge_mix,
):
    tile = (sz.rows, sz.cols)
    lane, row = lane_ids(tile), row_ids(tile)
    last_lane, last_row = sz.cols - 1, sz.rows - 1
    lev = levels[...].astype(jnp.float32)
    level_row = LEVEL_ROW * sz.lev
    side_base = 2 * sz.lev
    west_side = from_west[2 * sz.rows : 3 * sz.rows, :]
    east_side = from_east[2 * sz.rows : 3 * sz.rows, :]
    lev_w = shift_west(lev, lane, to_lane(west_side, side_base, 0))
    lev_e = shift_east(lev, lane, to_lane(east_side, side_base, last_lane))
    south_lev, north_lev = cross_south[level_row : level_row + 1, :], cross_north[level_row : level_row + 1, :]
    lev_s = shift_south(lev, row, south_lev)
    lev_n = shift_north(lev, row, north_lev)

    def masks(k):
        wet = lev > k
        return wet, wet & (lev_e > k), wet & (lev_w > k), wet & (lev_n > k), wet & (lev_s > k)

    def column(value, at):
        return jnp.broadcast_to(value[:, at : at + 1], value.shape)

    def both(west, east):
        return jnp.concatenate([west, east], axis=0)

    tall = (sz.lev, sz.cols)
    pair_row = row_ids((2 * sz.rows, sz.cols)) % sz.rows
    pair_lane = lane_ids((2 * sz.rows, sz.cols))

    def pair_south(value, edge):
        return jnp.where(pair_row == 0, edge, turn(value, 1, 0))

    def pair_north(value, edge):
        return jnp.where(pair_row == last_row, edge, turn(value, -1, 0))

    def edge_mixing():
        diagonal = lane_ids(tall) == row_ids(tall)

        def levels_in_lanes(rows, at):
            return jnp.broadcast_to(jnp.sum(keep(diagonal, column(rows, at)), axis=0, keepdims=True), tile)

        def place(index):
            return side[index * sz.rows : (index + 1) * sz.rows, :]

        own_pair, inner_w, inner_e = both(place(1), place(0)), place(3), place(2)

        def around(f, message_lane, cross_row):
            shift = -f * sz.lev
            outer_w, outer_e = turn(west_side, -message_lane, 1), turn(east_side, -message_lane, 1)
            own = turn(own_pair, shift, 1)
            low, high = (
                cross[cross_row * sz.lev : (cross_row + 1) * sz.lev, :] for cross in (cross_south, cross_north)
            )
            return (
                own,
                both(turn(inner_w, shift, 1), outer_e),
                both(outer_w, turn(inner_e, shift, 1)),
                pair_north(own, both(levels_in_lanes(high, 0), levels_in_lanes(high, last_lane))),
                pair_south(own, both(levels_in_lanes(low, 0), levels_in_lanes(low, last_lane))),
            )

        depth = pair_lane.astype(jnp.float32)

        def wet(value):
            return both(column(value, 0), column(value, last_lane)) > depth

        mid = wet(lev)
        mask = mid, mid & wet(lev_e), mid & wet(lev_w), mid & wet(lev_n), mid & wet(lev_s)
        warm = diffused(around(2, 0, TEMPER_ROW), around(4, sz.lev, VISC_ROW), mask)
        background = turn(own_pair, -5 * sz.lev, 1)
        return jnp.where(pair_lane == 0, 0.0, mixed(turn(warm, 1, 1), warm, background, mid))

    def column_strips(step):
        lane16, depth16 = lane_ids(tall), row_ids(tall)

        def all_fields(value, first):
            at = lane_ids(value.shape)
            value = jnp.where((at >= first) & (at < first + sz.lev), value, 0.0)
            width = sz.lev
            while width < sz.cols:
                value = value + turn(value, width, 1)
                width *= 2
            return value

        def corner_rows(message, r):
            items = message[3 * sz.rows : 3 * sz.rows + sz.lev, :]
            p = r * (sz.nf + 2)
            ends = 3 * sz.rows + sz.lev + r
            tracers = message[ends : ends + 1, :]
            spread = jnp.broadcast_to(items[:, p + sz.nf + 1 : p + sz.nf + 2], tall)
            velocity = jnp.where(lane16 % sz.lev == depth16, spread, 0.0)
            return tracers, jnp.sum(velocity, axis=0, keepdims=True)

        inside_w, inside_e = own_west[0 : sz.rows, :], own_east[0 : sz.rows, :]
        near = both(from_west[0 : sz.rows, :], from_east[0 : sz.rows, :])
        far_w, far_e = from_west[sz.rows : 2 * sz.rows, :], from_east[sz.rows : 2 * sz.rows, :]
        corners = [corner_rows(message, r) for message in (from_west, from_east) for r in range(2)]
        low_tracers, high_tracers, low_merid = (
            both(jnp.broadcast_to(corners[i][part], tile), jnp.broadcast_to(corners[i + 2][part], tile))
            for i, part in ((0, 0), (1, 0), (0, 1))
        )

        def side_levels(at):
            return column(west_side, at), column(east_side, at)

        near_lev = both(*side_levels(side_base))
        far_lev_w, far_lev_e = side_levels(side_base + 1)
        own_lev_w, own_lev_e = column(lev, 0), column(lev, last_lane)
        lev_at_s = pair_south(near_lev, both(*side_levels(side_base + 2)))
        lev_at_n = pair_north(near_lev, both(*side_levels(side_base + 3)))
        depth = (lane_ids(near.shape) % sz.lev).astype(jnp.float32)
        wet_near = near_lev > depth
        zonal_first = sz.nf * sz.lev
        west, east = both(far_w, inside_e), both(inside_w, far_e)
        flow_e = keep(wet_near & (both(own_lev_w, far_lev_e) > depth), all_fields(near, zonal_first))
        flow_w = keep(wet_near & (both(far_lev_w, own_lev_e) > depth), all_fields(west, zonal_first))
        merid = all_fields(near, zonal_first + sz.lev)
        flow_n = keep(wet_near & (lev_at_n > depth), merid)
        flow_s = keep(wet_near & (lev_at_s > depth), pair_south(merid, low_merid))
        weights = Weights(flow_e, flow_w, flow_n, flow_s, step)
        return weights.apply(near, east, west, pair_north(near, high_tracers), pair_south(near, low_tracers))

    @pl.when(lax.axis_index("sect") > 0)
    def _():
        west_old, east_old = from_west[0 : sz.rows, :], from_east[0 : sz.rows, :]
        strips = column_strips(TIME_STEP / NSUB)
        west_new, east_new = strips[0 : sz.rows, :], strips[sz.rows : 2 * sz.rows, :]
        edges = edge_mixing()
        edge_w, edge_e = edges[0 : sz.rows, :], edges[sz.rows : 2 * sz.rows, :]
        first, last = lane == 0, lane == last_lane
        for k in range(sz.lev):
            at = k * sz.rows
            edge_mix[at : at + sz.rows, :] = jnp.where(first, to_lane(edge_w, k, 0), to_lane(edge_e, k, last_lane))
            for f in range(sz.nf):
                here = slice(f * sz.slab + at, f * sz.slab + at + sz.rows)
                p = f * sz.lev + k
                around_e[here, :] = jnp.where(last, to_lane(east_old, p, last_lane), moved_e[here, :])
                around_w[here, :] = jnp.where(first, to_lane(west_old, p, 0), moved_w[here, :])
        for k in range(sz.lev):
            for f in range(sz.nf):
                here = slice(f * sz.slab + k * sz.rows, f * sz.slab + (k + 1) * sz.rows)
                p = f * sz.lev + k
                second[here, :] = jnp.where(first, to_lane(west_new, p, 0), to_lane(east_new, p, last_lane))


def finish(
    sz, fields, levels, south, north, cross_south, cross_north, bulk,
    side, from_west, from_east, moved_e, moved_w, around_e, around_w, around_n, around_s, second, edge_mix,
    result, out, div, mix, vert, low_strip, high_strip, ratio, forward, inv_ref, wref, pull, moved, sent,
):
    tile = (sz.rows, sz.cols)
    lane, row = lane_ids(tile), row_ids(tile)
    last_lane, last_row = sz.cols - 1, sz.rows - 1
    lev = levels[...].astype(jnp.float32)
    level_row = LEVEL_ROW * sz.lev
    side_base = 2 * sz.lev
    west_side = from_west[2 * sz.rows : 3 * sz.rows, :]
    east_side = from_east[2 * sz.rows : 3 * sz.rows, :]
    lev_w = shift_west(lev, lane, to_lane(west_side, side_base, 0))
    lev_e = shift_east(lev, lane, to_lane(east_side, side_base, last_lane))
    south_lev, north_lev = cross_south[level_row : level_row + 1, :], cross_north[level_row : level_row + 1, :]
    lev_s = shift_south(lev, row, south_lev)
    lev_n = shift_north(lev, row, north_lev)

    def masks(k):
        wet = lev > k
        return wet, wet & (lev_e > k), wet & (lev_w > k), wet & (lev_n > k), wet & (lev_s > k)

    is_dynamics = lax.axis_index("sect") == 0
    chunk = sz.lev // CHUNKS
    copies = []

    def send(first, last, part):
        at = pl.ds(part * chunk * sz.rows, chunk * sz.rows)
        copy = pltpu.make_async_copy(
            out.at[pl.ds(first, last - first), at, :], result.at[pl.ds(first, last - first), at, :], sent.at[len(copies)]
        )
        copy.start()
        copies.append(copy)

    def finish_copies():
        for copy in copies:
            copy.wait()
        copies.clear()

    def physics():
        def around(f, k):
            at = f * sz.slab + k * sz.rows
            here = slice(at, at + sz.rows)
            lane_at = f * sz.lev + k
            return (
                fields[here, :],
                jnp.where(lane == last_lane, to_lane(from_east[0 : sz.rows, :], lane_at, last_lane), moved_e[here, :]),
                jnp.where(lane == 0, to_lane(from_west[0 : sz.rows, :], lane_at, 0), moved_w[here, :]),
                around_n[here, :],
                around_s[here, :],
            )

        press = jnp.zeros(tile, jnp.float32)
        press_e, press_n, warm_above = press, press, press
        for k in range(sz.lev):
            at = k * sz.rows
            mask = masks(k)
            wet, wet_e, wet_w, wet_n, wet_s = mask
            zonal, merid, temper, saline, visc = (around(f, k) for f in range(5))
            flow_east, flow_west = keep(wet_e, zonal[0]), keep(wet_w, zonal[2])
            flow_north, flow_south = keep(wet_n, merid[0]), keep(wet_s, merid[4])
            div[at : at + sz.rows, :] = flow_east - flow_west + (flow_north - flow_south)
            warm = diffused(temper, visc, mask)
            mixing = jnp.zeros(tile, jnp.float32)
            if k > 0:
                background = fields[5 * sz.slab + at : 5 * sz.slab + at + sz.rows, :]
                mixing = mixed(warm_above, warm, background, wet)
            warm_above = warm

            def weight(place, wet_there):
                return keep(wet_there, HALINE * saline[place] - THERMAL * temper[place])

            press = press + GRAVITY_SCALE * weight(0, wet)
            press_e = press_e + GRAVITY_SCALE * weight(1, lev_e > k)
            press_n = press_n + GRAVITY_SCALE * weight(3, lev_n > k)
            zonal_new = diffused(zonal, visc, mask) + TIME_STEP * (CORIOLIS * merid[0] - (press_e - press))
            merid_new = diffused(merid, visc, mask) - TIME_STEP * (CORIOLIS * zonal[0] + (press_n - press))
            saline_new = diffused(saline, visc, mask)
            parts = (keep(wet_e, zonal_new), keep(wet_n, merid_new), warm, saline_new, None, mixing)
            for f, part in enumerate(parts):
                if part is not None:
                    out[f, at : at + sz.rows, :] = part
            if k % chunk == chunk - 1:
                send(0, 4, k // chunk)
                send(5, 6, k // chunk)
        total = jnp.zeros(tile, jnp.float32)
        for k in range(sz.lev - 1, -1, -1):
            at = k * sz.rows
            total = total + div[at : at + sz.rows, :]
            out[4, at : at + sz.rows, :] = -total if k > 0 else jnp.zeros(tile, jnp.float32)
            if k % chunk == 0:
                send(4, 5, k // chunk)

    tall = (sz.lev, sz.cols)

    def row_strips(step):
        lane16, depth = lane_ids(tall), row_ids(tall).astype(jnp.float32)

        def wet(levels_row):
            return levels_row > depth

        west_corner = from_west[3 * sz.rows : 3 * sz.rows + sz.lev, :]
        east_corner = from_east[3 * sz.rows : 3 * sz.rows + sz.lev, :]
        lane1 = lane_ids((1, sz.cols))
        for r in range(2):
            rows, cross = (south, cross_south) if r == 0 else (north, cross_north)
            strip = low_strip if r == 0 else high_strip
            edge = 0 if r == 0 else last_row
            near_lev = cross[level_row : level_row + 1, :]
            far_lev = cross[level_row + 1 : level_row + 2, :]
            own_lev = lev[edge : edge + 1, :]
            corner_lane = side_base + 2 + r
            lev_at_w = shift_west(near_lev, lane1, to_lane(west_side[0:1, :], corner_lane, 0))
            lev_at_e = shift_east(near_lev, lane1, to_lane(east_side[0:1, :], corner_lane, last_lane))
            wet_near = wet(near_lev)
            zonal = cross[ZONAL_ROW * sz.lev : (ZONAL_ROW + 1) * sz.lev, :]
            p = r * (sz.nf + 2)
            zonal_w = shift_west(zonal, lane16, to_lane(west_corner, p + sz.nf, 0))
            flow_e = keep(wet_near & wet(lev_at_e), zonal)
            flow_w = keep(wet_near & wet(lev_at_w), zonal_w)
            merid = cross[MERID_ROW * sz.lev : (MERID_ROW + 1) * sz.lev, :]
            if r == 0:
                merid_far = cross[MERID_ROW2 * sz.lev : (MERID_ROW2 + 1) * sz.lev, :]
                flow_n = keep(wet_near & wet(own_lev), merid)
                flow_s = keep(wet_near & wet(far_lev), merid_far)
            else:
                flow_n = keep(wet_near & wet(far_lev), merid)
                flow_s = keep(wet_near & wet(own_lev), level_rows(bulk, 0, last_row, sz))
            weights = Weights(flow_e, flow_w, flow_n, flow_s, step)
            for f in range(sz.nf):
                at = 2 * f * sz.lev
                near, far = rows[at : at + sz.lev, :], rows[at + sz.lev : at + 2 * sz.lev, :]
                inside = level_rows(fields, f * sz.slab, edge, sz)
                at_w = shift_west(near, lane16, to_lane(west_corner, p + f, 0))
                at_e = shift_east(near, lane16, to_lane(east_corner, p + f, last_lane))
                up, down = (inside, far) if r == 0 else (far, inside)
                strip[f * sz.lev : (f + 1) * sz.lev, :] = weights.apply(near, at_e, at_w, up, down)

    def transport(step):
        west_old = from_west[0 : sz.rows, :]
        zero = jnp.zeros(tile, jnp.float32)

        def faces(k):
            if k == sz.lev:
                return zero, zero
            at = k * sz.rows
            speed, mixing = vert[at : at + sz.rows, :], mix[at : at + sz.rows, :]
            return jnp.maximum(speed, 0.0) + mixing, jnp.minimum(speed, 0.0) - mixing

        every = range(sz.nf)

        def stored_weights(k):
            at = k * sz.rows
            return Weights.of(*(wref[i * sz.slab + at : i * sz.slab + at + sz.rows, :] for i in range(5)))

        for k in range(sz.lev):
            at = k * sz.rows
            wet, wet_e, wet_w, wet_n, wet_s = masks(k)
            zonal_at = zonal_place(sz) + at if at < early(sz) else 2 * sz.slab + at - early(sz)
            zonal = (side if at < early(sz) else bulk)[zonal_at : zonal_at + sz.rows, :]
            merid = bulk[at : at + sz.rows, :]
            zonal_first = sz.nf * sz.lev
            zonal_west = shift_west(zonal, lane, to_lane(west_old, zonal_first + k, 0))
            beyond = MERID_ROW * sz.lev + k
            merid_south = shift_south(merid, row, cross_south[beyond : beyond + 1, :])
            flow_e, flow_w, flow_n, flow_s = (
                keep(wet_e, zonal), keep(wet_w, zonal_west), keep(wet_n, merid), keep(wet_s, merid_south)
            )
            div[at : at + sz.rows, :] = flow_e - flow_w + (flow_n - flow_s)
            weights = Weights(flow_e, flow_w, flow_n, flow_s, step)
            for i, part in enumerate(weights.parts()):
                wref[i * sz.slab + at : i * sz.slab + at + sz.rows, :] = part
        row_strips(step)
        for k in range(sz.lev):
            at = k * sz.rows
            weights = stored_weights(k)
            for f in every:
                here = slice(f * sz.slab + at, f * sz.slab + at + sz.rows)
                forward[here, :] = weights.apply(*(ref[here, :] for ref in (fields, around_e, around_w, around_n, around_s)))
        at_edge = (lane == 0) | (lane == last_lane)
        total = zero
        for k in range(sz.lev - 1, -1, -1):
            at = k * sz.rows
            total = total + div[at : at + sz.rows, :]
            vert[at : at + sz.rows, :] = -total if k > 0 else zero
            mixing = bulk[sz.slab + at : sz.slab + at + sz.rows, :]
            mix[at : at + sz.rows, :] = jnp.where(at_edge, edge_mix[at : at + sz.rows, :], mixing)
        last_ratio = None
        up, down = faces(0)
        lower, inverse = [], []
        for k in range(sz.lev):
            at = k * sz.rows
            up_next, down_next = faces(k + 1)
            pivot = 1.0 + TIME_STEP * (up - down_next)
            lower.append(TIME_STEP * down)
            if k > 0:
                pivot = pivot - lower[k] * last_ratio
            inverse.append(1.0 / pivot)
            last_ratio = -TIME_STEP * up_next * inverse[k]
            ratio[at : at + sz.rows, :] = last_ratio
            inv_ref[at : at + sz.rows, :] = inverse[k]
            pull[at : at + sz.rows, :] = lower[k] * inverse[k]
            up, down = up_next, down_next
        previous = [None] * sz.nf
        for k in range(sz.lev):
            at = k * sz.rows
            weights = stored_weights(k)
            values = [forward[f * sz.slab + at : f * sz.slab + at + sz.rows, :] for f in every]
            to_e, to_w = [turn(value, -1, 1) for value in values], [turn(value, 1, 1) for value in values]
            for f in every:
                here = slice(f * sz.slab + at, f * sz.slab + at + sz.rows)
                beyond = slice(f * sz.lev + k, f * sz.lev + k + 1)
                edge = second[here, :]
                value = weights.apply(
                    values[f],
                    jnp.where(lane == last_lane, edge, to_e[f]),
                    jnp.where(lane == 0, edge, to_w[f]),
                    shift_north(values[f], row, high_strip[beyond, :]),
                    shift_south(values[f], row, low_strip[beyond, :]),
                )
                moved[here, :] = value * inv_ref[at : at + sz.rows, :]
        for k in range(sz.lev):
            at = k * sz.rows
            for f in every:
                here = f * sz.slab + at
                value = moved[here : here + sz.rows, :]
                if k > 0:
                    value = value - pull[at : at + sz.rows, :] * previous[f]
                forward[here : here + sz.rows, :] = value
                previous[f] = value
        for k in range(sz.lev - 1, -1, -1):
            at = k * sz.rows
            wet = lev > k
            for f in range(sz.nf):
                here = f * sz.slab + at
                if k < sz.lev - 1:
                    previous[f] = forward[here : here + sz.rows, :] - ratio[at : at + sz.rows, :] * previous[f]
                out[f, at : at + sz.rows, :] = keep(wet, previous[f])
            if k % chunk == 0:
                send(0, sz.nf, k // chunk)

    @pl.when(is_dynamics)
    def _():
        physics()
        finish_copies()

    @pl.when(jnp.logical_not(is_dynamics))
    def _():
        transport(TIME_STEP / NSUB)
        finish_copies()


def pair_of(index, count, odd):
    if not odd:
        return index ^ 1
    return (((index + 1) ^ 1) - 1) % count


def on_device(sizes_of, fields, levels):
    sz = Sizes(fields, levels)
    count_s, count_o, count_a = sizes_of
    flat = fields.reshape(sz.nf * sz.slab, sz.cols)

    def place(s, o, a):
        return (s * count_o + o) * count_a + a

    def partner(s, o, a, odd, hop):
        b = pair_of(a, count_a, odd)
        if abs(a - b) > 1 and count_o % 2 == 0:
            return place(s, o ^ 1, a)
        return place((s + hop) % count_s, o, b)

    def swap(value, odd, hop=0):
        pairs = [
            (place(s, o, a), partner(s, o, a, odd, hop))
            for s in range(count_s)
            for o in range(count_o)
            for a in range(count_a)
        ]
        return lax.ppermute(value, ("sect", "lon", "lat"), pairs)

    def from_dynamics(value, odd=None):
        mine = lax.axis_index("sect")
        got = None
        for hop in range(1, count_s):
            if odd is None:
                part = lax.ppermute(value, "sect", [(s, (s + hop) % count_s) for s in range(count_s)])
            else:
                part = swap(value, odd, hop)
            got = part if got is None else jnp.where(mine == hop, part, got)
        return got

    def around(value, step):
        return lax.ppermute(value, "lon", [(i, (i + step) % count_o) for i in range(count_o)])

    rows_shape = (2 * sz.nf * sz.lev, sz.cols)
    cross_shape = (LEVEL_ROW * sz.lev + 8, sz.cols)
    columns_shape = (4 * sz.rows + sz.lev, sz.cols)
    side_shape = (4 * sz.rows, sz.cols)
    row_a, row_b, own_side = call_kernel(functools.partial(pack_edges, sz), [rows_shape, rows_shape, side_shape], [flat])
    twin_shape = (zonal_place(sz) + early(sz), sz.cols)
    wide_shape = (max(cross_shape[0], twin_shape[0] + 8), sz.cols)
    (cross_b,) = call_kernel(functools.partial(pack_cross, sz), [wide_shape], [flat, levels])
    row_a = swap(row_a, False)
    levels_a = swap(levels, False)
    row_b = swap(row_b, True)
    (twin,) = call_kernel(
        functools.partial(pack_twin, sz), [twin_shape], [flat, own_side, row_a]
    )
    twin = from_dynamics(twin)
    cross_b = from_dynamics(cross_b, True)
    south, north, corners = call_kernel(
        functools.partial(place_rows, sz), [rows_shape, rows_shape, (sz.rows, sz.cols)], [row_a, row_b]
    )
    to_east, to_west, cross_south, cross_north, bulk = call_kernel(
        functools.partial(pack_columns, sz),
        [columns_shape] * 2 + [cross_shape] * 2 + [(3 * sz.slab - early(sz), sz.cols)],
        [flat, levels, levels_a, south, north, corners, twin, cross_b, own_side],
    )
    bulk = from_dynamics(bulk)
    from_east = around(to_west, -1)
    from_west = around(to_east, 1)
    kept, moved_e, moved_w, around_n, around_s = call_kernel(
        functools.partial(shift_fields, sz), [flat.shape] * 5, [flat, south, north]
    )
    slab = (sz.slab, sz.cols)
    around_e, around_w, second, edge_mix = call_kernel(
        functools.partial(column_edges, sz),
        [flat.shape] * 3 + [slab],
        [levels, cross_south, cross_north, to_east, to_west, twin, from_west, from_east, moved_e, moved_w],
    )
    out_shape = (sz.nf, sz.slab, sz.cols)
    strip = (sz.nf * sz.lev, sz.cols)
    (out,) = call_kernel(
        functools.partial(finish, sz),
        [out_shape],
        [
            kept, levels, south, north, cross_south, cross_north, bulk, twin, from_west, from_east,
            moved_e, moved_w, around_e, around_w, around_n, around_s, second, edge_mix,
        ],
        [out_shape, slab, slab, slab, strip, strip, slab, flat.shape, slab, (5 * sz.slab, sz.cols), slab, flat.shape],
        copies=3 * CHUNKS,
    )
    return out.reshape(fields.shape)


def solution(mesh):
    sizes_of = (mesh.shape["sect"], mesh.shape["lon"], mesh.shape["lat"])
    return jax.shard_map(
        functools.partial(on_device, sizes_of),
        mesh=mesh,
        in_specs=(P("sect", None, None, "lat", "lon"), P("lat", "lon")),
        out_specs=P("sect", None, None, "lat", "lon"),
        check_vma=False,
    )
```

```python
import functools
import jax
import jax.numpy as jnp
from jax import lax
from jax.experimental import pallas as pl
from jax.experimental.pallas import tpu as pltpu
from jax.sharding import PartitionSpec as P

NSUB = 2
TIME_STEP = 1.0
CORIOLIS = 0.3
THERMAL = 0.2
HALINE = 0.15
GRAVITY_SCALE = 0.05
MIX_BOOST = 4.0
RICHARDSON = 1.0

VMEM_LIMIT = 8 * 1024 * 1024
CHUNKS = 4
EARLY_LEVELS = 0

ZONAL_ROW, MERID_ROW, MERID_ROW2, END_ROW, LEVEL_ROW = range(5)
TEMPER_END, VISC_END = 0, 2


def call_kernel(body, outputs, inputs, scratch=(), copies=0):
    in_vmem = pl.BlockSpec(memory_space=pltpu.VMEM)
    scratch = [pltpu.VMEM(shape, jnp.float32) for shape in scratch]
    if copies:
        scratch.append(pltpu.SemaphoreType.DMA((copies,)))
    return pl.pallas_call(
        body,
        out_shape=[jax.ShapeDtypeStruct(shape, jnp.float32) for shape in outputs],
        in_specs=[in_vmem] * len(inputs),
        out_specs=[pl.BlockSpec(memory_space=pl.ANY) if copies else in_vmem] * len(outputs),
        scratch_shapes=scratch,
        compiler_params=pltpu.CompilerParams(vmem_limit_bytes=VMEM_LIMIT),
    )(*inputs)


class Sizes:
    def __init__(self, fields, levels):
        self.nf, self.lev = fields.shape[1], fields.shape[2]
        self.rows, self.cols = levels.shape
        self.slab = self.lev * self.rows


def lane_ids(shape):
    return lax.broadcasted_iota(jnp.int32, shape, 1)


def row_ids(shape):
    return lax.broadcasted_iota(jnp.int32, shape, 0)


def turn(value, shift, axis):
    size = value.shape[axis]
    shift = shift % size
    return value if shift == 0 else pltpu.roll(value, shift, axis)


def to_lane(value, source, target):
    return turn(value, target - source, 1)


def level_rows(ref, first, row, sz):
    return ref[pl.ds(first + row, sz.lev, stride=sz.rows), :]


def send_north_first(sz, fill):
    even = lax.axis_index("lat") % 2 == 0
    top, second = sz.rows - 1, sz.rows - 2

    @pl.when(even)
    def _():
        fill(0, top, second)
        fill(1, 0, 1)

    @pl.when(jnp.logical_not(even))
    def _():
        fill(0, 0, 1)
        fill(1, top, second)


def pack_edges(sz, fields, row_a, row_b, side, zonal, merid):
    zonal[...] = fields[0 : sz.slab, :]
    merid[...] = fields[sz.slab : 2 * sz.slab, :]

    def fill(which, near, far):
        message = (row_a, row_b)[which]
        for f in range(sz.nf):
            for r, row in enumerate((near, far)):
                at = (2 * f + r) * sz.lev
                message[at : at + sz.lev, :] = level_rows(fields, f * sz.slab, row, sz)

    send_north_first(sz, fill)
    for place, column in enumerate(edge_columns(sz, fields, sz.nf, 0)):
        side[place * sz.rows : (place + 1) * sz.rows, :] = column


def pack_cross(sz, fields, levels, cross):
    lev = levels[...].astype(jnp.float32)

    def fill(which, near, far):
        if which == 0:
            return
        for at, (f, row) in enumerate(((0, near), (1, near), (1, far))):
            cross[at * sz.lev : (at + 1) * sz.lev, :] = level_rows(fields, f * sz.slab, row, sz)
        cross[END_ROW * sz.lev : (END_ROW + 1) * sz.lev, :] = row_ends(
            level_rows(fields, 2 * sz.slab, near, sz), level_rows(fields, 4 * sz.slab, near, sz)
        )
        at = LEVEL_ROW * sz.lev
        cross[at : at + 1, :] = lev[near : near + 1, :]
        cross[at + 1 : at + 2, :] = lev[far : far + 1, :]
        cross[at + 2 :, :] = jnp.zeros((cross.shape[0] - at - 2, sz.cols), jnp.float32)

    send_north_first(sz, fill)


def row_ends(temper, visc):
    lane = lane_ids(temper.shape)
    ends = jnp.where(lane == TEMPER_END, temper, turn(temper, TEMPER_END + 2, 1))
    ends = jnp.where(lane == VISC_END, turn(visc, VISC_END, 1), ends)
    return jnp.where(lane == VISC_END + 1, turn(visc, VISC_END + 2, 1), ends)


def pack_twin(sz, fields, own_side, row_a, twin):
    base = 4 * sz.rows
    twin[0:base, :] = own_side[...]
    def row_of(f, r):
        first = (2 * f + r) * sz.lev
        return row_a[first : first + sz.lev, :]

    parts = (row_of(0, 0), row_of(1, 0), row_of(1, 1), row_ends(row_of(2, 0), row_of(4, 0)))
    for at, part in enumerate(parts):
        twin[base + at * sz.lev : base + (at + 1) * sz.lev, :] = part
    if early(sz):
        twin[zonal_place(sz) : zonal_place(sz) + early(sz), :] = fields[0 : early(sz), :]


def early(sz):
    return EARLY_LEVELS * sz.rows


def zonal_place(sz):
    return 4 * sz.rows + LEVEL_ROW * sz.lev


def edge_columns(sz, ref, count, first):
    tile = (sz.rows, sz.cols)
    lane = lane_ids(tile)
    zero = jnp.zeros(tile, jnp.float32)
    last = sz.cols - 1
    east_one, west_one, east_two, west_two = zero, zero, zero, zero
    for f in range(count):
        for k in range(sz.lev):
            at = f * sz.slab + k * sz.rows
            p = (first + f) * sz.lev + k
            moved = to_lane(ref[at : at + sz.rows, :], last, p)
            east_one = jnp.where(lane == p, moved, east_one)
            west_one = jnp.where(lane == (p + 1) % sz.cols, moved, west_one)
            west_two = jnp.where(lane == (p + 2) % sz.cols, moved, west_two)
            east_two = jnp.where(lane == (p - 1) % sz.cols, moved, east_two)
    return east_one, turn(west_one, -1, 1), turn(east_two, 1, 1), turn(west_two, -2, 1)


def place_rows(sz, row_a, row_b, south, north, corners):
    position = lax.axis_index("lat")
    even = position % 2 == 0
    first, other = row_a[...], row_b[...]
    tall = (sz.lev, sz.cols)
    lane, depth = lane_ids(tall), row_ids(tall)
    low = jnp.where(position > 0, jnp.where(even, other, first), 0.0)
    high = jnp.where(position < lax.axis_size("lat") - 1, jnp.where(even, first, other), 0.0)
    south[...] = low
    north[...] = high
    ends = []
    for column in (sz.cols - 1, 0):
        for rows in (low, high):
            total = jnp.zeros(tall, jnp.float32)
            for f in range(sz.nf):
                near = rows[2 * f * sz.lev : (2 * f + 1) * sz.lev, :]
                spread = jnp.broadcast_to(near[:, column : column + 1], tall)
                total = jnp.where(lane == f * sz.lev + depth, spread, total)
            ends.append(jnp.sum(total, axis=0, keepdims=True))
    for i, end in enumerate(ends):
        corners[i : i + 1, :] = end
    corners[len(ends) :, :] = jnp.zeros((sz.rows - len(ends), sz.cols), jnp.float32)


def beside_levels(sz, levels_a, cross_b):
    even = lax.axis_index("lat") % 2 == 0
    partner = levels_a[...].astype(jnp.float32)
    level_row = LEVEL_ROW * sz.lev

    def row_at(low, high):
        return jnp.where(even, partner[low : low + 1, :], partner[high : high + 1, :])

    near_b, far_b = (cross_b[level_row + i : level_row + i + 1, :] for i in range(2))
    return row_at(0, sz.rows - 1), row_at(1, sz.rows - 2), near_b, far_b


def pack_mixing(sz, fields, levels, levels_a, cross_b, south, north, mixing_out):
    position = lax.axis_index("lat")
    even = position % 2 == 0
    near_a, _, near_b, _ = beside_levels(sz, levels_a, cross_b)
    south_lev = jnp.where(position > 0, jnp.where(even, near_b, near_a), 0.0)
    north_lev = jnp.where(position < lax.axis_size("lat") - 1, jnp.where(even, near_a, near_b), 0.0)
    tile = (sz.rows, sz.cols)
    lev = levels[...].astype(jnp.float32)

    @pl.when(lax.axis_index("sect") == 0)
    def _():
        row = row_ids(tile)
        lev_e, lev_w = turn(lev, -1, 1), turn(lev, 1, 1)
        lev_n, lev_s = shift_north(lev, row, north_lev), shift_south(lev, row, south_lev)
        warm_above = None
        for k in range(sz.lev):
            at = k * sz.rows

            def around(f):
                value = fields[f * sz.slab + at : f * sz.slab + at + sz.rows, :]
                beyond = 2 * f * sz.lev + k
                return (
                    value, turn(value, -1, 1), turn(value, 1, 1),
                    shift_north(value, row, north[beyond : beyond + 1, :]),
                    shift_south(value, row, south[beyond : beyond + 1, :]),
                )

            wet = lev > k
            masks = wet, wet & (lev_e > k), wet & (lev_w > k), wet & (lev_n > k), wet & (lev_s > k)
            warm = diffused(around(2), around(4), masks)
            background = fields[5 * sz.slab + at : 5 * sz.slab + at + sz.rows, :]
            mixing = jnp.zeros(tile, jnp.float32) if k == 0 else mixed(warm_above, warm, background, wet)
            warm_above = warm
            mixing_out[at : at + sz.rows, :] = mixing


def pack_columns(
    sz, levels, levels_a, south, north, corners, twin, cross_b, own_side,
    to_east, to_west, cross_south, cross_north,
):
    position = lax.axis_index("lat")
    even = position % 2 == 0
    has_south = position > 0
    has_north = position < lax.axis_size("lat") - 1
    tile = (sz.rows, sz.cols)
    lane = lane_ids(tile)
    last = sz.cols - 1
    side = twin
    level_row = LEVEL_ROW * sz.lev
    near_a, far_a, near_b, far_b = beside_levels(sz, levels_a, cross_b)
    pairs = (
        (cross_south, cross_north, slice(0, level_row), twin[4 * sz.rows : 4 * sz.rows + level_row, :], cross_b[0:level_row, :]),
        (cross_south, cross_north, slice(level_row, level_row + 1), near_a, near_b),
        (cross_south, cross_north, slice(level_row + 1, level_row + 2), far_a, far_b),
    )
    for low, high, at, first, other in pairs:
        low[at, :] = jnp.where(has_south, jnp.where(even, other, first), 0.0)
        high[at, :] = jnp.where(has_north, jnp.where(even, first, other), 0.0)
    for ref in (cross_south, cross_north):
        ref[level_row + 2 : level_row + 8, :] = jnp.zeros((6, sz.cols), jnp.float32)

    tracer_lanes = lane < sz.nf * sz.lev
    for place, (message, at) in enumerate(((to_east, 0), (to_west, 0), (to_east, sz.rows), (to_west, sz.rows))):
        own = own_side[place * sz.rows : (place + 1) * sz.rows, :]
        dynamics = side[place * sz.rows : (place + 1) * sz.rows, :]
        message[at : at + sz.rows, :] = jnp.where(tracer_lanes, own, turn(dynamics, sz.nf * sz.lev, 1))

    lev = levels[...].astype(jnp.float32)
    south_lev = cross_south[level_row : level_row + 1, :]
    north_lev = cross_north[level_row : level_row + 1, :]
    base = 2 * sz.lev
    for place, (message, near, far) in enumerate(((to_east, last, last - 1), (to_west, 0, 1))):
        part = side[place * sz.rows : (place + 1) * sz.rows, :]
        part = jnp.where(lane < sz.lev, turn(part, -2 * sz.lev, 1), turn(part, -3 * sz.lev, 1))
        part = jnp.where(lane == base, to_lane(lev, near, base), part)
        part = jnp.where(lane == base + 1, to_lane(lev, far, base + 1), part)
        low = jnp.broadcast_to(to_lane(south_lev, near, base + 2), tile)
        high = jnp.broadcast_to(to_lane(north_lev, near, base + 3), tile)
        part = jnp.where(lane == base + 2, low, part)
        part = jnp.where(lane == base + 3, high, part)
        message[2 * sz.rows : 3 * sz.rows, :] = part

    tall = (sz.lev, sz.cols)
    tall_lane = lane_ids(tall)
    east_corner = jnp.zeros(tall, jnp.float32)
    west_corner = east_corner
    for r, (rows, cross) in enumerate(((south, cross_south), (north, cross_north))):
        for f in range(sz.nf + 2):
            if f < sz.nf:
                values = rows[2 * f * sz.lev : (2 * f + 1) * sz.lev, :]
            else:
                at = (ZONAL_ROW, MERID_ROW)[f - sz.nf] * sz.lev
                values = cross[at : at + sz.lev, :]
            p = r * (sz.nf + 2) + f
            moved = to_lane(values, last, p)
            east_corner = jnp.where(tall_lane == p, moved, east_corner)
            west_corner = jnp.where(tall_lane == p + 1, moved, west_corner)
    to_east[3 * sz.rows : 3 * sz.rows + sz.lev, :] = east_corner
    to_west[3 * sz.rows : 3 * sz.rows + sz.lev, :] = turn(west_corner, -1, 1)
    ends = corners[...]
    to_east[3 * sz.rows + sz.lev :, :] = ends
    to_west[3 * sz.rows + sz.lev :, :] = turn(ends, -2, 0)


def keep(mask, value):
    return jnp.where(mask, value, 0.0)


def diffused(quantity, viscosity, masks):
    mid, e, w, n, s = quantity
    visc, visc_e, visc_w, visc_n, visc_s = viscosity
    _, wet_e, wet_w, wet_n, wet_s = masks
    change = (
        keep(wet_e, 0.5 * (visc + visc_e)) * (e - mid)
        - keep(wet_w, 0.5 * (visc_w + visc)) * (mid - w)
        + keep(wet_n, 0.5 * (visc + visc_n)) * (n - mid)
        - keep(wet_s, 0.5 * (visc_s + visc)) * (mid - s)
    )
    return mid + TIME_STEP * change


def mixed(warm_above, warm, background, wet):
    jump = THERMAL * (warm_above - warm)
    return keep(wet, background * (1.0 + MIX_BOOST / (1.0 + RICHARDSON * jump * jump)))


def shift_west(value, lane, edge):
    return jnp.where(lane == 0, edge, turn(value, 1, 1))


def shift_east(value, lane, edge):
    return jnp.where(lane == value.shape[1] - 1, edge, turn(value, -1, 1))


def shift_south(value, row, edge):
    return jnp.where(row == 0, edge, turn(value, 1, 0))


def shift_north(value, row, edge):
    return jnp.where(row == value.shape[0] - 1, edge, turn(value, -1, 0))


class Weights:
    def __init__(self, east, west, north, south, step):
        self.own = 1.0 - step * (
            jnp.maximum(east, 0.0) - jnp.minimum(west, 0.0) + (jnp.maximum(north, 0.0) - jnp.minimum(south, 0.0))
        )
        self.east = -step * jnp.minimum(east, 0.0)
        self.west = step * jnp.maximum(west, 0.0)
        self.north = -step * jnp.minimum(north, 0.0)
        self.south = step * jnp.maximum(south, 0.0)

    def parts(self):
        return self.own, self.east, self.west, self.north, self.south

    @classmethod
    def of(cls, own, east, west, north, south):
        weights = cls.__new__(cls)
        weights.own, weights.east, weights.west, weights.north, weights.south = own, east, west, north, south
        return weights

    def apply(self, own, east, west, north, south):
        return self.own * own + self.east * east + self.west * west + (self.north * north + self.south * south)


def shift_fields(
    sz, fields, levels, south, north, cross_south, cross_north, kept, moved_e, moved_w, around_n, around_s
):
    kept[...] = fields[...]
    tile = (sz.rows, sz.cols)
    row = row_ids(tile)
    for at in range(0, sz.nf * sz.slab, sz.rows):
        here = slice(at, at + sz.rows)
        value = fields[here, :]
        moved_e[here, :] = turn(value, -1, 1)
        moved_w[here, :] = turn(value, 1, 1)

    def along_lat(f, k):
        value = fields[f * sz.slab + k * sz.rows : f * sz.slab + (k + 1) * sz.rows, :]
        beyond = slice(2 * f * sz.lev + k, 2 * f * sz.lev + k + 1)
        return value, shift_north(value, row, north[beyond, :]), shift_south(value, row, south[beyond, :])

    is_dynamics = lax.axis_index("sect") == 0

    @pl.when(jnp.logical_not(is_dynamics))
    def _():
        for f in range(sz.nf):
            for k in range(sz.lev):
                here = slice(f * sz.slab + k * sz.rows, f * sz.slab + (k + 1) * sz.rows)
                _, around_n[here, :], around_s[here, :] = along_lat(f, k)

    @pl.when(is_dynamics)
    def _():
        lev = levels[...].astype(jnp.float32)
        level_row = LEVEL_ROW * sz.lev
        lev_n = shift_north(lev, row, cross_north[level_row : level_row + 1, :])
        lev_s = shift_south(lev, row, cross_south[level_row : level_row + 1, :])
        press = jnp.zeros(tile, jnp.float32)
        press_n = press
        for k in range(sz.lev):
            wet, wet_n, wet_s = lev > k, lev_n > k, lev_s > k
            zonal, merid, temper, saline, visc = (along_lat(f, k) for f in range(5))
            coef_n = keep(wet & wet_n, 0.5 * (visc[0] + visc[1]))
            coef_s = keep(wet & wet_s, 0.5 * (visc[2] + visc[0]))

            def advanced(quantity):
                mid, n, s = quantity
                return mid + TIME_STEP * (coef_n * (n - mid) - coef_s * (mid - s))

            def weight(place, wet_there):
                return keep(wet_there, HALINE * saline[place] - THERMAL * temper[place])

            press = press + GRAVITY_SCALE * weight(0, wet)
            press_n = press_n + GRAVITY_SCALE * weight(1, wet_n)
            parts = (
                advanced(zonal) + TIME_STEP * CORIOLIS * merid[0],
                advanced(merid) - TIME_STEP * (CORIOLIS * zonal[0] + (press_n - press)),
                advanced(temper),
                advanced(saline),
                press,
                keep(wet & wet_n, merid[0]) - keep(wet & wet_s, merid[2]),
            )
            for f, part in enumerate(parts):
                around_n[f * sz.slab + k * sz.rows : f * sz.slab + (k + 1) * sz.rows, :] = part


def column_edges(
    sz, levels, cross_south, cross_north, own_east, own_west, side, from_west, from_east, moved_e, moved_w,
    around_e, around_w, second, edge_mix,
):
    tile = (sz.rows, sz.cols)
    lane, row = lane_ids(tile), row_ids(tile)
    last_lane, last_row = sz.cols - 1, sz.rows - 1
    lev = levels[...].astype(jnp.float32)
    level_row = LEVEL_ROW * sz.lev
    side_base = 2 * sz.lev
    west_side = from_west[2 * sz.rows : 3 * sz.rows, :]
    east_side = from_east[2 * sz.rows : 3 * sz.rows, :]
    lev_w = shift_west(lev, lane, to_lane(west_side, side_base, 0))
    lev_e = shift_east(lev, lane, to_lane(east_side, side_base, last_lane))
    south_lev, north_lev = cross_south[level_row : level_row + 1, :], cross_north[level_row : level_row + 1, :]
    lev_s = shift_south(lev, row, south_lev)
    lev_n = shift_north(lev, row, north_lev)

    def masks(k):
        wet = lev > k
        return wet, wet & (lev_e > k), wet & (lev_w > k), wet & (lev_n > k), wet & (lev_s > k)

    def column(value, at):
        return jnp.broadcast_to(value[:, at : at + 1], value.shape)

    def both(west, east):
        return jnp.concatenate([west, east], axis=0)

    tall = (sz.lev, sz.cols)
    pair_row = row_ids((2 * sz.rows, sz.cols)) % sz.rows
    pair_lane = lane_ids((2 * sz.rows, sz.cols))

    def pair_south(value, edge):
        return jnp.where(pair_row == 0, edge, turn(value, 1, 0))

    def pair_north(value, edge):
        return jnp.where(pair_row == last_row, edge, turn(value, -1, 0))

    def edge_mixing():
        diagonal = lane_ids(tall) == row_ids(tall)

        def levels_in_lanes(rows, at):
            return jnp.broadcast_to(jnp.sum(keep(diagonal, column(rows, at)), axis=0, keepdims=True), tile)

        def place(index):
            return side[index * sz.rows : (index + 1) * sz.rows, :]

        own_pair, inner_w, inner_e = both(place(1), place(0)), place(3), place(2)

        def around(f, message_lane, end):
            shift = -f * sz.lev
            outer_w, outer_e = turn(west_side, -message_lane, 1), turn(east_side, -message_lane, 1)
            own = turn(own_pair, shift, 1)
            low, high = (cross[END_ROW * sz.lev : (END_ROW + 1) * sz.lev, :] for cross in (cross_south, cross_north))
            return (
                own,
                both(turn(inner_w, shift, 1), outer_e),
                both(outer_w, turn(inner_e, shift, 1)),
                pair_north(own, both(levels_in_lanes(high, end), levels_in_lanes(high, end + 1))),
                pair_south(own, both(levels_in_lanes(low, end), levels_in_lanes(low, end + 1))),
            )

        depth = pair_lane.astype(jnp.float32)

        def wet(value):
            return both(column(value, 0), column(value, last_lane)) > depth

        mid = wet(lev)
        mask = mid, mid & wet(lev_e), mid & wet(lev_w), mid & wet(lev_n), mid & wet(lev_s)
        warm = diffused(around(2, 0, TEMPER_END), around(4, sz.lev, VISC_END), mask)
        background = turn(own_pair, -5 * sz.lev, 1)
        return jnp.where(pair_lane == 0, 0.0, mixed(turn(warm, 1, 1), warm, background, mid))

    def column_strips(step):
        lane16, depth16 = lane_ids(tall), row_ids(tall)

        def all_fields(value, first):
            at = lane_ids(value.shape)
            value = jnp.where((at >= first) & (at < first + sz.lev), value, 0.0)
            width = sz.lev
            while width < sz.cols:
                value = value + turn(value, width, 1)
                width *= 2
            return value

        def corner_rows(message, r):
            items = message[3 * sz.rows : 3 * sz.rows + sz.lev, :]
            p = r * (sz.nf + 2)
            ends = 3 * sz.rows + sz.lev + r
            tracers = message[ends : ends + 1, :]
            spread = jnp.broadcast_to(items[:, p + sz.nf + 1 : p + sz.nf + 2], tall)
            velocity = jnp.where(lane16 % sz.lev == depth16, spread, 0.0)
            return tracers, jnp.sum(velocity, axis=0, keepdims=True)

        inside_w, inside_e = own_west[0 : sz.rows, :], own_east[0 : sz.rows, :]
        near = both(from_west[0 : sz.rows, :], from_east[0 : sz.rows, :])
        far_w, far_e = from_west[sz.rows : 2 * sz.rows, :], from_east[sz.rows : 2 * sz.rows, :]
        corners = [corner_rows(message, r) for message in (from_west, from_east) for r in range(2)]
        low_tracers, high_tracers, low_merid = (
            both(jnp.broadcast_to(corners[i][part], tile), jnp.broadcast_to(corners[i + 2][part], tile))
            for i, part in ((0, 0), (1, 0), (0, 1))
        )

        def side_levels(at):
            return column(west_side, at), column(east_side, at)

        near_lev = both(*side_levels(side_base))
        far_lev_w, far_lev_e = side_levels(side_base + 1)
        own_lev_w, own_lev_e = column(lev, 0), column(lev, last_lane)
        lev_at_s = pair_south(near_lev, both(*side_levels(side_base + 2)))
        lev_at_n = pair_north(near_lev, both(*side_levels(side_base + 3)))
        depth = (lane_ids(near.shape) % sz.lev).astype(jnp.float32)
        wet_near = near_lev > depth
        zonal_first = sz.nf * sz.lev
        west, east = both(far_w, inside_e), both(inside_w, far_e)
        flow_e = keep(wet_near & (both(own_lev_w, far_lev_e) > depth), all_fields(near, zonal_first))
        flow_w = keep(wet_near & (both(far_lev_w, own_lev_e) > depth), all_fields(west, zonal_first))
        merid = all_fields(near, zonal_first + sz.lev)
        flow_n = keep(wet_near & (lev_at_n > depth), merid)
        flow_s = keep(wet_near & (lev_at_s > depth), pair_south(merid, low_merid))
        weights = Weights(flow_e, flow_w, flow_n, flow_s, step)
        return weights.apply(near, east, west, pair_north(near, high_tracers), pair_south(near, low_tracers))

    @pl.when(lax.axis_index("sect") > 0)
    def _():
        west_old, east_old = from_west[0 : sz.rows, :], from_east[0 : sz.rows, :]
        strips = column_strips(TIME_STEP / NSUB)
        west_new, east_new = strips[0 : sz.rows, :], strips[sz.rows : 2 * sz.rows, :]
        edges = edge_mixing()
        edge_w, edge_e = edges[0 : sz.rows, :], edges[sz.rows : 2 * sz.rows, :]
        first, last = lane == 0, lane == last_lane
        for k in range(sz.lev):
            at = k * sz.rows
            edge_mix[at : at + sz.rows, :] = jnp.where(first, to_lane(edge_w, k, 0), to_lane(edge_e, k, last_lane))
            for f in range(sz.nf):
                here = slice(f * sz.slab + at, f * sz.slab + at + sz.rows)
                p = f * sz.lev + k
                around_e[here, :] = jnp.where(last, to_lane(east_old, p, last_lane), moved_e[here, :])
                around_w[here, :] = jnp.where(first, to_lane(west_old, p, 0), moved_w[here, :])
        for k in range(sz.lev):
            for f in range(sz.nf):
                here = slice(f * sz.slab + k * sz.rows, f * sz.slab + (k + 1) * sz.rows)
                p = f * sz.lev + k
                second[here, :] = jnp.where(first, to_lane(west_new, p, 0), to_lane(east_new, p, last_lane))


def finish(
    sz, fields, levels, south, north, cross_south, cross_north, zonal_in, merid_in, mixing_in,
    side, from_west, from_east, moved_e, moved_w, around_e, around_w, around_n, around_s, second, edge_mix,
    result, out, div, mix, vert, low_strip, high_strip, ratio, forward, inv_ref, wref, pull, moved, sent,
):
    tile = (sz.rows, sz.cols)
    lane, row = lane_ids(tile), row_ids(tile)
    last_lane, last_row = sz.cols - 1, sz.rows - 1
    lev = levels[...].astype(jnp.float32)
    level_row = LEVEL_ROW * sz.lev
    side_base = 2 * sz.lev
    west_side = from_west[2 * sz.rows : 3 * sz.rows, :]
    east_side = from_east[2 * sz.rows : 3 * sz.rows, :]
    lev_w = shift_west(lev, lane, to_lane(west_side, side_base, 0))
    lev_e = shift_east(lev, lane, to_lane(east_side, side_base, last_lane))
    south_lev, north_lev = cross_south[level_row : level_row + 1, :], cross_north[level_row : level_row + 1, :]
    lev_s = shift_south(lev, row, south_lev)
    lev_n = shift_north(lev, row, north_lev)

    def masks(k):
        wet = lev > k
        return wet, wet & (lev_e > k), wet & (lev_w > k), wet & (lev_n > k), wet & (lev_s > k)

    is_dynamics = lax.axis_index("sect") == 0
    chunk = sz.lev // CHUNKS
    copies = []

    def send(first, last, part):
        at = pl.ds(part * chunk * sz.rows, chunk * sz.rows)
        copy = pltpu.make_async_copy(
            out.at[pl.ds(first, last - first), at, :], result.at[pl.ds(first, last - first), at, :], sent.at[len(copies)]
        )
        copy.start()
        copies.append(copy)

    def finish_copies():
        for copy in copies:
            copy.wait()
        copies.clear()

    def physics():
        def around(f, k):
            here = slice(f * sz.slab + k * sz.rows, f * sz.slab + (k + 1) * sz.rows)
            lane_at = f * sz.lev + k
            return (
                fields[here, :],
                jnp.where(lane == last_lane, to_lane(from_east[0 : sz.rows, :], lane_at, last_lane), moved_e[here, :]),
                jnp.where(lane == 0, to_lane(from_west[0 : sz.rows, :], lane_at, 0), moved_w[here, :]),
            )

        press_e, warm_above = jnp.zeros(tile, jnp.float32), None
        for k in range(sz.lev):
            at = k * sz.rows
            wet, wet_e, wet_w, wet_n, _ = masks(k)
            zonal, merid, temper, saline, visc = (around(f, k) for f in range(5))
            zonal_far, merid_far, temper_far, saline_far, press, div_far = (
                around_n[f * sz.slab + at : f * sz.slab + at + sz.rows, :] for f in range(6)
            )
            div[at : at + sz.rows, :] = keep(wet_e, zonal[0]) - keep(wet_w, zonal[2]) + div_far
            coef_e = keep(wet_e, 0.5 * (visc[0] + visc[1]))
            coef_w = keep(wet_w, 0.5 * (visc[2] + visc[0]))

            def along_lon(quantity):
                mid, e, w = quantity
                return TIME_STEP * (coef_e * (e - mid) - coef_w * (mid - w))

            warm = temper_far + along_lon(temper)
            mixing = jnp.zeros(tile, jnp.float32)
            if k > 0:
                background = fields[5 * sz.slab + at : 5 * sz.slab + at + sz.rows, :]
                mixing = mixed(warm_above, warm, background, wet)
            warm_above = warm
            press_e = press_e + GRAVITY_SCALE * keep(lev_e > k, HALINE * saline[1] - THERMAL * temper[1])
            zonal_new = zonal_far + along_lon(zonal) - TIME_STEP * (press_e - press)
            merid_new = merid_far + along_lon(merid)
            saline_new = saline_far + along_lon(saline)
            parts = (keep(wet_e, zonal_new), keep(wet_n, merid_new), warm, saline_new, None, mixing)
            for f, part in enumerate(parts):
                if part is not None:
                    out[f, at : at + sz.rows, :] = part
            if k % chunk == chunk - 1:
                send(0, 4, k // chunk)
                send(5, 6, k // chunk)
        total = jnp.zeros(tile, jnp.float32)
        for k in range(sz.lev - 1, -1, -1):
            at = k * sz.rows
            total = total + div[at : at + sz.rows, :]
            out[4, at : at + sz.rows, :] = -total if k > 0 else jnp.zeros(tile, jnp.float32)
            if k % chunk == 0:
                send(4, 5, k // chunk)

    tall = (sz.lev, sz.cols)

    def row_strips(step):
        lane16, depth = lane_ids(tall), row_ids(tall).astype(jnp.float32)

        def wet(levels_row):
            return levels_row > depth

        west_corner = from_west[3 * sz.rows : 3 * sz.rows + sz.lev, :]
        east_corner = from_east[3 * sz.rows : 3 * sz.rows + sz.lev, :]
        lane1 = lane_ids((1, sz.cols))
        for r in range(2):
            rows, cross = (south, cross_south) if r == 0 else (north, cross_north)
            strip = low_strip if r == 0 else high_strip
            edge = 0 if r == 0 else last_row
            near_lev = cross[level_row : level_row + 1, :]
            far_lev = cross[level_row + 1 : level_row + 2, :]
            own_lev = lev[edge : edge + 1, :]
            corner_lane = side_base + 2 + r
            lev_at_w = shift_west(near_lev, lane1, to_lane(west_side[0:1, :], corner_lane, 0))
            lev_at_e = shift_east(near_lev, lane1, to_lane(east_side[0:1, :], corner_lane, last_lane))
            wet_near = wet(near_lev)
            zonal = cross[ZONAL_ROW * sz.lev : (ZONAL_ROW + 1) * sz.lev, :]
            p = r * (sz.nf + 2)
            zonal_w = shift_west(zonal, lane16, to_lane(west_corner, p + sz.nf, 0))
            flow_e = keep(wet_near & wet(lev_at_e), zonal)
            flow_w = keep(wet_near & wet(lev_at_w), zonal_w)
            merid = cross[MERID_ROW * sz.lev : (MERID_ROW + 1) * sz.lev, :]
            if r == 0:
                merid_far = cross[MERID_ROW2 * sz.lev : (MERID_ROW2 + 1) * sz.lev, :]
                flow_n = keep(wet_near & wet(own_lev), merid)
                flow_s = keep(wet_near & wet(far_lev), merid_far)
            else:
                flow_n = keep(wet_near & wet(far_lev), merid)
                flow_s = keep(wet_near & wet(own_lev), level_rows(merid_in, 0, last_row, sz))
            weights = Weights(flow_e, flow_w, flow_n, flow_s, step)
            for f in range(sz.nf):
                at = 2 * f * sz.lev
                near, far = rows[at : at + sz.lev, :], rows[at + sz.lev : at + 2 * sz.lev, :]
                inside = level_rows(fields, f * sz.slab, edge, sz)
                at_w = shift_west(near, lane16, to_lane(west_corner, p + f, 0))
                at_e = shift_east(near, lane16, to_lane(east_corner, p + f, last_lane))
                up, down = (inside, far) if r == 0 else (far, inside)
                strip[f * sz.lev : (f + 1) * sz.lev, :] = weights.apply(near, at_e, at_w, up, down)

    def transport(step):
        west_old = from_west[0 : sz.rows, :]
        zero = jnp.zeros(tile, jnp.float32)

        def faces(k):
            if k == sz.lev:
                return zero, zero
            at = k * sz.rows
            speed, mixing = vert[at : at + sz.rows, :], mix[at : at + sz.rows, :]
            return jnp.maximum(speed, 0.0) + mixing, jnp.minimum(speed, 0.0) - mixing

        every = range(sz.nf)

        def stored_weights(k):
            at = k * sz.rows
            return Weights.of(*(wref[i * sz.slab + at : i * sz.slab + at + sz.rows, :] for i in range(5)))

        for k in range(sz.lev):
            at = k * sz.rows
            wet, wet_e, wet_w, wet_n, wet_s = masks(k)
            zonal, merid = zonal_in[at : at + sz.rows, :], merid_in[at : at + sz.rows, :]
            zonal_first = sz.nf * sz.lev
            zonal_west = shift_west(zonal, lane, to_lane(west_old, zonal_first + k, 0))
            beyond = MERID_ROW * sz.lev + k
            merid_south = shift_south(merid, row, cross_south[beyond : beyond + 1, :])
            flow_e, flow_w, flow_n, flow_s = (
                keep(wet_e, zonal), keep(wet_w, zonal_west), keep(wet_n, merid), keep(wet_s, merid_south)
            )
            div[at : at + sz.rows, :] = flow_e - flow_w + (flow_n - flow_s)
            weights = Weights(flow_e, flow_w, flow_n, flow_s, step)
            for i, part in enumerate(weights.parts()):
                wref[i * sz.slab + at : i * sz.slab + at + sz.rows, :] = part
        row_strips(step)
        for k in range(sz.lev):
            at = k * sz.rows
            weights = stored_weights(k)
            for f in every:
                here = slice(f * sz.slab + at, f * sz.slab + at + sz.rows)
                forward[here, :] = weights.apply(*(ref[here, :] for ref in (fields, around_e, around_w, around_n, around_s)))
        at_edge = (lane == 0) | (lane == last_lane)
        total = zero
        for k in range(sz.lev - 1, -1, -1):
            at = k * sz.rows
            total = total + div[at : at + sz.rows, :]
            vert[at : at + sz.rows, :] = -total if k > 0 else zero
            mixing = mixing_in[at : at + sz.rows, :]
            mix[at : at + sz.rows, :] = jnp.where(at_edge, edge_mix[at : at + sz.rows, :], mixing)
        last_ratio = None
        up, down = faces(0)
        lower, inverse = [], []
        for k in range(sz.lev):
            at = k * sz.rows
            up_next, down_next = faces(k + 1)
            pivot = 1.0 + TIME_STEP * (up - down_next)
            lower.append(TIME_STEP * down)
            if k > 0:
                pivot = pivot - lower[k] * last_ratio
            inverse.append(1.0 / pivot)
            last_ratio = -TIME_STEP * up_next * inverse[k]
            ratio[at : at + sz.rows, :] = last_ratio
            inv_ref[at : at + sz.rows, :] = inverse[k]
            pull[at : at + sz.rows, :] = lower[k] * inverse[k]
            up, down = up_next, down_next
        previous = [None] * sz.nf
        for k in range(sz.lev):
            at = k * sz.rows
            weights = stored_weights(k)
            values = [forward[f * sz.slab + at : f * sz.slab + at + sz.rows, :] for f in every]
            to_e, to_w = [turn(value, -1, 1) for value in values], [turn(value, 1, 1) for value in values]
            for f in every:
                here = slice(f * sz.slab + at, f * sz.slab + at + sz.rows)
                beyond = slice(f * sz.lev + k, f * sz.lev + k + 1)
                edge = second[here, :]
                value = weights.apply(
                    values[f],
                    jnp.where(lane == last_lane, edge, to_e[f]),
                    jnp.where(lane == 0, edge, to_w[f]),
                    shift_north(values[f], row, high_strip[beyond, :]),
                    shift_south(values[f], row, low_strip[beyond, :]),
                )
                moved[here, :] = value * inv_ref[at : at + sz.rows, :]
        for k in range(sz.lev):
            at = k * sz.rows
            for f in every:
                here = f * sz.slab + at
                value = moved[here : here + sz.rows, :]
                if k > 0:
                    value = value - pull[at : at + sz.rows, :] * previous[f]
                forward[here : here + sz.rows, :] = value
                previous[f] = value
        for k in range(sz.lev - 1, -1, -1):
            at = k * sz.rows
            wet = lev > k
            for f in range(sz.nf):
                here = f * sz.slab + at
                if k < sz.lev - 1:
                    previous[f] = forward[here : here + sz.rows, :] - ratio[at : at + sz.rows, :] * previous[f]
                out[f, at : at + sz.rows, :] = keep(wet, previous[f])
            if k % chunk == 0:
                send(0, sz.nf, k // chunk)

    @pl.when(is_dynamics)
    def _():
        physics()
        finish_copies()

    @pl.when(jnp.logical_not(is_dynamics))
    def _():
        transport(TIME_STEP / NSUB)
        finish_copies()


def pair_of(index, count, odd):
    if not odd:
        return index ^ 1
    return (((index + 1) ^ 1) - 1) % count


def on_device(sizes_of, fields, levels):
    sz = Sizes(fields, levels)
    count_s, count_o, count_a = sizes_of
    flat = fields.reshape(sz.nf * sz.slab, sz.cols)

    def place(s, o, a):
        return (s * count_o + o) * count_a + a

    def partner(s, o, a, odd, hop):
        b = pair_of(a, count_a, odd)
        if abs(a - b) > 1 and count_o % 2 == 0:
            return place(s, o ^ 1, a)
        return place((s + hop) % count_s, o, b)

    def swap(value, odd, hop=0):
        pairs = [
            (place(s, o, a), partner(s, o, a, odd, hop))
            for s in range(count_s)
            for o in range(count_o)
            for a in range(count_a)
        ]
        return lax.ppermute(value, ("sect", "lon", "lat"), pairs)

    def from_dynamics(value, odd=None):
        mine = lax.axis_index("sect")
        got = None
        for hop in range(1, count_s):
            if odd is None:
                part = lax.ppermute(value, "sect", [(s, (s + hop) % count_s) for s in range(count_s)])
            else:
                part = swap(value, odd, hop)
            got = part if got is None else jnp.where(mine == hop, part, got)
        return got

    def around(value, step):
        return lax.ppermute(value, "lon", [(i, (i + step) % count_o) for i in range(count_o)])

    rows_shape = (2 * sz.nf * sz.lev, sz.cols)
    cross_shape = (LEVEL_ROW * sz.lev + 8, sz.cols)
    columns_shape = (4 * sz.rows + sz.lev, sz.cols)
    side_shape = (4 * sz.rows, sz.cols)
    slab = (sz.slab, sz.cols)
    row_a, row_b, own_side, zonal, merid = call_kernel(
        functools.partial(pack_edges, sz), [rows_shape, rows_shape, side_shape, slab, slab], [flat]
    )
    twin_shape = (zonal_place(sz) + early(sz), sz.cols)
    wide_shape = (max(cross_shape[0], twin_shape[0] + 8), sz.cols)
    (cross_b,) = call_kernel(functools.partial(pack_cross, sz), [wide_shape], [flat, levels])
    row_a = swap(row_a, False)
    levels_a = swap(levels, False)
    row_b = swap(row_b, True)
    (twin,) = call_kernel(
        functools.partial(pack_twin, sz), [twin_shape], [flat, own_side, row_a]
    )
    twin = from_dynamics(twin)
    cross_b = from_dynamics(cross_b, True)
    south, north, corners = call_kernel(
        functools.partial(place_rows, sz), [rows_shape, rows_shape, (sz.rows, sz.cols)], [row_a, row_b]
    )
    (mixing,) = call_kernel(
        functools.partial(pack_mixing, sz), [(sz.slab, sz.cols)], [flat, levels, levels_a, cross_b, south, north]
    )
    to_east, to_west, cross_south, cross_north = call_kernel(
        functools.partial(pack_columns, sz),
        [columns_shape] * 2 + [cross_shape] * 2,
        [levels, levels_a, south, north, corners, twin, cross_b, own_side],
    )
    mixing = from_dynamics(mixing)
    zonal, merid = from_dynamics(zonal), from_dynamics(merid)
    from_east = around(to_west, -1)
    from_west = around(to_east, 1)
    kept, moved_e, moved_w, around_n, around_s = call_kernel(
        functools.partial(shift_fields, sz), [flat.shape] * 5, [flat, levels, south, north, cross_south, cross_north]
    )
    around_e, around_w, second, edge_mix = call_kernel(
        functools.partial(column_edges, sz),
        [flat.shape] * 3 + [slab],
        [levels, cross_south, cross_north, to_east, to_west, twin, from_west, from_east, moved_e, moved_w],
    )
    out_shape = (sz.nf, sz.slab, sz.cols)
    strip = (sz.nf * sz.lev, sz.cols)
    (out,) = call_kernel(
        functools.partial(finish, sz),
        [out_shape],
        [
            kept, levels, south, north, cross_south, cross_north, zonal, merid, mixing, twin, from_west, from_east,
            moved_e, moved_w, around_e, around_w, around_n, around_s, second, edge_mix,
        ],
        [out_shape, slab, slab, slab, strip, strip, slab, flat.shape, slab, (5 * sz.slab, sz.cols), slab, flat.shape],
        copies=3 * CHUNKS,
    )
    return out.reshape(fields.shape)


def solution(mesh):
    sizes_of = (mesh.shape["sect"], mesh.shape["lon"], mesh.shape["lat"])
    return jax.shard_map(
        functools.partial(on_device, sizes_of),
        mesh=mesh,
        in_specs=(P("sect", None, None, "lat", "lon"), P("lat", "lon")),
        out_specs=P("sect", None, None, "lat", "lon"),
        check_vma=False,
    )
```

```python
import functools
import jax
import jax.numpy as jnp
from jax import lax
from jax.experimental import pallas as pl
from jax.experimental.pallas import tpu as pltpu
from jax.sharding import PartitionSpec as P

NSUB = 2
TIME_STEP = 1.0
CORIOLIS = 0.3
THERMAL = 0.2
HALINE = 0.15
GRAVITY_SCALE = 0.05
MIX_BOOST = 4.0
RICHARDSON = 1.0

VMEM_LIMIT = 8 * 1024 * 1024
CHUNKS = 2

ZONAL_ROW, MERID_ROW, MERID_ROW2, END_ROW, LEVEL_ROW = range(5)
TEMPER_END, VISC_END = 0, 2


def call_kernel(body, outputs, inputs, scratch=(), copies=0):
    in_vmem = pl.BlockSpec(memory_space=pltpu.VMEM)
    scratch = [pltpu.VMEM(shape, jnp.float32) for shape in scratch]
    if copies:
        scratch.append(pltpu.SemaphoreType.DMA((copies,)))
    return pl.pallas_call(
        body,
        out_shape=[jax.ShapeDtypeStruct(shape, jnp.float32) for shape in outputs],
        in_specs=[in_vmem] * len(inputs),
        out_specs=[pl.BlockSpec(memory_space=pl.ANY) if copies else in_vmem] * len(outputs),
        scratch_shapes=scratch,
        compiler_params=pltpu.CompilerParams(vmem_limit_bytes=VMEM_LIMIT),
    )(*inputs)


class Sizes:
    def __init__(self, fields, levels):
        self.nf, self.lev = fields.shape[1], fields.shape[2]
        self.rows, self.cols = levels.shape
        self.slab = self.lev * self.rows


def lane_ids(shape):
    return lax.broadcasted_iota(jnp.int32, shape, 1)


def row_ids(shape):
    return lax.broadcasted_iota(jnp.int32, shape, 0)


def turn(value, shift, axis):
    size = value.shape[axis]
    shift = shift % size
    return value if shift == 0 else pltpu.roll(value, shift, axis)


def to_lane(value, source, target):
    return turn(value, target - source, 1)


def level_rows(ref, first, row, sz):
    return ref[pl.ds(first + row, sz.lev, stride=sz.rows), :]


def send_north_first(sz, fill):
    even = lax.axis_index("lat") % 2 == 0
    top, second = sz.rows - 1, sz.rows - 2

    @pl.when(even)
    def _():
        fill(0, top, second)
        fill(1, 0, 1)

    @pl.when(jnp.logical_not(even))
    def _():
        fill(0, 0, 1)
        fill(1, top, second)


def pack_edges(sz, fields, row_a, row_b, side, zonal, merid):
    zonal[...] = fields[0 : sz.slab, :]
    merid[...] = fields[sz.slab : 2 * sz.slab, :]

    def fill(which, near, far):
        message = (row_a, row_b)[which]
        for f in range(sz.nf):
            for r, row in enumerate((near, far)):
                at = (2 * f + r) * sz.lev
                message[at : at + sz.lev, :] = level_rows(fields, f * sz.slab, row, sz)

    send_north_first(sz, fill)
    for place, column in enumerate(edge_columns(sz, fields, sz.nf, 0)):
        side[place * sz.rows : (place + 1) * sz.rows, :] = column


def pack_cross(sz, fields, levels, cross):
    lev = levels[...].astype(jnp.float32)

    def fill(which, near, far):
        if which == 0:
            return
        for at, (f, row) in enumerate(((0, near), (1, near), (1, far))):
            cross[at * sz.lev : (at + 1) * sz.lev, :] = level_rows(fields, f * sz.slab, row, sz)
        cross[END_ROW * sz.lev : (END_ROW + 1) * sz.lev, :] = row_ends(
            level_rows(fields, 2 * sz.slab, near, sz), level_rows(fields, 4 * sz.slab, near, sz)
        )
        at = LEVEL_ROW * sz.lev
        cross[at : at + 1, :] = lev[near : near + 1, :]
        cross[at + 1 : at + 2, :] = lev[far : far + 1, :]
        cross[at + 2 :, :] = jnp.zeros((cross.shape[0] - at - 2, sz.cols), jnp.float32)

    send_north_first(sz, fill)


def row_ends(temper, visc):
    lane = lane_ids(temper.shape)
    ends = jnp.where(lane == TEMPER_END, temper, turn(temper, TEMPER_END + 2, 1))
    ends = jnp.where(lane == VISC_END, turn(visc, VISC_END, 1), ends)
    return jnp.where(lane == VISC_END + 1, turn(visc, VISC_END + 2, 1), ends)


def pack_twin(sz, own_side, row_a, twin):
    base = 4 * sz.rows
    twin[0:base, :] = own_side[...]
    def row_of(f, r):
        first = (2 * f + r) * sz.lev
        return row_a[first : first + sz.lev, :]

    parts = (row_of(0, 0), row_of(1, 0), row_of(1, 1), row_ends(row_of(2, 0), row_of(4, 0)))
    for at, part in enumerate(parts):
        twin[base + at * sz.lev : base + (at + 1) * sz.lev, :] = part


def edge_columns(sz, ref, count, first):
    tile = (sz.rows, sz.cols)
    lane = lane_ids(tile)
    zero = jnp.zeros(tile, jnp.float32)
    last = sz.cols - 1
    east_one, west_one, east_two, west_two = zero, zero, zero, zero
    for f in range(count):
        for k in range(sz.lev):
            at = f * sz.slab + k * sz.rows
            p = (first + f) * sz.lev + k
            moved = to_lane(ref[at : at + sz.rows, :], last, p)
            east_one = jnp.where(lane == p, moved, east_one)
            west_one = jnp.where(lane == (p + 1) % sz.cols, moved, west_one)
            west_two = jnp.where(lane == (p + 2) % sz.cols, moved, west_two)
            east_two = jnp.where(lane == (p - 1) % sz.cols, moved, east_two)
    return east_one, turn(west_one, -1, 1), turn(east_two, 1, 1), turn(west_two, -2, 1)


def place_rows(sz, row_a, row_b, south, north, corners):
    position = lax.axis_index("lat")
    even = position % 2 == 0
    first, other = row_a[...], row_b[...]
    tall = (sz.lev, sz.cols)
    lane, depth = lane_ids(tall), row_ids(tall)
    low = jnp.where(position > 0, jnp.where(even, other, first), 0.0)
    high = jnp.where(position < lax.axis_size("lat") - 1, jnp.where(even, first, other), 0.0)
    south[...] = low
    north[...] = high
    ends = []
    for column in (sz.cols - 1, 0):
        for rows in (low, high):
            total = jnp.zeros(tall, jnp.float32)
            for f in range(sz.nf):
                near = rows[2 * f * sz.lev : (2 * f + 1) * sz.lev, :]
                spread = jnp.broadcast_to(near[:, column : column + 1], tall)
                total = jnp.where(lane == f * sz.lev + depth, spread, total)
            ends.append(jnp.sum(total, axis=0, keepdims=True))
    for i, end in enumerate(ends):
        corners[i : i + 1, :] = end
    corners[len(ends) :, :] = jnp.zeros((sz.rows - len(ends), sz.cols), jnp.float32)


def beside_levels(sz, levels_a, cross_b):
    even = lax.axis_index("lat") % 2 == 0
    partner = levels_a[...].astype(jnp.float32)
    level_row = LEVEL_ROW * sz.lev

    def row_at(low, high):
        return jnp.where(even, partner[low : low + 1, :], partner[high : high + 1, :])

    near_b, far_b = (cross_b[level_row + i : level_row + i + 1, :] for i in range(2))
    return row_at(0, sz.rows - 1), row_at(1, sz.rows - 2), near_b, far_b


def pack_mixing(sz, fields, levels, levels_a, cross_b, south, north, mixing_out):
    position = lax.axis_index("lat")
    even = position % 2 == 0
    near_a, _, near_b, _ = beside_levels(sz, levels_a, cross_b)
    south_lev = jnp.where(position > 0, jnp.where(even, near_b, near_a), 0.0)
    north_lev = jnp.where(position < lax.axis_size("lat") - 1, jnp.where(even, near_a, near_b), 0.0)
    tile = (sz.rows, sz.cols)
    lev = levels[...].astype(jnp.float32)

    @pl.when(lax.axis_index("sect") == 0)
    def _():
        row = row_ids(tile)
        lev_e, lev_w = turn(lev, -1, 1), turn(lev, 1, 1)
        lev_n, lev_s = shift_north(lev, row, north_lev), shift_south(lev, row, south_lev)
        warm_above = None
        for k in range(sz.lev):
            at = k * sz.rows

            def around(f):
                value = fields[f * sz.slab + at : f * sz.slab + at + sz.rows, :]
                beyond = 2 * f * sz.lev + k
                return (
                    value, turn(value, -1, 1), turn(value, 1, 1),
                    shift_north(value, row, north[beyond : beyond + 1, :]),
                    shift_south(value, row, south[beyond : beyond + 1, :]),
                )

            wet = lev > k
            masks = wet, wet & (lev_e > k), wet & (lev_w > k), wet & (lev_n > k), wet & (lev_s > k)
            warm = diffused(around(2), around(4), masks)
            background = fields[5 * sz.slab + at : 5 * sz.slab + at + sz.rows, :]
            mixing = jnp.zeros(tile, jnp.float32) if k == 0 else mixed(warm_above, warm, background, wet)
            warm_above = warm
            mixing_out[at : at + sz.rows, :] = mixing


def pack_columns(
    sz, levels, levels_a, south, north, corners, twin, cross_b, own_side,
    to_east, to_west, cross_south, cross_north,
):
    position = lax.axis_index("lat")
    even = position % 2 == 0
    has_south = position > 0
    has_north = position < lax.axis_size("lat") - 1
    tile = (sz.rows, sz.cols)
    lane = lane_ids(tile)
    last = sz.cols - 1
    side = twin
    level_row = LEVEL_ROW * sz.lev
    near_a, far_a, near_b, far_b = beside_levels(sz, levels_a, cross_b)
    pairs = (
        (cross_south, cross_north, slice(0, level_row), twin[4 * sz.rows : 4 * sz.rows + level_row, :], cross_b[0:level_row, :]),
        (cross_south, cross_north, slice(level_row, level_row + 1), near_a, near_b),
        (cross_south, cross_north, slice(level_row + 1, level_row + 2), far_a, far_b),
    )
    for low, high, at, first, other in pairs:
        low[at, :] = jnp.where(has_south, jnp.where(even, other, first), 0.0)
        high[at, :] = jnp.where(has_north, jnp.where(even, first, other), 0.0)
    for ref in (cross_south, cross_north):
        ref[level_row + 2 : level_row + 8, :] = jnp.zeros((6, sz.cols), jnp.float32)

    tracer_lanes = lane < sz.nf * sz.lev
    for place, (message, at) in enumerate(((to_east, 0), (to_west, 0), (to_east, sz.rows), (to_west, sz.rows))):
        own = own_side[place * sz.rows : (place + 1) * sz.rows, :]
        dynamics = side[place * sz.rows : (place + 1) * sz.rows, :]
        message[at : at + sz.rows, :] = jnp.where(tracer_lanes, own, turn(dynamics, sz.nf * sz.lev, 1))

    lev = levels[...].astype(jnp.float32)
    south_lev = cross_south[level_row : level_row + 1, :]
    north_lev = cross_north[level_row : level_row + 1, :]
    base = 2 * sz.lev
    for place, (message, near, far) in enumerate(((to_east, last, last - 1), (to_west, 0, 1))):
        part = side[place * sz.rows : (place + 1) * sz.rows, :]
        part = jnp.where(lane < sz.lev, turn(part, -2 * sz.lev, 1), turn(part, -3 * sz.lev, 1))
        part = jnp.where(lane == base, to_lane(lev, near, base), part)
        part = jnp.where(lane == base + 1, to_lane(lev, far, base + 1), part)
        low = jnp.broadcast_to(to_lane(south_lev, near, base + 2), tile)
        high = jnp.broadcast_to(to_lane(north_lev, near, base + 3), tile)
        part = jnp.where(lane == base + 2, low, part)
        part = jnp.where(lane == base + 3, high, part)
        message[2 * sz.rows : 3 * sz.rows, :] = part

    tall = (sz.lev, sz.cols)
    tall_lane = lane_ids(tall)
    east_corner = jnp.zeros(tall, jnp.float32)
    west_corner = east_corner
    for r, (rows, cross) in enumerate(((south, cross_south), (north, cross_north))):
        for f in range(sz.nf + 2):
            if f < sz.nf:
                values = rows[2 * f * sz.lev : (2 * f + 1) * sz.lev, :]
            else:
                at = (ZONAL_ROW, MERID_ROW)[f - sz.nf] * sz.lev
                values = cross[at : at + sz.lev, :]
            p = r * (sz.nf + 2) + f
            moved = to_lane(values, last, p)
            east_corner = jnp.where(tall_lane == p, moved, east_corner)
            west_corner = jnp.where(tall_lane == p + 1, moved, west_corner)
    to_east[3 * sz.rows : 3 * sz.rows + sz.lev, :] = east_corner
    to_west[3 * sz.rows : 3 * sz.rows + sz.lev, :] = turn(west_corner, -1, 1)
    ends = corners[...]
    to_east[3 * sz.rows + sz.lev :, :] = ends
    to_west[3 * sz.rows + sz.lev :, :] = turn(ends, -2, 0)


def keep(mask, value):
    return jnp.where(mask, value, 0.0)


def diffused(quantity, viscosity, masks):
    mid, e, w, n, s = quantity
    visc, visc_e, visc_w, visc_n, visc_s = viscosity
    _, wet_e, wet_w, wet_n, wet_s = masks
    change = (
        keep(wet_e, 0.5 * (visc + visc_e)) * (e - mid)
        - keep(wet_w, 0.5 * (visc_w + visc)) * (mid - w)
        + keep(wet_n, 0.5 * (visc + visc_n)) * (n - mid)
        - keep(wet_s, 0.5 * (visc_s + visc)) * (mid - s)
    )
    return mid + TIME_STEP * change


def mixed(warm_above, warm, background, wet):
    jump = THERMAL * (warm_above - warm)
    return keep(wet, background * (1.0 + MIX_BOOST / (1.0 + RICHARDSON * jump * jump)))


def shift_west(value, lane, edge):
    return jnp.where(lane == 0, edge, turn(value, 1, 1))


def shift_east(value, lane, edge):
    return jnp.where(lane == value.shape[1] - 1, edge, turn(value, -1, 1))


def shift_south(value, row, edge):
    return jnp.where(row == 0, edge, turn(value, 1, 0))


def shift_north(value, row, edge):
    return jnp.where(row == value.shape[0] - 1, edge, turn(value, -1, 0))


class Weights:
    def __init__(self, east, west, north, south, step):
        self.own = 1.0 - step * (
            jnp.maximum(east, 0.0) - jnp.minimum(west, 0.0) + (jnp.maximum(north, 0.0) - jnp.minimum(south, 0.0))
        )
        self.east = -step * jnp.minimum(east, 0.0)
        self.west = step * jnp.maximum(west, 0.0)
        self.north = -step * jnp.minimum(north, 0.0)
        self.south = step * jnp.maximum(south, 0.0)

    def parts(self):
        return self.own, self.east, self.west, self.north, self.south

    @classmethod
    def of(cls, own, east, west, north, south):
        weights = cls.__new__(cls)
        weights.own, weights.east, weights.west, weights.north, weights.south = own, east, west, north, south
        return weights

    def apply(self, own, east, west, north, south):
        return self.own * own + self.east * east + self.west * west + (self.north * north + self.south * south)


def shift_fields(
    sz, fields, levels, south, north, cross_south, cross_north, kept, moved_e, moved_w, around_n, around_s
):
    kept[...] = fields[...]
    tile = (sz.rows, sz.cols)
    row = row_ids(tile)
    for at in range(0, sz.nf * sz.slab, sz.rows):
        here = slice(at, at + sz.rows)
        value = fields[here, :]
        moved_e[here, :] = turn(value, -1, 1)
        moved_w[here, :] = turn(value, 1, 1)

    def along_lat(f, k):
        value = fields[f * sz.slab + k * sz.rows : f * sz.slab + (k + 1) * sz.rows, :]
        beyond = slice(2 * f * sz.lev + k, 2 * f * sz.lev + k + 1)
        return value, shift_north(value, row, north[beyond, :]), shift_south(value, row, south[beyond, :])

    is_dynamics = lax.axis_index("sect") == 0

    @pl.when(jnp.logical_not(is_dynamics))
    def _():
        for f in range(sz.nf):
            for k in range(sz.lev):
                here = slice(f * sz.slab + k * sz.rows, f * sz.slab + (k + 1) * sz.rows)
                _, around_n[here, :], around_s[here, :] = along_lat(f, k)

    @pl.when(is_dynamics)
    def _():
        lev = levels[...].astype(jnp.float32)
        level_row = LEVEL_ROW * sz.lev
        lev_n = shift_north(lev, row, cross_north[level_row : level_row + 1, :])
        lev_s = shift_south(lev, row, cross_south[level_row : level_row + 1, :])
        press = jnp.zeros(tile, jnp.float32)
        press_n = press
        for k in range(sz.lev):
            wet, wet_n, wet_s = lev > k, lev_n > k, lev_s > k
            zonal, merid, temper, saline, visc = (along_lat(f, k) for f in range(5))
            coef_n = keep(wet & wet_n, 0.5 * (visc[0] + visc[1]))
            coef_s = keep(wet & wet_s, 0.5 * (visc[2] + visc[0]))

            def advanced(quantity):
                mid, n, s = quantity
                return mid + TIME_STEP * (coef_n * (n - mid) - coef_s * (mid - s))

            def weight(place, wet_there):
                return keep(wet_there, HALINE * saline[place] - THERMAL * temper[place])

            press = press + GRAVITY_SCALE * weight(0, wet)
            press_n = press_n + GRAVITY_SCALE * weight(1, wet_n)
            parts = (
                advanced(zonal) + TIME_STEP * CORIOLIS * merid[0],
                advanced(merid) - TIME_STEP * (CORIOLIS * zonal[0] + (press_n - press)),
                advanced(temper),
                advanced(saline),
                press,
                keep(wet & wet_n, merid[0]) - keep(wet & wet_s, merid[2]),
            )
            for f, part in enumerate(parts):
                around_n[f * sz.slab + k * sz.rows : f * sz.slab + (k + 1) * sz.rows, :] = part


def column_edges(
    sz, levels, cross_south, cross_north, own_east, own_west, side, from_west, from_east, moved_e, moved_w,
    around_e, around_w, second, edge_mix,
):
    tile = (sz.rows, sz.cols)
    lane, row = lane_ids(tile), row_ids(tile)
    last_lane, last_row = sz.cols - 1, sz.rows - 1
    lev = levels[...].astype(jnp.float32)
    level_row = LEVEL_ROW * sz.lev
    side_base = 2 * sz.lev
    west_side = from_west[2 * sz.rows : 3 * sz.rows, :]
    east_side = from_east[2 * sz.rows : 3 * sz.rows, :]
    lev_w = shift_west(lev, lane, to_lane(west_side, side_base, 0))
    lev_e = shift_east(lev, lane, to_lane(east_side, side_base, last_lane))
    south_lev, north_lev = cross_south[level_row : level_row + 1, :], cross_north[level_row : level_row + 1, :]
    lev_s = shift_south(lev, row, south_lev)
    lev_n = shift_north(lev, row, north_lev)

    def masks(k):
        wet = lev > k
        return wet, wet & (lev_e > k), wet & (lev_w > k), wet & (lev_n > k), wet & (lev_s > k)

    def column(value, at):
        return jnp.broadcast_to(value[:, at : at + 1], value.shape)

    def both(west, east):
        return jnp.concatenate([west, east], axis=0)

    tall = (sz.lev, sz.cols)
    pair_row = row_ids((2 * sz.rows, sz.cols)) % sz.rows
    pair_lane = lane_ids((2 * sz.rows, sz.cols))

    def pair_south(value, edge):
        return jnp.where(pair_row == 0, edge, turn(value, 1, 0))

    def pair_north(value, edge):
        return jnp.where(pair_row == last_row, edge, turn(value, -1, 0))

    def edge_mixing():
        diagonal = lane_ids(tall) == row_ids(tall)

        def levels_in_lanes(rows, at):
            return jnp.broadcast_to(jnp.sum(keep(diagonal, column(rows, at)), axis=0, keepdims=True), tile)

        def place(index):
            return side[index * sz.rows : (index + 1) * sz.rows, :]

        own_pair, inner_w, inner_e = both(place(1), place(0)), place(3), place(2)

        def around(f, message_lane, end):
            shift = -f * sz.lev
            outer_w, outer_e = turn(west_side, -message_lane, 1), turn(east_side, -message_lane, 1)
            own = turn(own_pair, shift, 1)
            low, high = (cross[END_ROW * sz.lev : (END_ROW + 1) * sz.lev, :] for cross in (cross_south, cross_north))
            return (
                own,
                both(turn(inner_w, shift, 1), outer_e),
                both(outer_w, turn(inner_e, shift, 1)),
                pair_north(own, both(levels_in_lanes(high, end), levels_in_lanes(high, end + 1))),
                pair_south(own, both(levels_in_lanes(low, end), levels_in_lanes(low, end + 1))),
            )

        depth = pair_lane.astype(jnp.float32)

        def wet(value):
            return both(column(value, 0), column(value, last_lane)) > depth

        mid = wet(lev)
        mask = mid, mid & wet(lev_e), mid & wet(lev_w), mid & wet(lev_n), mid & wet(lev_s)
        warm = diffused(around(2, 0, TEMPER_END), around(4, sz.lev, VISC_END), mask)
        background = turn(own_pair, -5 * sz.lev, 1)
        return jnp.where(pair_lane == 0, 0.0, mixed(turn(warm, 1, 1), warm, background, mid))

    def column_strips(step):
        lane16, depth16 = lane_ids(tall), row_ids(tall)

        def all_fields(value, first):
            at = lane_ids(value.shape)
            value = jnp.where((at >= first) & (at < first + sz.lev), value, 0.0)
            width = sz.lev
            while width < sz.cols:
                value = value + turn(value, width, 1)
                width *= 2
            return value

        def corner_rows(message, r):
            items = message[3 * sz.rows : 3 * sz.rows + sz.lev, :]
            p = r * (sz.nf + 2)
            ends = 3 * sz.rows + sz.lev + r
            tracers = message[ends : ends + 1, :]
            spread = jnp.broadcast_to(items[:, p + sz.nf + 1 : p + sz.nf + 2], tall)
            velocity = jnp.where(lane16 % sz.lev == depth16, spread, 0.0)
            return tracers, jnp.sum(velocity, axis=0, keepdims=True)

        inside_w, inside_e = own_west[0 : sz.rows, :], own_east[0 : sz.rows, :]
        near = both(from_west[0 : sz.rows, :], from_east[0 : sz.rows, :])
        far_w, far_e = from_west[sz.rows : 2 * sz.rows, :], from_east[sz.rows : 2 * sz.rows, :]
        corners = [corner_rows(message, r) for message in (from_west, from_east) for r in range(2)]
        low_tracers, high_tracers, low_merid = (
            both(jnp.broadcast_to(corners[i][part], tile), jnp.broadcast_to(corners[i + 2][part], tile))
            for i, part in ((0, 0), (1, 0), (0, 1))
        )

        def side_levels(at):
            return column(west_side, at), column(east_side, at)

        near_lev = both(*side_levels(side_base))
        far_lev_w, far_lev_e = side_levels(side_base + 1)
        own_lev_w, own_lev_e = column(lev, 0), column(lev, last_lane)
        lev_at_s = pair_south(near_lev, both(*side_levels(side_base + 2)))
        lev_at_n = pair_north(near_lev, both(*side_levels(side_base + 3)))
        depth = (lane_ids(near.shape) % sz.lev).astype(jnp.float32)
        wet_near = near_lev > depth
        zonal_first = sz.nf * sz.lev
        west, east = both(far_w, inside_e), both(inside_w, far_e)
        flow_e = keep(wet_near & (both(own_lev_w, far_lev_e) > depth), all_fields(near, zonal_first))
        flow_w = keep(wet_near & (both(far_lev_w, own_lev_e) > depth), all_fields(west, zonal_first))
        merid = all_fields(near, zonal_first + sz.lev)
        flow_n = keep(wet_near & (lev_at_n > depth), merid)
        flow_s = keep(wet_near & (lev_at_s > depth), pair_south(merid, low_merid))
        weights = Weights(flow_e, flow_w, flow_n, flow_s, step)
        return weights.apply(near, east, west, pair_north(near, high_tracers), pair_south(near, low_tracers))

    @pl.when(lax.axis_index("sect") > 0)
    def _():
        west_old, east_old = from_west[0 : sz.rows, :], from_east[0 : sz.rows, :]
        strips = column_strips(TIME_STEP / NSUB)
        west_new, east_new = strips[0 : sz.rows, :], strips[sz.rows : 2 * sz.rows, :]
        edges = edge_mixing()
        edge_w, edge_e = edges[0 : sz.rows, :], edges[sz.rows : 2 * sz.rows, :]
        first, last = lane == 0, lane == last_lane
        for k in range(sz.lev):
            at = k * sz.rows
            edge_mix[at : at + sz.rows, :] = jnp.where(first, to_lane(edge_w, k, 0), to_lane(edge_e, k, last_lane))
            for f in range(sz.nf):
                here = slice(f * sz.slab + at, f * sz.slab + at + sz.rows)
                p = f * sz.lev + k
                around_e[here, :] = jnp.where(last, to_lane(east_old, p, last_lane), moved_e[here, :])
                around_w[here, :] = jnp.where(first, to_lane(west_old, p, 0), moved_w[here, :])
        for k in range(sz.lev):
            for f in range(sz.nf):
                here = slice(f * sz.slab + k * sz.rows, f * sz.slab + (k + 1) * sz.rows)
                p = f * sz.lev + k
                second[here, :] = jnp.where(first, to_lane(west_new, p, 0), to_lane(east_new, p, last_lane))


def finish(
    sz, fields, levels, south, north, cross_south, cross_north, zonal_in, merid_in, mixing_in,
    side, from_west, from_east, moved_e, moved_w, around_e, around_w, around_n, around_s, second, edge_mix,
    result, out, div, mix, vert, low_strip, high_strip, ratio, forward, inv_ref, wref, pull, moved, sent,
):
    tile = (sz.rows, sz.cols)
    lane, row = lane_ids(tile), row_ids(tile)
    last_lane, last_row = sz.cols - 1, sz.rows - 1
    lev = levels[...].astype(jnp.float32)
    level_row = LEVEL_ROW * sz.lev
    side_base = 2 * sz.lev
    west_side = from_west[2 * sz.rows : 3 * sz.rows, :]
    east_side = from_east[2 * sz.rows : 3 * sz.rows, :]
    lev_w = shift_west(lev, lane, to_lane(west_side, side_base, 0))
    lev_e = shift_east(lev, lane, to_lane(east_side, side_base, last_lane))
    south_lev, north_lev = cross_south[level_row : level_row + 1, :], cross_north[level_row : level_row + 1, :]
    lev_s = shift_south(lev, row, south_lev)
    lev_n = shift_north(lev, row, north_lev)

    def masks(k):
        wet = lev > k
        return wet, wet & (lev_e > k), wet & (lev_w > k), wet & (lev_n > k), wet & (lev_s > k)

    is_dynamics = lax.axis_index("sect") == 0
    chunk = sz.lev // CHUNKS
    copies = []

    def send(first, last, part):
        at = pl.ds(part * chunk * sz.rows, chunk * sz.rows)
        copy = pltpu.make_async_copy(
            out.at[pl.ds(first, last - first), at, :], result.at[pl.ds(first, last - first), at, :], sent.at[len(copies)]
        )
        copy.start()
        copies.append(copy)

    def finish_copies():
        for copy in copies:
            copy.wait()
        copies.clear()

    def physics():
        def around(f, k):
            here = slice(f * sz.slab + k * sz.rows, f * sz.slab + (k + 1) * sz.rows)
            lane_at = f * sz.lev + k
            return (
                fields[here, :],
                jnp.where(lane == last_lane, to_lane(from_east[0 : sz.rows, :], lane_at, last_lane), moved_e[here, :]),
                jnp.where(lane == 0, to_lane(from_west[0 : sz.rows, :], lane_at, 0), moved_w[here, :]),
            )

        press_e, warm_above = jnp.zeros(tile, jnp.float32), None
        for k in range(sz.lev):
            at = k * sz.rows
            wet, wet_e, wet_w, wet_n, _ = masks(k)
            zonal, merid, temper, saline, visc = (around(f, k) for f in range(5))
            zonal_far, merid_far, temper_far, saline_far, press, div_far = (
                around_n[f * sz.slab + at : f * sz.slab + at + sz.rows, :] for f in range(6)
            )
            div[at : at + sz.rows, :] = keep(wet_e, zonal[0]) - keep(wet_w, zonal[2]) + div_far
            coef_e = keep(wet_e, 0.5 * (visc[0] + visc[1]))
            coef_w = keep(wet_w, 0.5 * (visc[2] + visc[0]))

            def along_lon(quantity):
                mid, e, w = quantity
                return TIME_STEP * (coef_e * (e - mid) - coef_w * (mid - w))

            warm = temper_far + along_lon(temper)
            mixing = jnp.zeros(tile, jnp.float32)
            if k > 0:
                background = fields[5 * sz.slab + at : 5 * sz.slab + at + sz.rows, :]
                mixing = mixed(warm_above, warm, background, wet)
            warm_above = warm
            press_e = press_e + GRAVITY_SCALE * keep(lev_e > k, HALINE * saline[1] - THERMAL * temper[1])
            zonal_new = zonal_far + along_lon(zonal) - TIME_STEP * (press_e - press)
            merid_new = merid_far + along_lon(merid)
            saline_new = saline_far + along_lon(saline)
            parts = (keep(wet_e, zonal_new), keep(wet_n, merid_new), warm, saline_new, None, mixing)
            for f, part in enumerate(parts):
                if part is not None:
                    out[f, at : at + sz.rows, :] = part
            if k % chunk == chunk - 1:
                send(0, 4, k // chunk)
                send(5, 6, k // chunk)
        total = jnp.zeros(tile, jnp.float32)
        for k in range(sz.lev - 1, -1, -1):
            at = k * sz.rows
            total = total + div[at : at + sz.rows, :]
            out[4, at : at + sz.rows, :] = -total if k > 0 else jnp.zeros(tile, jnp.float32)
            if k % chunk == 0:
                send(4, 5, k // chunk)

    tall = (sz.lev, sz.cols)

    def row_strips(step):
        lane16, depth = lane_ids(tall), row_ids(tall).astype(jnp.float32)

        def wet(levels_row):
            return levels_row > depth

        west_corner = from_west[3 * sz.rows : 3 * sz.rows + sz.lev, :]
        east_corner = from_east[3 * sz.rows : 3 * sz.rows + sz.lev, :]
        lane1 = lane_ids((1, sz.cols))
        for r in range(2):
            rows, cross = (south, cross_south) if r == 0 else (north, cross_north)
            strip = low_strip if r == 0 else high_strip
            edge = 0 if r == 0 else last_row
            near_lev = cross[level_row : level_row + 1, :]
            far_lev = cross[level_row + 1 : level_row + 2, :]
            own_lev = lev[edge : edge + 1, :]
            corner_lane = side_base + 2 + r
            lev_at_w = shift_west(near_lev, lane1, to_lane(west_side[0:1, :], corner_lane, 0))
            lev_at_e = shift_east(near_lev, lane1, to_lane(east_side[0:1, :], corner_lane, last_lane))
            wet_near = wet(near_lev)
            zonal = cross[ZONAL_ROW * sz.lev : (ZONAL_ROW + 1) * sz.lev, :]
            p = r * (sz.nf + 2)
            zonal_w = shift_west(zonal, lane16, to_lane(west_corner, p + sz.nf, 0))
            flow_e = keep(wet_near & wet(lev_at_e), zonal)
            flow_w = keep(wet_near & wet(lev_at_w), zonal_w)
            merid = cross[MERID_ROW * sz.lev : (MERID_ROW + 1) * sz.lev, :]
            if r == 0:
                merid_far = cross[MERID_ROW2 * sz.lev : (MERID_ROW2 + 1) * sz.lev, :]
                flow_n = keep(wet_near & wet(own_lev), merid)
                flow_s = keep(wet_near & wet(far_lev), merid_far)
            else:
                flow_n = keep(wet_near & wet(far_lev), merid)
                flow_s = keep(wet_near & wet(own_lev), level_rows(merid_in, 0, last_row, sz))
            weights = Weights(flow_e, flow_w, flow_n, flow_s, step)
            for f in range(sz.nf):
                at = 2 * f * sz.lev
                near, far = rows[at : at + sz.lev, :], rows[at + sz.lev : at + 2 * sz.lev, :]
                inside = level_rows(fields, f * sz.slab, edge, sz)
                at_w = shift_west(near, lane16, to_lane(west_corner, p + f, 0))
                at_e = shift_east(near, lane16, to_lane(east_corner, p + f, last_lane))
                up, down = (inside, far) if r == 0 else (far, inside)
                strip[f * sz.lev : (f + 1) * sz.lev, :] = weights.apply(near, at_e, at_w, up, down)

    def transport(step):
        west_old = from_west[0 : sz.rows, :]
        zero = jnp.zeros(tile, jnp.float32)

        def faces(k):
            if k == sz.lev:
                return zero, zero
            at = k * sz.rows
            speed, mixing = vert[at : at + sz.rows, :], mix[at : at + sz.rows, :]
            return jnp.maximum(speed, 0.0) + mixing, jnp.minimum(speed, 0.0) - mixing

        every = range(sz.nf)

        def stored_weights(k):
            at = k * sz.rows
            return Weights.of(*(wref[i * sz.slab + at : i * sz.slab + at + sz.rows, :] for i in range(5)))

        for k in range(sz.lev):
            at = k * sz.rows
            wet, wet_e, wet_w, wet_n, wet_s = masks(k)
            zonal, merid = zonal_in[at : at + sz.rows, :], merid_in[at : at + sz.rows, :]
            zonal_first = sz.nf * sz.lev
            zonal_west = shift_west(zonal, lane, to_lane(west_old, zonal_first + k, 0))
            beyond = MERID_ROW * sz.lev + k
            merid_south = shift_south(merid, row, cross_south[beyond : beyond + 1, :])
            flow_e, flow_w, flow_n, flow_s = (
                keep(wet_e, zonal), keep(wet_w, zonal_west), keep(wet_n, merid), keep(wet_s, merid_south)
            )
            div[at : at + sz.rows, :] = flow_e - flow_w + (flow_n - flow_s)
            weights = Weights(flow_e, flow_w, flow_n, flow_s, step)
            for i, part in enumerate(weights.parts()):
                wref[i * sz.slab + at : i * sz.slab + at + sz.rows, :] = part
        row_strips(step)
        for k in range(sz.lev):
            at = k * sz.rows
            weights = stored_weights(k)
            for f in every:
                here = slice(f * sz.slab + at, f * sz.slab + at + sz.rows)
                forward[here, :] = weights.apply(*(ref[here, :] for ref in (fields, around_e, around_w, around_n, around_s)))
        at_edge = (lane == 0) | (lane == last_lane)
        total = zero
        for k in range(sz.lev - 1, -1, -1):
            at = k * sz.rows
            total = total + div[at : at + sz.rows, :]
            vert[at : at + sz.rows, :] = -total if k > 0 else zero
            mixing = mixing_in[at : at + sz.rows, :]
            mix[at : at + sz.rows, :] = jnp.where(at_edge, edge_mix[at : at + sz.rows, :], mixing)
        last_ratio = None
        up, down = faces(0)
        lower, inverse = [], []
        for k in range(sz.lev):
            at = k * sz.rows
            up_next, down_next = faces(k + 1)
            pivot = 1.0 + TIME_STEP * (up - down_next)
            lower.append(TIME_STEP * down)
            if k > 0:
                pivot = pivot - lower[k] * last_ratio
            inverse.append(1.0 / pivot)
            last_ratio = -TIME_STEP * up_next * inverse[k]
            ratio[at : at + sz.rows, :] = last_ratio
            inv_ref[at : at + sz.rows, :] = inverse[k]
            pull[at : at + sz.rows, :] = lower[k] * inverse[k]
            up, down = up_next, down_next
        previous = [None] * sz.nf
        for k in range(sz.lev):
            at = k * sz.rows
            weights = stored_weights(k)
            values = [forward[f * sz.slab + at : f * sz.slab + at + sz.rows, :] for f in every]
            to_e, to_w = [turn(value, -1, 1) for value in values], [turn(value, 1, 1) for value in values]
            for f in every:
                here = slice(f * sz.slab + at, f * sz.slab + at + sz.rows)
                beyond = slice(f * sz.lev + k, f * sz.lev + k + 1)
                edge = second[here, :]
                value = weights.apply(
                    values[f],
                    jnp.where(lane == last_lane, edge, to_e[f]),
                    jnp.where(lane == 0, edge, to_w[f]),
                    shift_north(values[f], row, high_strip[beyond, :]),
                    shift_south(values[f], row, low_strip[beyond, :]),
                )
                moved[here, :] = value * inv_ref[at : at + sz.rows, :]
        for k in range(sz.lev):
            at = k * sz.rows
            for f in every:
                here = f * sz.slab + at
                value = moved[here : here + sz.rows, :]
                if k > 0:
                    value = value - pull[at : at + sz.rows, :] * previous[f]
                forward[here : here + sz.rows, :] = value
                previous[f] = value
        for k in range(sz.lev - 1, -1, -1):
            at = k * sz.rows
            wet = lev > k
            for f in range(sz.nf):
                here = f * sz.slab + at
                if k < sz.lev - 1:
                    previous[f] = forward[here : here + sz.rows, :] - ratio[at : at + sz.rows, :] * previous[f]
                out[f, at : at + sz.rows, :] = keep(wet, previous[f])
            if k % chunk == 0:
                send(0, sz.nf, k // chunk)

    @pl.when(is_dynamics)
    def _():
        physics()
        finish_copies()

    @pl.when(jnp.logical_not(is_dynamics))
    def _():
        transport(TIME_STEP / NSUB)
        finish_copies()


def pair_of(index, count, odd):
    if not odd:
        return index ^ 1
    return (((index + 1) ^ 1) - 1) % count


def on_device(sizes_of, fields, levels):
    sz = Sizes(fields, levels)
    count_s, count_o, count_a = sizes_of
    flat = fields.reshape(sz.nf * sz.slab, sz.cols)

    def place(s, o, a):
        return (s * count_o + o) * count_a + a

    def partner(s, o, a, odd, hop):
        b = pair_of(a, count_a, odd)
        if abs(a - b) > 1 and count_o % 2 == 0:
            return place(s, o ^ 1, a)
        return place((s + hop) % count_s, o, b)

    def swap(value, odd, hop=0):
        pairs = [
            (place(s, o, a), partner(s, o, a, odd, hop))
            for s in range(count_s)
            for o in range(count_o)
            for a in range(count_a)
        ]
        return lax.ppermute(value, ("sect", "lon", "lat"), pairs)

    def from_dynamics(value, odd=None):
        mine = lax.axis_index("sect")
        got = None
        for hop in range(1, count_s):
            if odd is None:
                part = lax.ppermute(value, "sect", [(s, (s + hop) % count_s) for s in range(count_s)])
            else:
                part = swap(value, odd, hop)
            got = part if got is None else jnp.where(mine == hop, part, got)
        return got

    def around(value, step):
        return lax.ppermute(value, "lon", [(i, (i + step) % count_o) for i in range(count_o)])

    rows_shape = (2 * sz.nf * sz.lev, sz.cols)
    cross_shape = (LEVEL_ROW * sz.lev + 8, sz.cols)
    columns_shape = (4 * sz.rows + sz.lev, sz.cols)
    side_shape = (4 * sz.rows, sz.cols)
    slab = (sz.slab, sz.cols)
    row_a, row_b, own_side, zonal, merid = call_kernel(
        functools.partial(pack_edges, sz), [rows_shape, rows_shape, side_shape, slab, slab], [flat]
    )
    twin_shape = (4 * sz.rows + LEVEL_ROW * sz.lev, sz.cols)
    (cross_b,) = call_kernel(functools.partial(pack_cross, sz), [cross_shape], [flat, levels])
    row_a = swap(row_a, False)
    levels_a = swap(levels, False)
    row_b = swap(row_b, True)
    (twin,) = call_kernel(
        functools.partial(pack_twin, sz), [twin_shape], [own_side, row_a]
    )
    twin = from_dynamics(twin)
    cross_b = from_dynamics(cross_b, True)
    south, north, corners = call_kernel(
        functools.partial(place_rows, sz), [rows_shape, rows_shape, (sz.rows, sz.cols)], [row_a, row_b]
    )
    (mixing,) = call_kernel(
        functools.partial(pack_mixing, sz), [(sz.slab, sz.cols)], [flat, levels, levels_a, cross_b, south, north]
    )
    to_east, to_west, cross_south, cross_north = call_kernel(
        functools.partial(pack_columns, sz),
        [columns_shape] * 2 + [cross_shape] * 2,
        [levels, levels_a, south, north, corners, twin, cross_b, own_side],
    )
    mixing = from_dynamics(mixing)
    zonal, merid = from_dynamics(zonal), from_dynamics(merid)
    from_east = around(to_west, -1)
    from_west = around(to_east, 1)
    kept, moved_e, moved_w, around_n, around_s = call_kernel(
        functools.partial(shift_fields, sz), [flat.shape] * 5, [flat, levels, south, north, cross_south, cross_north]
    )
    around_e, around_w, second, edge_mix = call_kernel(
        functools.partial(column_edges, sz),
        [flat.shape] * 3 + [slab],
        [levels, cross_south, cross_north, to_east, to_west, twin, from_west, from_east, moved_e, moved_w],
    )
    out_shape = (sz.nf, sz.slab, sz.cols)
    strip = (sz.nf * sz.lev, sz.cols)
    (out,) = call_kernel(
        functools.partial(finish, sz),
        [out_shape],
        [
            kept, levels, south, north, cross_south, cross_north, zonal, merid, mixing, twin, from_west, from_east,
            moved_e, moved_w, around_e, around_w, around_n, around_s, second, edge_mix,
        ],
        [out_shape, slab, slab, slab, strip, strip, slab, flat.shape, slab, (5 * sz.slab, sz.cols), slab, flat.shape],
        copies=3 * CHUNKS,
    )
    return out.reshape(fields.shape)


def solution(mesh):
    sizes_of = (mesh.shape["sect"], mesh.shape["lon"], mesh.shape["lat"])
    return jax.shard_map(
        functools.partial(on_device, sizes_of),
        mesh=mesh,
        in_specs=(P("sect", None, None, "lat", "lon"), P("lat", "lon")),
        out_specs=P("sect", None, None, "lat", "lon"),
        check_vma=False,
    )
```

```python
import functools
import jax
import jax.numpy as jnp
from jax import lax
from jax.experimental import pallas as pl
from jax.experimental.pallas import tpu as pltpu
from jax.sharding import PartitionSpec as P

NSUB = 2
TIME_STEP = 1.0
CORIOLIS = 0.3
THERMAL = 0.2
HALINE = 0.15
GRAVITY_SCALE = 0.05
MIX_BOOST = 4.0
RICHARDSON = 1.0

VMEM_LIMIT = 8 * 1024 * 1024
CHUNKS = 2

ZONAL_ROW, MERID_ROW, MERID_ROW2, END_ROW, LEVEL_ROW = range(5)
TEMPER_END, VISC_END = 0, 2


def call_kernel(body, outputs, inputs, scratch=(), copies=0):
    in_vmem = pl.BlockSpec(memory_space=pltpu.VMEM)
    scratch = [pltpu.VMEM(shape, jnp.float32) for shape in scratch]
    if copies:
        scratch.append(pltpu.SemaphoreType.DMA((copies,)))
    return pl.pallas_call(
        body,
        out_shape=[jax.ShapeDtypeStruct(shape, jnp.float32) for shape in outputs],
        in_specs=[in_vmem] * len(inputs),
        out_specs=[pl.BlockSpec(memory_space=pl.ANY) if copies else in_vmem] * len(outputs),
        scratch_shapes=scratch,
        compiler_params=pltpu.CompilerParams(vmem_limit_bytes=VMEM_LIMIT),
    )(*inputs)


class Sizes:
    def __init__(self, fields, levels):
        self.nf, self.lev = fields.shape[1], fields.shape[2]
        self.rows, self.cols = levels.shape
        self.slab = self.lev * self.rows


def lane_ids(shape):
    return lax.broadcasted_iota(jnp.int32, shape, 1)


def row_ids(shape):
    return lax.broadcasted_iota(jnp.int32, shape, 0)


def turn(value, shift, axis):
    size = value.shape[axis]
    shift = shift % size
    return value if shift == 0 else pltpu.roll(value, shift, axis)


def to_lane(value, source, target):
    return turn(value, target - source, 1)


def level_rows(ref, first, row, sz):
    return ref[pl.ds(first + row, sz.lev, stride=sz.rows), :]


def send_north_first(sz, fill):
    even = lax.axis_index("lat") % 2 == 0
    top, second = sz.rows - 1, sz.rows - 2

    @pl.when(even)
    def _():
        fill(0, top, second)
        fill(1, 0, 1)

    @pl.when(jnp.logical_not(even))
    def _():
        fill(0, 0, 1)
        fill(1, top, second)


def pack_edges(sz, fields, row_a, row_b, side, zonal, merid):
    zonal[...] = fields[0 : sz.slab, :]
    merid[...] = fields[sz.slab : 2 * sz.slab, :]

    def fill(which, near, far):
        message = (row_a, row_b)[which]
        for f in range(sz.nf):
            for r, row in enumerate((near, far)):
                at = (2 * f + r) * sz.lev
                message[at : at + sz.lev, :] = level_rows(fields, f * sz.slab, row, sz)

    send_north_first(sz, fill)
    for place, column in enumerate(edge_columns(sz, fields, sz.nf, 0)):
        side[place * sz.rows : (place + 1) * sz.rows, :] = column


def pack_cross(sz, fields, levels, cross):
    lev = levels[...].astype(jnp.float32)

    def fill(which, near, far):
        if which == 0:
            return
        for at, (f, row) in enumerate(((0, near), (1, near), (1, far))):
            cross[at * sz.lev : (at + 1) * sz.lev, :] = level_rows(fields, f * sz.slab, row, sz)
        cross[END_ROW * sz.lev : (END_ROW + 1) * sz.lev, :] = row_ends(
            level_rows(fields, 2 * sz.slab, near, sz), level_rows(fields, 4 * sz.slab, near, sz)
        )
        at = LEVEL_ROW * sz.lev
        cross[at : at + 1, :] = lev[near : near + 1, :]
        cross[at + 1 : at + 2, :] = lev[far : far + 1, :]
        cross[at + 2 :, :] = jnp.zeros((cross.shape[0] - at - 2, sz.cols), jnp.float32)

    send_north_first(sz, fill)


def row_ends(temper, visc):
    lane = lane_ids(temper.shape)
    ends = jnp.where(lane == TEMPER_END, temper, turn(temper, TEMPER_END + 2, 1))
    ends = jnp.where(lane == VISC_END, turn(visc, VISC_END, 1), ends)
    return jnp.where(lane == VISC_END + 1, turn(visc, VISC_END + 2, 1), ends)


def pack_twin(sz, own_side, row_a, twin):
    base = 4 * sz.rows
    twin[0:base, :] = own_side[...]
    def row_of(f, r):
        first = (2 * f + r) * sz.lev
        return row_a[first : first + sz.lev, :]

    parts = (row_of(0, 0), row_of(1, 0), row_of(1, 1), row_ends(row_of(2, 0), row_of(4, 0)))
    for at, part in enumerate(parts):
        twin[base + at * sz.lev : base + (at + 1) * sz.lev, :] = part


def edge_columns(sz, ref, count, first):
    tile = (sz.rows, sz.cols)
    lane = lane_ids(tile)
    zero = jnp.zeros(tile, jnp.float32)
    last = sz.cols - 1
    east_one, west_one, east_two, west_two = zero, zero, zero, zero
    for f in range(count):
        for k in range(sz.lev):
            at = f * sz.slab + k * sz.rows
            p = (first + f) * sz.lev + k
            moved = to_lane(ref[at : at + sz.rows, :], last, p)
            east_one = jnp.where(lane == p, moved, east_one)
            west_one = jnp.where(lane == (p + 1) % sz.cols, moved, west_one)
            west_two = jnp.where(lane == (p + 2) % sz.cols, moved, west_two)
            east_two = jnp.where(lane == (p - 1) % sz.cols, moved, east_two)
    return east_one, turn(west_one, -1, 1), turn(east_two, 1, 1), turn(west_two, -2, 1)


def place_rows(sz, row_a, row_b, south, north, corners):
    position = lax.axis_index("lat")
    even = position % 2 == 0
    first, other = row_a[...], row_b[...]
    tall = (sz.lev, sz.cols)
    lane, depth = lane_ids(tall), row_ids(tall)
    low = jnp.where(position > 0, jnp.where(even, other, first), 0.0)
    high = jnp.where(position < lax.axis_size("lat") - 1, jnp.where(even, first, other), 0.0)
    south[...] = low
    north[...] = high
    ends = []
    for column in (sz.cols - 1, 0):
        for rows in (low, high):
            total = jnp.zeros(tall, jnp.float32)
            for f in range(sz.nf):
                near = rows[2 * f * sz.lev : (2 * f + 1) * sz.lev, :]
                spread = jnp.broadcast_to(near[:, column : column + 1], tall)
                total = jnp.where(lane == f * sz.lev + depth, spread, total)
            ends.append(jnp.sum(total, axis=0, keepdims=True))
    for i, end in enumerate(ends):
        corners[i : i + 1, :] = end
    corners[len(ends) :, :] = jnp.zeros((sz.rows - len(ends), sz.cols), jnp.float32)


def beside_levels(sz, levels_a, cross_b):
    even = lax.axis_index("lat") % 2 == 0
    partner = levels_a[...].astype(jnp.float32)
    level_row = LEVEL_ROW * sz.lev

    def row_at(low, high):
        return jnp.where(even, partner[low : low + 1, :], partner[high : high + 1, :])

    near_b, far_b = (cross_b[level_row + i : level_row + i + 1, :] for i in range(2))
    return row_at(0, sz.rows - 1), row_at(1, sz.rows - 2), near_b, far_b


def pack_mixing(sz, fields, levels, levels_a, cross_b, south, north, mixing_out):
    position = lax.axis_index("lat")
    even = position % 2 == 0
    near_a, _, near_b, _ = beside_levels(sz, levels_a, cross_b)
    south_lev = jnp.where(position > 0, jnp.where(even, near_b, near_a), 0.0)
    north_lev = jnp.where(position < lax.axis_size("lat") - 1, jnp.where(even, near_a, near_b), 0.0)
    tile = (sz.rows, sz.cols)
    lev = levels[...].astype(jnp.float32)

    @pl.when(lax.axis_index("sect") == 0)
    def _():
        row = row_ids(tile)
        lev_e, lev_w = turn(lev, -1, 1), turn(lev, 1, 1)
        lev_n, lev_s = shift_north(lev, row, north_lev), shift_south(lev, row, south_lev)
        warm_above = None
        for k in range(sz.lev):
            at = k * sz.rows

            def around(f):
                value = fields[f * sz.slab + at : f * sz.slab + at + sz.rows, :]
                beyond = 2 * f * sz.lev + k
                return (
                    value, turn(value, -1, 1), turn(value, 1, 1),
                    shift_north(value, row, north[beyond : beyond + 1, :]),
                    shift_south(value, row, south[beyond : beyond + 1, :]),
                )

            wet = lev > k
            masks = wet, wet & (lev_e > k), wet & (lev_w > k), wet & (lev_n > k), wet & (lev_s > k)
            warm = diffused(around(2), around(4), masks)
            background = fields[5 * sz.slab + at : 5 * sz.slab + at + sz.rows, :]
            mixing = jnp.zeros(tile, jnp.float32) if k == 0 else mixed(warm_above, warm, background, wet)
            warm_above = warm
            mixing_out[at : at + sz.rows, :] = mixing


def pack_columns(
    sz, levels, levels_a, south, north, corners, twin, cross_b, own_side,
    to_east, to_west, cross_south, cross_north,
):
    position = lax.axis_index("lat")
    even = position % 2 == 0
    has_south = position > 0
    has_north = position < lax.axis_size("lat") - 1
    tile = (sz.rows, sz.cols)
    lane = lane_ids(tile)
    last = sz.cols - 1
    side = twin
    level_row = LEVEL_ROW * sz.lev
    near_a, far_a, near_b, far_b = beside_levels(sz, levels_a, cross_b)
    pairs = (
        (cross_south, cross_north, slice(0, level_row), twin[4 * sz.rows : 4 * sz.rows + level_row, :], cross_b[0:level_row, :]),
        (cross_south, cross_north, slice(level_row, level_row + 1), near_a, near_b),
        (cross_south, cross_north, slice(level_row + 1, level_row + 2), far_a, far_b),
    )
    for low, high, at, first, other in pairs:
        low[at, :] = jnp.where(has_south, jnp.where(even, other, first), 0.0)
        high[at, :] = jnp.where(has_north, jnp.where(even, first, other), 0.0)
    for ref in (cross_south, cross_north):
        ref[level_row + 2 : level_row + 8, :] = jnp.zeros((6, sz.cols), jnp.float32)

    tracer_lanes = lane < sz.nf * sz.lev
    for place, (message, at) in enumerate(((to_east, 0), (to_west, 0), (to_east, sz.rows), (to_west, sz.rows))):
        own = own_side[place * sz.rows : (place + 1) * sz.rows, :]
        dynamics = side[place * sz.rows : (place + 1) * sz.rows, :]
        message[at : at + sz.rows, :] = jnp.where(tracer_lanes, own, turn(dynamics, sz.nf * sz.lev, 1))

    lev = levels[...].astype(jnp.float32)
    south_lev = cross_south[level_row : level_row + 1, :]
    north_lev = cross_north[level_row : level_row + 1, :]
    base = 2 * sz.lev
    for place, (message, near, far) in enumerate(((to_east, last, last - 1), (to_west, 0, 1))):
        part = side[place * sz.rows : (place + 1) * sz.rows, :]
        part = jnp.where(lane < sz.lev, turn(part, -2 * sz.lev, 1), turn(part, -3 * sz.lev, 1))
        part = jnp.where(lane == base, to_lane(lev, near, base), part)
        part = jnp.where(lane == base + 1, to_lane(lev, far, base + 1), part)
        low = jnp.broadcast_to(to_lane(south_lev, near, base + 2), tile)
        high = jnp.broadcast_to(to_lane(north_lev, near, base + 3), tile)
        part = jnp.where(lane == base + 2, low, part)
        part = jnp.where(lane == base + 3, high, part)
        message[2 * sz.rows : 3 * sz.rows, :] = part

    tall = (sz.lev, sz.cols)
    tall_lane = lane_ids(tall)
    east_corner = jnp.zeros(tall, jnp.float32)
    west_corner = east_corner
    for r, (rows, cross) in enumerate(((south, cross_south), (north, cross_north))):
        for f in range(sz.nf + 2):
            if f < sz.nf:
                values = rows[2 * f * sz.lev : (2 * f + 1) * sz.lev, :]
            else:
                at = (ZONAL_ROW, MERID_ROW)[f - sz.nf] * sz.lev
                values = cross[at : at + sz.lev, :]
            p = r * (sz.nf + 2) + f
            moved = to_lane(values, last, p)
            east_corner = jnp.where(tall_lane == p, moved, east_corner)
            west_corner = jnp.where(tall_lane == p + 1, moved, west_corner)
    to_east[3 * sz.rows : 3 * sz.rows + sz.lev, :] = east_corner
    to_west[3 * sz.rows : 3 * sz.rows + sz.lev, :] = turn(west_corner, -1, 1)
    ends = corners[...]
    to_east[3 * sz.rows + sz.lev :, :] = ends
    to_west[3 * sz.rows + sz.lev :, :] = turn(ends, -2, 0)


def keep(mask, value):
    return jnp.where(mask, value, 0.0)


def diffused(quantity, viscosity, masks):
    mid, e, w, n, s = quantity
    visc, visc_e, visc_w, visc_n, visc_s = viscosity
    _, wet_e, wet_w, wet_n, wet_s = masks
    change = (
        keep(wet_e, 0.5 * (visc + visc_e)) * (e - mid)
        - keep(wet_w, 0.5 * (visc_w + visc)) * (mid - w)
        + keep(wet_n, 0.5 * (visc + visc_n)) * (n - mid)
        - keep(wet_s, 0.5 * (visc_s + visc)) * (mid - s)
    )
    return mid + TIME_STEP * change


def mixed(warm_above, warm, background, wet):
    jump = THERMAL * (warm_above - warm)
    return keep(wet, background * (1.0 + MIX_BOOST / (1.0 + RICHARDSON * jump * jump)))


def shift_west(value, lane, edge):
    return jnp.where(lane == 0, edge, turn(value, 1, 1))


def shift_east(value, lane, edge):
    return jnp.where(lane == value.shape[1] - 1, edge, turn(value, -1, 1))


def shift_south(value, row, edge):
    return jnp.where(row == 0, edge, turn(value, 1, 0))


def shift_north(value, row, edge):
    return jnp.where(row == value.shape[0] - 1, edge, turn(value, -1, 0))


class Weights:
    def __init__(self, east, west, north, south, step):
        self.own = 1.0 - step * (
            jnp.maximum(east, 0.0) - jnp.minimum(west, 0.0) + (jnp.maximum(north, 0.0) - jnp.minimum(south, 0.0))
        )
        self.east = -step * jnp.minimum(east, 0.0)
        self.west = step * jnp.maximum(west, 0.0)
        self.north = -step * jnp.minimum(north, 0.0)
        self.south = step * jnp.maximum(south, 0.0)

    def parts(self):
        return self.own, self.east, self.west, self.north, self.south

    @classmethod
    def of(cls, own, east, west, north, south):
        weights = cls.__new__(cls)
        weights.own, weights.east, weights.west, weights.north, weights.south = own, east, west, north, south
        return weights

    def apply(self, own, east, west, north, south):
        return self.own * own + self.east * east + self.west * west + (self.north * north + self.south * south)


def shift_fields(
    sz, fields, levels, south, north, cross_south, cross_north, kept, moved_e, moved_w, around_n, around_s
):
    kept[...] = fields[...]
    tile = (sz.rows, sz.cols)
    row = row_ids(tile)
    for at in range(0, sz.nf * sz.slab, sz.rows):
        here = slice(at, at + sz.rows)
        value = fields[here, :]
        moved_e[here, :] = turn(value, -1, 1)
        moved_w[here, :] = turn(value, 1, 1)

    def along_lat(f, k):
        value = fields[f * sz.slab + k * sz.rows : f * sz.slab + (k + 1) * sz.rows, :]
        beyond = slice(2 * f * sz.lev + k, 2 * f * sz.lev + k + 1)
        return value, shift_north(value, row, north[beyond, :]), shift_south(value, row, south[beyond, :])

    is_dynamics = lax.axis_index("sect") == 0

    @pl.when(jnp.logical_not(is_dynamics))
    def _():
        for f in range(sz.nf):
            for k in range(sz.lev):
                here = slice(f * sz.slab + k * sz.rows, f * sz.slab + (k + 1) * sz.rows)
                _, around_n[here, :], around_s[here, :] = along_lat(f, k)

    @pl.when(is_dynamics)
    def _():
        lev = levels[...].astype(jnp.float32)
        level_row = LEVEL_ROW * sz.lev
        lev_n = shift_north(lev, row, cross_north[level_row : level_row + 1, :])
        lev_s = shift_south(lev, row, cross_south[level_row : level_row + 1, :])
        press = jnp.zeros(tile, jnp.float32)
        press_n = press
        for k in range(sz.lev):
            wet, wet_n, wet_s = lev > k, lev_n > k, lev_s > k
            zonal, merid, temper, saline, visc = (along_lat(f, k) for f in range(5))
            coef_n = keep(wet & wet_n, 0.5 * (visc[0] + visc[1]))
            coef_s = keep(wet & wet_s, 0.5 * (visc[2] + visc[0]))

            def advanced(quantity):
                mid, n, s = quantity
                return mid + TIME_STEP * (coef_n * (n - mid) - coef_s * (mid - s))

            def weight(place, wet_there):
                return keep(wet_there, HALINE * saline[place] - THERMAL * temper[place])

            press = press + GRAVITY_SCALE * weight(0, wet)
            press_n = press_n + GRAVITY_SCALE * weight(1, wet_n)
            parts = (
                advanced(zonal) + TIME_STEP * CORIOLIS * merid[0],
                advanced(merid) - TIME_STEP * (CORIOLIS * zonal[0] + (press_n - press)),
                advanced(temper),
                advanced(saline),
                press,
                keep(wet & wet_n, merid[0]) - keep(wet & wet_s, merid[2]),
            )
            for f, part in enumerate(parts):
                around_n[f * sz.slab + k * sz.rows : f * sz.slab + (k + 1) * sz.rows, :] = part


def column_edges(
    sz, levels, cross_south, cross_north, own_east, own_west, side, from_west, from_east, moved_e, moved_w,
    around_e, around_w, second, edge_mix,
):
    tile = (sz.rows, sz.cols)
    lane, row = lane_ids(tile), row_ids(tile)
    last_lane, last_row = sz.cols - 1, sz.rows - 1
    lev = levels[...].astype(jnp.float32)
    level_row = LEVEL_ROW * sz.lev
    side_base = 2 * sz.lev
    west_side = from_west[2 * sz.rows : 3 * sz.rows, :]
    east_side = from_east[2 * sz.rows : 3 * sz.rows, :]
    lev_w = shift_west(lev, lane, to_lane(west_side, side_base, 0))
    lev_e = shift_east(lev, lane, to_lane(east_side, side_base, last_lane))
    south_lev, north_lev = cross_south[level_row : level_row + 1, :], cross_north[level_row : level_row + 1, :]
    lev_s = shift_south(lev, row, south_lev)
    lev_n = shift_north(lev, row, north_lev)

    def masks(k):
        wet = lev > k
        return wet, wet & (lev_e > k), wet & (lev_w > k), wet & (lev_n > k), wet & (lev_s > k)

    def column(value, at):
        return jnp.broadcast_to(value[:, at : at + 1], value.shape)

    def both(west, east):
        return jnp.concatenate([west, east], axis=0)

    tall = (sz.lev, sz.cols)
    pair_row = row_ids((2 * sz.rows, sz.cols)) % sz.rows
    pair_lane = lane_ids((2 * sz.rows, sz.cols))

    def pair_south(value, edge):
        return jnp.where(pair_row == 0, edge, turn(value, 1, 0))

    def pair_north(value, edge):
        return jnp.where(pair_row == last_row, edge, turn(value, -1, 0))

    def edge_mixing():
        diagonal = lane_ids(tall) == row_ids(tall)

        def levels_in_lanes(rows, at):
            return jnp.broadcast_to(jnp.sum(keep(diagonal, column(rows, at)), axis=0, keepdims=True), tile)

        def place(index):
            return side[index * sz.rows : (index + 1) * sz.rows, :]

        own_pair, inner_w, inner_e = both(place(1), place(0)), place(3), place(2)

        def around(f, message_lane, end):
            shift = -f * sz.lev
            outer_w, outer_e = turn(west_side, -message_lane, 1), turn(east_side, -message_lane, 1)
            own = turn(own_pair, shift, 1)
            low, high = (cross[END_ROW * sz.lev : (END_ROW + 1) * sz.lev, :] for cross in (cross_south, cross_north))
            return (
                own,
                both(turn(inner_w, shift, 1), outer_e),
                both(outer_w, turn(inner_e, shift, 1)),
                pair_north(own, both(levels_in_lanes(high, end), levels_in_lanes(high, end + 1))),
                pair_south(own, both(levels_in_lanes(low, end), levels_in_lanes(low, end + 1))),
            )

        depth = pair_lane.astype(jnp.float32)

        def wet(value):
            return both(column(value, 0), column(value, last_lane)) > depth

        mid = wet(lev)
        mask = mid, mid & wet(lev_e), mid & wet(lev_w), mid & wet(lev_n), mid & wet(lev_s)
        warm = diffused(around(2, 0, TEMPER_END), around(4, sz.lev, VISC_END), mask)
        background = turn(own_pair, -5 * sz.lev, 1)
        return jnp.where(pair_lane == 0, 0.0, mixed(turn(warm, 1, 1), warm, background, mid))

    def column_strips(step):
        lane16, depth16 = lane_ids(tall), row_ids(tall)

        def all_fields(value, first):
            at = lane_ids(value.shape)
            value = jnp.where((at >= first) & (at < first + sz.lev), value, 0.0)
            width = sz.lev
            while width < sz.cols:
                value = value + turn(value, width, 1)
                width *= 2
            return value

        def corner_rows(message, r):
            items = message[3 * sz.rows : 3 * sz.rows + sz.lev, :]
            p = r * (sz.nf + 2)
            ends = 3 * sz.rows + sz.lev + r
            tracers = message[ends : ends + 1, :]
            spread = jnp.broadcast_to(items[:, p + sz.nf + 1 : p + sz.nf + 2], tall)
            velocity = jnp.where(lane16 % sz.lev == depth16, spread, 0.0)
            return tracers, jnp.sum(velocity, axis=0, keepdims=True)

        inside_w, inside_e = own_west[0 : sz.rows, :], own_east[0 : sz.rows, :]
        near = both(from_west[0 : sz.rows, :], from_east[0 : sz.rows, :])
        far_w, far_e = from_west[sz.rows : 2 * sz.rows, :], from_east[sz.rows : 2 * sz.rows, :]
        corners = [corner_rows(message, r) for message in (from_west, from_east) for r in range(2)]
        low_tracers, high_tracers, low_merid = (
            both(jnp.broadcast_to(corners[i][part], tile), jnp.broadcast_to(corners[i + 2][part], tile))
            for i, part in ((0, 0), (1, 0), (0, 1))
        )

        def side_levels(at):
            return column(west_side, at), column(east_side, at)

        near_lev = both(*side_levels(side_base))
        far_lev_w, far_lev_e = side_levels(side_base + 1)
        own_lev_w, own_lev_e = column(lev, 0), column(lev, last_lane)
        lev_at_s = pair_south(near_lev, both(*side_levels(side_base + 2)))
        lev_at_n = pair_north(near_lev, both(*side_levels(side_base + 3)))
        depth = (lane_ids(near.shape) % sz.lev).astype(jnp.float32)
        wet_near = near_lev > depth
        zonal_first = sz.nf * sz.lev
        west, east = both(far_w, inside_e), both(inside_w, far_e)
        flow_e = keep(wet_near & (both(own_lev_w, far_lev_e) > depth), all_fields(near, zonal_first))
        flow_w = keep(wet_near & (both(far_lev_w, own_lev_e) > depth), all_fields(west, zonal_first))
        merid = all_fields(near, zonal_first + sz.lev)
        flow_n = keep(wet_near & (lev_at_n > depth), merid)
        flow_s = keep(wet_near & (lev_at_s > depth), pair_south(merid, low_merid))
        weights = Weights(flow_e, flow_w, flow_n, flow_s, step)
        return weights.apply(near, east, west, pair_north(near, high_tracers), pair_south(near, low_tracers))

    @pl.when(lax.axis_index("sect") > 0)
    def _():
        west_old, east_old = from_west[0 : sz.rows, :], from_east[0 : sz.rows, :]
        strips = column_strips(TIME_STEP / NSUB)
        west_new, east_new = strips[0 : sz.rows, :], strips[sz.rows : 2 * sz.rows, :]
        edges = edge_mixing()
        edge_w, edge_e = edges[0 : sz.rows, :], edges[sz.rows : 2 * sz.rows, :]
        first, last = lane == 0, lane == last_lane
        for k in range(sz.lev):
            at = k * sz.rows
            edge_mix[at : at + sz.rows, :] = jnp.where(first, to_lane(edge_w, k, 0), to_lane(edge_e, k, last_lane))
            for f in range(sz.nf):
                here = slice(f * sz.slab + at, f * sz.slab + at + sz.rows)
                p = f * sz.lev + k
                around_e[here, :] = jnp.where(last, to_lane(east_old, p, last_lane), moved_e[here, :])
                around_w[here, :] = jnp.where(first, to_lane(west_old, p, 0), moved_w[here, :])
        for k in range(sz.lev):
            for f in range(sz.nf):
                here = slice(f * sz.slab + k * sz.rows, f * sz.slab + (k + 1) * sz.rows)
                p = f * sz.lev + k
                second[here, :] = jnp.where(first, to_lane(west_new, p, 0), to_lane(east_new, p, last_lane))


def finish(
    sz, fields, levels, south, north, cross_south, cross_north, zonal_in, merid_in, mixing_in,
    side, from_west, from_east, moved_e, moved_w, around_e, around_w, around_n, around_s, second, edge_mix,
    result, out, div, mix, vert, low_strip, high_strip, ratio, forward, inv_ref, wref, pull, moved, sent,
):
    tile = (sz.rows, sz.cols)
    lane, row = lane_ids(tile), row_ids(tile)
    last_lane, last_row = sz.cols - 1, sz.rows - 1
    lev = levels[...].astype(jnp.float32)
    level_row = LEVEL_ROW * sz.lev
    side_base = 2 * sz.lev
    west_side = from_west[2 * sz.rows : 3 * sz.rows, :]
    east_side = from_east[2 * sz.rows : 3 * sz.rows, :]
    lev_w = shift_west(lev, lane, to_lane(west_side, side_base, 0))
    lev_e = shift_east(lev, lane, to_lane(east_side, side_base, last_lane))
    south_lev, north_lev = cross_south[level_row : level_row + 1, :], cross_north[level_row : level_row + 1, :]
    lev_s = shift_south(lev, row, south_lev)
    lev_n = shift_north(lev, row, north_lev)

    def masks(k):
        wet = lev > k
        return wet, wet & (lev_e > k), wet & (lev_w > k), wet & (lev_n > k), wet & (lev_s > k)

    is_dynamics = lax.axis_index("sect") == 0
    chunk = sz.lev // CHUNKS
    copies = []

    def send(first, last, part):
        at = pl.ds(part * chunk * sz.rows, chunk * sz.rows)
        copy = pltpu.make_async_copy(
            out.at[pl.ds(first, last - first), at, :], result.at[pl.ds(first, last - first), at, :], sent.at[len(copies)]
        )
        copy.start()
        copies.append(copy)

    def finish_copies():
        for copy in copies:
            copy.wait()
        copies.clear()

    def physics():
        def around(f, k):
            here = slice(f * sz.slab + k * sz.rows, f * sz.slab + (k + 1) * sz.rows)
            lane_at = f * sz.lev + k
            return (
                fields[here, :],
                jnp.where(lane == last_lane, to_lane(from_east[0 : sz.rows, :], lane_at, last_lane), moved_e[here, :]),
                jnp.where(lane == 0, to_lane(from_west[0 : sz.rows, :], lane_at, 0), moved_w[here, :]),
            )

        total = jnp.zeros(tile, jnp.float32)
        for k in range(sz.lev - 1, -1, -1):
            at = k * sz.rows
            _, wet_e, wet_w, _, _ = masks(k)
            zonal_mid, _, zonal_west = around(0, k)
            div_far = around_n[5 * sz.slab + at : 5 * sz.slab + at + sz.rows, :]
            total = total + (keep(wet_e, zonal_mid) - keep(wet_w, zonal_west) + div_far)
            out[4, at : at + sz.rows, :] = -total if k > 0 else jnp.zeros(tile, jnp.float32)
            if k % chunk == 0:
                send(4, 5, k // chunk)
        press_e, warm_above = jnp.zeros(tile, jnp.float32), None
        for k in range(sz.lev):
            at = k * sz.rows
            wet, wet_e, wet_w, wet_n, _ = masks(k)
            zonal, merid, temper, saline, visc = (around(f, k) for f in range(5))
            zonal_far, merid_far, temper_far, saline_far, press = (
                around_n[f * sz.slab + at : f * sz.slab + at + sz.rows, :] for f in range(5)
            )
            coef_e = keep(wet_e, 0.5 * (visc[0] + visc[1]))
            coef_w = keep(wet_w, 0.5 * (visc[2] + visc[0]))

            def along_lon(quantity):
                mid, e, w = quantity
                return TIME_STEP * (coef_e * (e - mid) - coef_w * (mid - w))

            warm = temper_far + along_lon(temper)
            mixing = jnp.zeros(tile, jnp.float32)
            if k > 0:
                background = fields[5 * sz.slab + at : 5 * sz.slab + at + sz.rows, :]
                mixing = mixed(warm_above, warm, background, wet)
            warm_above = warm
            press_e = press_e + GRAVITY_SCALE * keep(lev_e > k, HALINE * saline[1] - THERMAL * temper[1])
            zonal_new = zonal_far + along_lon(zonal) - TIME_STEP * (press_e - press)
            merid_new = merid_far + along_lon(merid)
            saline_new = saline_far + along_lon(saline)
            parts = (keep(wet_e, zonal_new), keep(wet_n, merid_new), warm, saline_new, None, mixing)
            for f, part in enumerate(parts):
                if part is not None:
                    out[f, at : at + sz.rows, :] = part
            if k % chunk == chunk - 1:
                send(0, 4, k // chunk)
                send(5, 6, k // chunk)

    tall = (sz.lev, sz.cols)

    def row_strips(step):
        lane16, depth = lane_ids(tall), row_ids(tall).astype(jnp.float32)

        def wet(levels_row):
            return levels_row > depth

        west_corner = from_west[3 * sz.rows : 3 * sz.rows + sz.lev, :]
        east_corner = from_east[3 * sz.rows : 3 * sz.rows + sz.lev, :]
        lane1 = lane_ids((1, sz.cols))
        for r in range(2):
            rows, cross = (south, cross_south) if r == 0 else (north, cross_north)
            strip = low_strip if r == 0 else high_strip
            edge = 0 if r == 0 else last_row
            near_lev = cross[level_row : level_row + 1, :]
            far_lev = cross[level_row + 1 : level_row + 2, :]
            own_lev = lev[edge : edge + 1, :]
            corner_lane = side_base + 2 + r
            lev_at_w = shift_west(near_lev, lane1, to_lane(west_side[0:1, :], corner_lane, 0))
            lev_at_e = shift_east(near_lev, lane1, to_lane(east_side[0:1, :], corner_lane, last_lane))
            wet_near = wet(near_lev)
            zonal = cross[ZONAL_ROW * sz.lev : (ZONAL_ROW + 1) * sz.lev, :]
            p = r * (sz.nf + 2)
            zonal_w = shift_west(zonal, lane16, to_lane(west_corner, p + sz.nf, 0))
            flow_e = keep(wet_near & wet(lev_at_e), zonal)
            flow_w = keep(wet_near & wet(lev_at_w), zonal_w)
            merid = cross[MERID_ROW * sz.lev : (MERID_ROW + 1) * sz.lev, :]
            if r == 0:
                merid_far = cross[MERID_ROW2 * sz.lev : (MERID_ROW2 + 1) * sz.lev, :]
                flow_n = keep(wet_near & wet(own_lev), merid)
                flow_s = keep(wet_near & wet(far_lev), merid_far)
            else:
                flow_n = keep(wet_near & wet(far_lev), merid)
                flow_s = keep(wet_near & wet(own_lev), level_rows(merid_in, 0, last_row, sz))
            weights = Weights(flow_e, flow_w, flow_n, flow_s, step)
            for f in range(sz.nf):
                at = 2 * f * sz.lev
                near, far = rows[at : at + sz.lev, :], rows[at + sz.lev : at + 2 * sz.lev, :]
                inside = level_rows(fields, f * sz.slab, edge, sz)
                at_w = shift_west(near, lane16, to_lane(west_corner, p + f, 0))
                at_e = shift_east(near, lane16, to_lane(east_corner, p + f, last_lane))
                up, down = (inside, far) if r == 0 else (far, inside)
                strip[f * sz.lev : (f + 1) * sz.lev, :] = weights.apply(near, at_e, at_w, up, down)

    def transport(step):
        west_old = from_west[0 : sz.rows, :]
        zero = jnp.zeros(tile, jnp.float32)

        def faces(k):
            if k == sz.lev:
                return zero, zero
            at = k * sz.rows
            speed, mixing = vert[at : at + sz.rows, :], mix[at : at + sz.rows, :]
            return jnp.maximum(speed, 0.0) + mixing, jnp.minimum(speed, 0.0) - mixing

        every = range(sz.nf)

        def stored_weights(k):
            at = k * sz.rows
            return Weights.of(*(wref[i * sz.slab + at : i * sz.slab + at + sz.rows, :] for i in range(5)))

        for k in range(sz.lev):
            at = k * sz.rows
            wet, wet_e, wet_w, wet_n, wet_s = masks(k)
            zonal, merid = zonal_in[at : at + sz.rows, :], merid_in[at : at + sz.rows, :]
            zonal_first = sz.nf * sz.lev
            zonal_west = shift_west(zonal, lane, to_lane(west_old, zonal_first + k, 0))
            beyond = MERID_ROW * sz.lev + k
            merid_south = shift_south(merid, row, cross_south[beyond : beyond + 1, :])
            flow_e, flow_w, flow_n, flow_s = (
                keep(wet_e, zonal), keep(wet_w, zonal_west), keep(wet_n, merid), keep(wet_s, merid_south)
            )
            div[at : at + sz.rows, :] = flow_e - flow_w + (flow_n - flow_s)
            weights = Weights(flow_e, flow_w, flow_n, flow_s, step)
            for i, part in enumerate(weights.parts()):
                wref[i * sz.slab + at : i * sz.slab + at + sz.rows, :] = part
        row_strips(step)
        for k in range(sz.lev):
            at = k * sz.rows
            weights = stored_weights(k)
            for f in every:
                here = slice(f * sz.slab + at, f * sz.slab + at + sz.rows)
                forward[here, :] = weights.apply(*(ref[here, :] for ref in (fields, around_e, around_w, around_n, around_s)))
        at_edge = (lane == 0) | (lane == last_lane)
        total = zero
        for k in range(sz.lev - 1, -1, -1):
            at = k * sz.rows
            total = total + div[at : at + sz.rows, :]
            vert[at : at + sz.rows, :] = -total if k > 0 else zero
            mixing = mixing_in[at : at + sz.rows, :]
            mix[at : at + sz.rows, :] = jnp.where(at_edge, edge_mix[at : at + sz.rows, :], mixing)
        last_ratio = None
        up, down = faces(0)
        lower, inverse = [], []
        for k in range(sz.lev):
            at = k * sz.rows
            up_next, down_next = faces(k + 1)
            pivot = 1.0 + TIME_STEP * (up - down_next)
            lower.append(TIME_STEP * down)
            if k > 0:
                pivot = pivot - lower[k] * last_ratio
            inverse.append(1.0 / pivot)
            last_ratio = -TIME_STEP * up_next * inverse[k]
            ratio[at : at + sz.rows, :] = last_ratio
            inv_ref[at : at + sz.rows, :] = inverse[k]
            pull[at : at + sz.rows, :] = lower[k] * inverse[k]
            up, down = up_next, down_next
        previous = [None] * sz.nf
        for k in range(sz.lev):
            at = k * sz.rows
            weights = stored_weights(k)
            values = [forward[f * sz.slab + at : f * sz.slab + at + sz.rows, :] for f in every]
            to_e, to_w = [turn(value, -1, 1) for value in values], [turn(value, 1, 1) for value in values]
            for f in every:
                here = slice(f * sz.slab + at, f * sz.slab + at + sz.rows)
                beyond = slice(f * sz.lev + k, f * sz.lev + k + 1)
                edge = second[here, :]
                value = weights.apply(
                    values[f],
                    jnp.where(lane == last_lane, edge, to_e[f]),
                    jnp.where(lane == 0, edge, to_w[f]),
                    shift_north(values[f], row, high_strip[beyond, :]),
                    shift_south(values[f], row, low_strip[beyond, :]),
                )
                moved[here, :] = value * inv_ref[at : at + sz.rows, :]
        for k in range(sz.lev):
            at = k * sz.rows
            for f in every:
                here = f * sz.slab + at
                value = moved[here : here + sz.rows, :]
                if k > 0:
                    value = value - pull[at : at + sz.rows, :] * previous[f]
                forward[here : here + sz.rows, :] = value
                previous[f] = value
        for k in range(sz.lev - 1, -1, -1):
            at = k * sz.rows
            wet = lev > k
            for f in range(sz.nf):
                here = f * sz.slab + at
                if k < sz.lev - 1:
                    previous[f] = forward[here : here + sz.rows, :] - ratio[at : at + sz.rows, :] * previous[f]
                out[f, at : at + sz.rows, :] = keep(wet, previous[f])
            if k % chunk == 0:
                send(0, sz.nf, k // chunk)

    @pl.when(is_dynamics)
    def _():
        physics()
        finish_copies()

    @pl.when(jnp.logical_not(is_dynamics))
    def _():
        transport(TIME_STEP / NSUB)
        finish_copies()


def pair_of(index, count, odd):
    if not odd:
        return index ^ 1
    return (((index + 1) ^ 1) - 1) % count


def on_device(sizes_of, fields, levels):
    sz = Sizes(fields, levels)
    count_s, count_o, count_a = sizes_of
    flat = fields.reshape(sz.nf * sz.slab, sz.cols)

    def place(s, o, a):
        return (s * count_o + o) * count_a + a

    def partner(s, o, a, odd, hop):
        b = pair_of(a, count_a, odd)
        if abs(a - b) > 1 and count_o % 2 == 0:
            return place(s, o ^ 1, a)
        return place((s + hop) % count_s, o, b)

    def swap(value, odd, hop=0):
        pairs = [
            (place(s, o, a), partner(s, o, a, odd, hop))
            for s in range(count_s)
            for o in range(count_o)
            for a in range(count_a)
        ]
        return lax.ppermute(value, ("sect", "lon", "lat"), pairs)

    def from_dynamics(value, odd=None):
        mine = lax.axis_index("sect")
        got = None
        for hop in range(1, count_s):
            if odd is None:
                part = lax.ppermute(value, "sect", [(s, (s + hop) % count_s) for s in range(count_s)])
            else:
                part = swap(value, odd, hop)
            got = part if got is None else jnp.where(mine == hop, part, got)
        return got

    def around(value, step):
        return lax.ppermute(value, "lon", [(i, (i + step) % count_o) for i in range(count_o)])

    rows_shape = (2 * sz.nf * sz.lev, sz.cols)
    cross_shape = (LEVEL_ROW * sz.lev + 8, sz.cols)
    columns_shape = (4 * sz.rows + sz.lev, sz.cols)
    side_shape = (4 * sz.rows, sz.cols)
    slab = (sz.slab, sz.cols)
    row_a, row_b, own_side, zonal, merid = call_kernel(
        functools.partial(pack_edges, sz), [rows_shape, rows_shape, side_shape, slab, slab], [flat]
    )
    twin_shape = (4 * sz.rows + LEVEL_ROW * sz.lev, sz.cols)
    (cross_b,) = call_kernel(functools.partial(pack_cross, sz), [cross_shape], [flat, levels])
    row_a = swap(row_a, False)
    levels_a = swap(levels, False)
    row_b = swap(row_b, True)
    (twin,) = call_kernel(
        functools.partial(pack_twin, sz), [twin_shape], [own_side, row_a]
    )
    twin = from_dynamics(twin)
    cross_b = from_dynamics(cross_b, True)
    south, north, corners = call_kernel(
        functools.partial(place_rows, sz), [rows_shape, rows_shape, (sz.rows, sz.cols)], [row_a, row_b]
    )
    (mixing,) = call_kernel(
        functools.partial(pack_mixing, sz), [(sz.slab, sz.cols)], [flat, levels, levels_a, cross_b, south, north]
    )
    to_east, to_west, cross_south, cross_north = call_kernel(
        functools.partial(pack_columns, sz),
        [columns_shape] * 2 + [cross_shape] * 2,
        [levels, levels_a, south, north, corners, twin, cross_b, own_side],
    )
    mixing = from_dynamics(mixing)
    zonal, merid = from_dynamics(zonal), from_dynamics(merid)
    from_east = around(to_west, -1)
    from_west = around(to_east, 1)
    kept, moved_e, moved_w, around_n, around_s = call_kernel(
        functools.partial(shift_fields, sz), [flat.shape] * 5, [flat, levels, south, north, cross_south, cross_north]
    )
    around_e, around_w, second, edge_mix = call_kernel(
        functools.partial(column_edges, sz),
        [flat.shape] * 3 + [slab],
        [levels, cross_south, cross_north, to_east, to_west, twin, from_west, from_east, moved_e, moved_w],
    )
    out_shape = (sz.nf, sz.slab, sz.cols)
    strip = (sz.nf * sz.lev, sz.cols)
    (out,) = call_kernel(
        functools.partial(finish, sz),
        [out_shape],
        [
            kept, levels, south, north, cross_south, cross_north, zonal, merid, mixing, twin, from_west, from_east,
            moved_e, moved_w, around_e, around_w, around_n, around_s, second, edge_mix,
        ],
        [out_shape, slab, slab, slab, strip, strip, slab, flat.shape, slab, (5 * sz.slab, sz.cols), slab, flat.shape],
        copies=3 * CHUNKS,
    )
    return out.reshape(fields.shape)


def solution(mesh):
    sizes_of = (mesh.shape["sect"], mesh.shape["lon"], mesh.shape["lat"])
    return jax.shard_map(
        functools.partial(on_device, sizes_of),
        mesh=mesh,
        in_specs=(P("sect", None, None, "lat", "lon"), P("lat", "lon")),
        out_specs=P("sect", None, None, "lat", "lon"),
        check_vma=False,
    )
```

```python
import functools
import jax
import jax.numpy as jnp
from jax import lax
from jax.experimental import pallas as pl
from jax.experimental.pallas import tpu as pltpu
from jax.sharding import PartitionSpec as P

NSUB = 2
TIME_STEP = 1.0
CORIOLIS = 0.3
THERMAL = 0.2
HALINE = 0.15
GRAVITY_SCALE = 0.05
MIX_BOOST = 4.0
RICHARDSON = 1.0

VMEM_LIMIT = 8 * 1024 * 1024
CHUNKS = 1

ZONAL_ROW, MERID_ROW, MERID_ROW2, END_ROW, LEVEL_ROW = range(5)
TEMPER_END, VISC_END = 0, 2


def call_kernel(body, outputs, inputs, scratch=(), copies=0):
    in_vmem = pl.BlockSpec(memory_space=pltpu.VMEM)
    scratch = [pltpu.VMEM(shape, jnp.float32) for shape in scratch]
    if copies:
        scratch.append(pltpu.SemaphoreType.DMA((copies,)))
    return pl.pallas_call(
        body,
        out_shape=[jax.ShapeDtypeStruct(shape, jnp.float32) for shape in outputs],
        in_specs=[in_vmem] * len(inputs),
        out_specs=[pl.BlockSpec(memory_space=pl.ANY) if copies else in_vmem] * len(outputs),
        scratch_shapes=scratch,
        compiler_params=pltpu.CompilerParams(vmem_limit_bytes=VMEM_LIMIT),
    )(*inputs)


class Sizes:
    def __init__(self, fields, levels):
        self.nf, self.lev = fields.shape[1], fields.shape[2]
        self.rows, self.cols = levels.shape
        self.slab = self.lev * self.rows


def lane_ids(shape):
    return lax.broadcasted_iota(jnp.int32, shape, 1)


def row_ids(shape):
    return lax.broadcasted_iota(jnp.int32, shape, 0)


def turn(value, shift, axis):
    size = value.shape[axis]
    shift = shift % size
    return value if shift == 0 else pltpu.roll(value, shift, axis)


def to_lane(value, source, target):
    return turn(value, target - source, 1)


def level_rows(ref, first, row, sz):
    return ref[pl.ds(first + row, sz.lev, stride=sz.rows), :]


def send_north_first(sz, fill):
    even = lax.axis_index("lat") % 2 == 0
    top, second = sz.rows - 1, sz.rows - 2

    @pl.when(even)
    def _():
        fill(0, top, second)
        fill(1, 0, 1)

    @pl.when(jnp.logical_not(even))
    def _():
        fill(0, 0, 1)
        fill(1, top, second)


def pack_edges(sz, fields, row_a, row_b, side, zonal, merid):
    zonal[...] = fields[0 : sz.slab, :]
    merid[...] = fields[sz.slab : 2 * sz.slab, :]

    def fill(which, near, far):
        message = (row_a, row_b)[which]
        for f in range(sz.nf):
            for r, row in enumerate((near, far)):
                at = (2 * f + r) * sz.lev
                message[at : at + sz.lev, :] = level_rows(fields, f * sz.slab, row, sz)

    send_north_first(sz, fill)
    for place, column in enumerate(edge_columns(sz, fields, sz.nf, 0)):
        side[place * sz.rows : (place + 1) * sz.rows, :] = column


def pack_cross(sz, fields, levels, cross):
    lev = levels[...].astype(jnp.float32)

    def fill(which, near, far):
        if which == 0:
            return
        for at, (f, row) in enumerate(((0, near), (1, near), (1, far))):
            cross[at * sz.lev : (at + 1) * sz.lev, :] = level_rows(fields, f * sz.slab, row, sz)
        cross[END_ROW * sz.lev : (END_ROW + 1) * sz.lev, :] = row_ends(
            level_rows(fields, 2 * sz.slab, near, sz), level_rows(fields, 4 * sz.slab, near, sz)
        )
        at = LEVEL_ROW * sz.lev
        cross[at : at + 1, :] = lev[near : near + 1, :]
        cross[at + 1 : at + 2, :] = lev[far : far + 1, :]
        cross[at + 2 :, :] = jnp.zeros((cross.shape[0] - at - 2, sz.cols), jnp.float32)

    send_north_first(sz, fill)


def row_ends(temper, visc):
    lane = lane_ids(temper.shape)
    ends = jnp.where(lane == TEMPER_END, temper, turn(temper, TEMPER_END + 2, 1))
    ends = jnp.where(lane == VISC_END, turn(visc, VISC_END, 1), ends)
    return jnp.where(lane == VISC_END + 1, turn(visc, VISC_END + 2, 1), ends)


def pack_twin(sz, own_side, row_a, twin):
    base = 4 * sz.rows
    twin[0:base, :] = own_side[...]
    def row_of(f, r):
        first = (2 * f + r) * sz.lev
        return row_a[first : first + sz.lev, :]

    parts = (row_of(0, 0), row_of(1, 0), row_of(1, 1), row_ends(row_of(2, 0), row_of(4, 0)))
    for at, part in enumerate(parts):
        twin[base + at * sz.lev : base + (at + 1) * sz.lev, :] = part


def edge_columns(sz, ref, count, first):
    tile = (sz.rows, sz.cols)
    lane = lane_ids(tile)
    zero = jnp.zeros(tile, jnp.float32)
    last = sz.cols - 1
    east_one, west_one, east_two, west_two = zero, zero, zero, zero
    for f in range(count):
        for k in range(sz.lev):
            at = f * sz.slab + k * sz.rows
            p = (first + f) * sz.lev + k
            moved = to_lane(ref[at : at + sz.rows, :], last, p)
            east_one = jnp.where(lane == p, moved, east_one)
            west_one = jnp.where(lane == (p + 1) % sz.cols, moved, west_one)
            west_two = jnp.where(lane == (p + 2) % sz.cols, moved, west_two)
            east_two = jnp.where(lane == (p - 1) % sz.cols, moved, east_two)
    return east_one, turn(west_one, -1, 1), turn(east_two, 1, 1), turn(west_two, -2, 1)


def place_rows(sz, row_a, row_b, south, north, corners):
    position = lax.axis_index("lat")
    even = position % 2 == 0
    first, other = row_a[...], row_b[...]
    tall = (sz.lev, sz.cols)
    lane, depth = lane_ids(tall), row_ids(tall)
    low = jnp.where(position > 0, jnp.where(even, other, first), 0.0)
    high = jnp.where(position < lax.axis_size("lat") - 1, jnp.where(even, first, other), 0.0)
    south[...] = low
    north[...] = high
    ends = []
    for column in (sz.cols - 1, 0):
        for rows in (low, high):
            total = jnp.zeros(tall, jnp.float32)
            for f in range(sz.nf):
                near = rows[2 * f * sz.lev : (2 * f + 1) * sz.lev, :]
                spread = jnp.broadcast_to(near[:, column : column + 1], tall)
                total = jnp.where(lane == f * sz.lev + depth, spread, total)
            ends.append(jnp.sum(total, axis=0, keepdims=True))
    for i, end in enumerate(ends):
        corners[i : i + 1, :] = end
    corners[len(ends) :, :] = jnp.zeros((sz.rows - len(ends), sz.cols), jnp.float32)


def beside_levels(sz, levels_a, cross_b):
    even = lax.axis_index("lat") % 2 == 0
    partner = levels_a[...].astype(jnp.float32)
    level_row = LEVEL_ROW * sz.lev

    def row_at(low, high):
        return jnp.where(even, partner[low : low + 1, :], partner[high : high + 1, :])

    near_b, far_b = (cross_b[level_row + i : level_row + i + 1, :] for i in range(2))
    return row_at(0, sz.rows - 1), row_at(1, sz.rows - 2), near_b, far_b


def pack_mixing(sz, fields, levels, levels_a, cross_b, south, north, mixing_out):
    position = lax.axis_index("lat")
    even = position % 2 == 0
    near_a, _, near_b, _ = beside_levels(sz, levels_a, cross_b)
    south_lev = jnp.where(position > 0, jnp.where(even, near_b, near_a), 0.0)
    north_lev = jnp.where(position < lax.axis_size("lat") - 1, jnp.where(even, near_a, near_b), 0.0)
    tile = (sz.rows, sz.cols)
    lev = levels[...].astype(jnp.float32)

    @pl.when(lax.axis_index("sect") == 0)
    def _():
        row = row_ids(tile)
        lev_e, lev_w = turn(lev, -1, 1), turn(lev, 1, 1)
        lev_n, lev_s = shift_north(lev, row, north_lev), shift_south(lev, row, south_lev)
        warm_above = None
        for k in range(sz.lev):
            at = k * sz.rows

            def around(f):
                value = fields[f * sz.slab + at : f * sz.slab + at + sz.rows, :]
                beyond = 2 * f * sz.lev + k
                return (
                    value, turn(value, -1, 1), turn(value, 1, 1),
                    shift_north(value, row, north[beyond : beyond + 1, :]),
                    shift_south(value, row, south[beyond : beyond + 1, :]),
                )

            wet = lev > k
            masks = wet, wet & (lev_e > k), wet & (lev_w > k), wet & (lev_n > k), wet & (lev_s > k)
            warm = diffused(around(2), around(4), masks)
            background = fields[5 * sz.slab + at : 5 * sz.slab + at + sz.rows, :]
            mixing = jnp.zeros(tile, jnp.float32) if k == 0 else mixed(warm_above, warm, background, wet)
            warm_above = warm
            mixing_out[at : at + sz.rows, :] = mixing


def pack_columns(
    sz, levels, levels_a, south, north, corners, twin, cross_b, own_side,
    to_east, to_west, cross_south, cross_north,
):
    position = lax.axis_index("lat")
    even = position % 2 == 0
    has_south = position > 0
    has_north = position < lax.axis_size("lat") - 1
    tile = (sz.rows, sz.cols)
    lane = lane_ids(tile)
    last = sz.cols - 1
    side = twin
    level_row = LEVEL_ROW * sz.lev
    near_a, far_a, near_b, far_b = beside_levels(sz, levels_a, cross_b)
    pairs = (
        (cross_south, cross_north, slice(0, level_row), twin[4 * sz.rows : 4 * sz.rows + level_row, :], cross_b[0:level_row, :]),
        (cross_south, cross_north, slice(level_row, level_row + 1), near_a, near_b),
        (cross_south, cross_north, slice(level_row + 1, level_row + 2), far_a, far_b),
    )
    for low, high, at, first, other in pairs:
        low[at, :] = jnp.where(has_south, jnp.where(even, other, first), 0.0)
        high[at, :] = jnp.where(has_north, jnp.where(even, first, other), 0.0)
    for ref in (cross_south, cross_north):
        ref[level_row + 2 : level_row + 8, :] = jnp.zeros((6, sz.cols), jnp.float32)

    tracer_lanes = lane < sz.nf * sz.lev
    for place, (message, at) in enumerate(((to_east, 0), (to_west, 0), (to_east, sz.rows), (to_west, sz.rows))):
        own = own_side[place * sz.rows : (place + 1) * sz.rows, :]
        dynamics = side[place * sz.rows : (place + 1) * sz.rows, :]
        message[at : at + sz.rows, :] = jnp.where(tracer_lanes, own, turn(dynamics, sz.nf * sz.lev, 1))

    lev = levels[...].astype(jnp.float32)
    south_lev = cross_south[level_row : level_row + 1, :]
    north_lev = cross_north[level_row : level_row + 1, :]
    base = 2 * sz.lev
    for place, (message, near, far) in enumerate(((to_east, last, last - 1), (to_west, 0, 1))):
        part = side[place * sz.rows : (place + 1) * sz.rows, :]
        part = jnp.where(lane < sz.lev, turn(part, -2 * sz.lev, 1), turn(part, -3 * sz.lev, 1))
        part = jnp.where(lane == base, to_lane(lev, near, base), part)
        part = jnp.where(lane == base + 1, to_lane(lev, far, base + 1), part)
        low = jnp.broadcast_to(to_lane(south_lev, near, base + 2), tile)
        high = jnp.broadcast_to(to_lane(north_lev, near, base + 3), tile)
        part = jnp.where(lane == base + 2, low, part)
        part = jnp.where(lane == base + 3, high, part)
        message[2 * sz.rows : 3 * sz.rows, :] = part

    tall = (sz.lev, sz.cols)
    tall_lane = lane_ids(tall)
    east_corner = jnp.zeros(tall, jnp.float32)
    west_corner = east_corner
    for r, (rows, cross) in enumerate(((south, cross_south), (north, cross_north))):
        for f in range(sz.nf + 2):
            if f < sz.nf:
                values = rows[2 * f * sz.lev : (2 * f + 1) * sz.lev, :]
            else:
                at = (ZONAL_ROW, MERID_ROW)[f - sz.nf] * sz.lev
                values = cross[at : at + sz.lev, :]
            p = r * (sz.nf + 2) + f
            moved = to_lane(values, last, p)
            east_corner = jnp.where(tall_lane == p, moved, east_corner)
            west_corner = jnp.where(tall_lane == p + 1, moved, west_corner)
    to_east[3 * sz.rows : 3 * sz.rows + sz.lev, :] = east_corner
    to_west[3 * sz.rows : 3 * sz.rows + sz.lev, :] = turn(west_corner, -1, 1)
    ends = corners[...]
    to_east[3 * sz.rows + sz.lev :, :] = ends
    to_west[3 * sz.rows + sz.lev :, :] = turn(ends, -2, 0)


def keep(mask, value):
    return jnp.where(mask, value, 0.0)


def diffused(quantity, viscosity, masks):
    mid, e, w, n, s = quantity
    visc, visc_e, visc_w, visc_n, visc_s = viscosity
    _, wet_e, wet_w, wet_n, wet_s = masks
    change = (
        keep(wet_e, 0.5 * (visc + visc_e)) * (e - mid)
        - keep(wet_w, 0.5 * (visc_w + visc)) * (mid - w)
        + keep(wet_n, 0.5 * (visc + visc_n)) * (n - mid)
        - keep(wet_s, 0.5 * (visc_s + visc)) * (mid - s)
    )
    return mid + TIME_STEP * change


def mixed(warm_above, warm, background, wet):
    jump = THERMAL * (warm_above - warm)
    return keep(wet, background * (1.0 + MIX_BOOST / (1.0 + RICHARDSON * jump * jump)))


def shift_west(value, lane, edge):
    return jnp.where(lane == 0, edge, turn(value, 1, 1))


def shift_east(value, lane, edge):
    return jnp.where(lane == value.shape[1] - 1, edge, turn(value, -1, 1))


def shift_south(value, row, edge):
    return jnp.where(row == 0, edge, turn(value, 1, 0))


def shift_north(value, row, edge):
    return jnp.where(row == value.shape[0] - 1, edge, turn(value, -1, 0))


class Weights:
    def __init__(self, east, west, north, south, step):
        self.own = 1.0 - step * (
            jnp.maximum(east, 0.0) - jnp.minimum(west, 0.0) + (jnp.maximum(north, 0.0) - jnp.minimum(south, 0.0))
        )
        self.east = -step * jnp.minimum(east, 0.0)
        self.west = step * jnp.maximum(west, 0.0)
        self.north = -step * jnp.minimum(north, 0.0)
        self.south = step * jnp.maximum(south, 0.0)

    def parts(self):
        return self.own, self.east, self.west, self.north, self.south

    @classmethod
    def of(cls, own, east, west, north, south):
        weights = cls.__new__(cls)
        weights.own, weights.east, weights.west, weights.north, weights.south = own, east, west, north, south
        return weights

    def apply(self, own, east, west, north, south):
        return self.own * own + self.east * east + self.west * west + (self.north * north + self.south * south)


def shift_fields(
    sz, fields, levels, south, north, cross_south, cross_north, kept, moved_e, moved_w, around_n, around_s
):
    kept[...] = fields[...]
    tile = (sz.rows, sz.cols)
    row = row_ids(tile)
    for at in range(0, sz.nf * sz.slab, sz.rows):
        here = slice(at, at + sz.rows)
        value = fields[here, :]
        moved_e[here, :] = turn(value, -1, 1)
        moved_w[here, :] = turn(value, 1, 1)

    def along_lat(f, k):
        value = fields[f * sz.slab + k * sz.rows : f * sz.slab + (k + 1) * sz.rows, :]
        beyond = slice(2 * f * sz.lev + k, 2 * f * sz.lev + k + 1)
        return value, shift_north(value, row, north[beyond, :]), shift_south(value, row, south[beyond, :])

    is_dynamics = lax.axis_index("sect") == 0

    @pl.when(jnp.logical_not(is_dynamics))
    def _():
        for f in range(sz.nf):
            for k in range(sz.lev):
                here = slice(f * sz.slab + k * sz.rows, f * sz.slab + (k + 1) * sz.rows)
                _, around_n[here, :], around_s[here, :] = along_lat(f, k)

    @pl.when(is_dynamics)
    def _():
        lev = levels[...].astype(jnp.float32)
        level_row = LEVEL_ROW * sz.lev
        lev_n = shift_north(lev, row, cross_north[level_row : level_row + 1, :])
        lev_s = shift_south(lev, row, cross_south[level_row : level_row + 1, :])
        press = jnp.zeros(tile, jnp.float32)
        press_n = press
        for k in range(sz.lev):
            wet, wet_n, wet_s = lev > k, lev_n > k, lev_s > k
            zonal, merid, temper, saline, visc = (along_lat(f, k) for f in range(5))
            coef_n = keep(wet & wet_n, 0.5 * (visc[0] + visc[1]))
            coef_s = keep(wet & wet_s, 0.5 * (visc[2] + visc[0]))

            def advanced(quantity):
                mid, n, s = quantity
                return mid + TIME_STEP * (coef_n * (n - mid) - coef_s * (mid - s))

            def weight(place, wet_there):
                return keep(wet_there, HALINE * saline[place] - THERMAL * temper[place])

            press = press + GRAVITY_SCALE * weight(0, wet)
            press_n = press_n + GRAVITY_SCALE * weight(1, wet_n)
            parts = (
                advanced(zonal) + TIME_STEP * CORIOLIS * merid[0],
                advanced(merid) - TIME_STEP * (CORIOLIS * zonal[0] + (press_n - press)),
                advanced(temper),
                advanced(saline),
                press,
                keep(wet & wet_n, merid[0]) - keep(wet & wet_s, merid[2]),
            )
            for f, part in enumerate(parts):
                around_n[f * sz.slab + k * sz.rows : f * sz.slab + (k + 1) * sz.rows, :] = part


def column_edges(
    sz, levels, cross_south, cross_north, own_east, own_west, side, from_west, from_east, moved_e, moved_w,
    around_e, around_w, second, edge_mix,
):
    tile = (sz.rows, sz.cols)
    lane, row = lane_ids(tile), row_ids(tile)
    last_lane, last_row = sz.cols - 1, sz.rows - 1
    lev = levels[...].astype(jnp.float32)
    level_row = LEVEL_ROW * sz.lev
    side_base = 2 * sz.lev
    west_side = from_west[2 * sz.rows : 3 * sz.rows, :]
    east_side = from_east[2 * sz.rows : 3 * sz.rows, :]
    lev_w = shift_west(lev, lane, to_lane(west_side, side_base, 0))
    lev_e = shift_east(lev, lane, to_lane(east_side, side_base, last_lane))
    south_lev, north_lev = cross_south[level_row : level_row + 1, :], cross_north[level_row : level_row + 1, :]
    lev_s = shift_south(lev, row, south_lev)
    lev_n = shift_north(lev, row, north_lev)

    def masks(k):
        wet = lev > k
        return wet, wet & (lev_e > k), wet & (lev_w > k), wet & (lev_n > k), wet & (lev_s > k)

    def column(value, at):
        return jnp.broadcast_to(value[:, at : at + 1], value.shape)

    def both(west, east):
        return jnp.concatenate([west, east], axis=0)

    tall = (sz.lev, sz.cols)
    pair_row = row_ids((2 * sz.rows, sz.cols)) % sz.rows
    pair_lane = lane_ids((2 * sz.rows, sz.cols))

    def pair_south(value, edge):
        return jnp.where(pair_row == 0, edge, turn(value, 1, 0))

    def pair_north(value, edge):
        return jnp.where(pair_row == last_row, edge, turn(value, -1, 0))

    def edge_mixing():
        diagonal = lane_ids(tall) == row_ids(tall)

        def levels_in_lanes(rows, at):
            return jnp.broadcast_to(jnp.sum(keep(diagonal, column(rows, at)), axis=0, keepdims=True), tile)

        def place(index):
            return side[index * sz.rows : (index + 1) * sz.rows, :]

        own_pair, inner_w, inner_e = both(place(1), place(0)), place(3), place(2)

        def around(f, message_lane, end):
            shift = -f * sz.lev
            outer_w, outer_e = turn(west_side, -message_lane, 1), turn(east_side, -message_lane, 1)
            own = turn(own_pair, shift, 1)
            low, high = (cross[END_ROW * sz.lev : (END_ROW + 1) * sz.lev, :] for cross in (cross_south, cross_north))
            return (
                own,
                both(turn(inner_w, shift, 1), outer_e),
                both(outer_w, turn(inner_e, shift, 1)),
                pair_north(own, both(levels_in_lanes(high, end), levels_in_lanes(high, end + 1))),
                pair_south(own, both(levels_in_lanes(low, end), levels_in_lanes(low, end + 1))),
            )

        depth = pair_lane.astype(jnp.float32)

        def wet(value):
            return both(column(value, 0), column(value, last_lane)) > depth

        mid = wet(lev)
        mask = mid, mid & wet(lev_e), mid & wet(lev_w), mid & wet(lev_n), mid & wet(lev_s)
        warm = diffused(around(2, 0, TEMPER_END), around(4, sz.lev, VISC_END), mask)
        background = turn(own_pair, -5 * sz.lev, 1)
        return jnp.where(pair_lane == 0, 0.0, mixed(turn(warm, 1, 1), warm, background, mid))

    def column_strips(step):
        lane16, depth16 = lane_ids(tall), row_ids(tall)

        def all_fields(value, first):
            at = lane_ids(value.shape)
            value = jnp.where((at >= first) & (at < first + sz.lev), value, 0.0)
            width = sz.lev
            while width < sz.cols:
                value = value + turn(value, width, 1)
                width *= 2
            return value

        def corner_rows(message, r):
            items = message[3 * sz.rows : 3 * sz.rows + sz.lev, :]
            p = r * (sz.nf + 2)
            ends = 3 * sz.rows + sz.lev + r
            tracers = message[ends : ends + 1, :]
            spread = jnp.broadcast_to(items[:, p + sz.nf + 1 : p + sz.nf + 2], tall)
            velocity = jnp.where(lane16 % sz.lev == depth16, spread, 0.0)
            return tracers, jnp.sum(velocity, axis=0, keepdims=True)

        inside_w, inside_e = own_west[0 : sz.rows, :], own_east[0 : sz.rows, :]
        near = both(from_west[0 : sz.rows, :], from_east[0 : sz.rows, :])
        far_w, far_e = from_west[sz.rows : 2 * sz.rows, :], from_east[sz.rows : 2 * sz.rows, :]
        corners = [corner_rows(message, r) for message in (from_west, from_east) for r in range(2)]
        low_tracers, high_tracers, low_merid = (
            both(jnp.broadcast_to(corners[i][part], tile), jnp.broadcast_to(corners[i + 2][part], tile))
            for i, part in ((0, 0), (1, 0), (0, 1))
        )

        def side_levels(at):
            return column(west_side, at), column(east_side, at)

        near_lev = both(*side_levels(side_base))
        far_lev_w, far_lev_e = side_levels(side_base + 1)
        own_lev_w, own_lev_e = column(lev, 0), column(lev, last_lane)
        lev_at_s = pair_south(near_lev, both(*side_levels(side_base + 2)))
        lev_at_n = pair_north(near_lev, both(*side_levels(side_base + 3)))
        depth = (lane_ids(near.shape) % sz.lev).astype(jnp.float32)
        wet_near = near_lev > depth
        zonal_first = sz.nf * sz.lev
        west, east = both(far_w, inside_e), both(inside_w, far_e)
        flow_e = keep(wet_near & (both(own_lev_w, far_lev_e) > depth), all_fields(near, zonal_first))
        flow_w = keep(wet_near & (both(far_lev_w, own_lev_e) > depth), all_fields(west, zonal_first))
        merid = all_fields(near, zonal_first + sz.lev)
        flow_n = keep(wet_near & (lev_at_n > depth), merid)
        flow_s = keep(wet_near & (lev_at_s > depth), pair_south(merid, low_merid))
        weights = Weights(flow_e, flow_w, flow_n, flow_s, step)
        return weights.apply(near, east, west, pair_north(near, high_tracers), pair_south(near, low_tracers))

    @pl.when(lax.axis_index("sect") > 0)
    def _():
        west_old, east_old = from_west[0 : sz.rows, :], from_east[0 : sz.rows, :]
        strips = column_strips(TIME_STEP / NSUB)
        west_new, east_new = strips[0 : sz.rows, :], strips[sz.rows : 2 * sz.rows, :]
        edges = edge_mixing()
        edge_w, edge_e = edges[0 : sz.rows, :], edges[sz.rows : 2 * sz.rows, :]
        first, last = lane == 0, lane == last_lane
        for k in range(sz.lev):
            at = k * sz.rows
            edge_mix[at : at + sz.rows, :] = jnp.where(first, to_lane(edge_w, k, 0), to_lane(edge_e, k, last_lane))
            for f in range(sz.nf):
                here = slice(f * sz.slab + at, f * sz.slab + at + sz.rows)
                p = f * sz.lev + k
                around_e[here, :] = jnp.where(last, to_lane(east_old, p, last_lane), moved_e[here, :])
                around_w[here, :] = jnp.where(first, to_lane(west_old, p, 0), moved_w[here, :])
        for k in range(sz.lev):
            for f in range(sz.nf):
                here = slice(f * sz.slab + k * sz.rows, f * sz.slab + (k + 1) * sz.rows)
                p = f * sz.lev + k
                second[here, :] = jnp.where(first, to_lane(west_new, p, 0), to_lane(east_new, p, last_lane))


def finish(
    sz, fields, levels, south, north, cross_south, cross_north, zonal_in, merid_in, mixing_in,
    side, from_west, from_east, moved_e, moved_w, around_e, around_w, around_n, around_s, second, edge_mix,
    result, out, div, mix, vert, low_strip, high_strip, ratio, forward, inv_ref, wref, pull, moved, sent,
):
    tile = (sz.rows, sz.cols)
    lane, row = lane_ids(tile), row_ids(tile)
    last_lane, last_row = sz.cols - 1, sz.rows - 1
    lev = levels[...].astype(jnp.float32)
    level_row = LEVEL_ROW * sz.lev
    side_base = 2 * sz.lev
    west_side = from_west[2 * sz.rows : 3 * sz.rows, :]
    east_side = from_east[2 * sz.rows : 3 * sz.rows, :]
    lev_w = shift_west(lev, lane, to_lane(west_side, side_base, 0))
    lev_e = shift_east(lev, lane, to_lane(east_side, side_base, last_lane))
    south_lev, north_lev = cross_south[level_row : level_row + 1, :], cross_north[level_row : level_row + 1, :]
    lev_s = shift_south(lev, row, south_lev)
    lev_n = shift_north(lev, row, north_lev)

    def masks(k):
        wet = lev > k
        return wet, wet & (lev_e > k), wet & (lev_w > k), wet & (lev_n > k), wet & (lev_s > k)

    is_dynamics = lax.axis_index("sect") == 0
    chunk = sz.lev // CHUNKS
    copies = []

    def send(first, last, part):
        at = pl.ds(part * chunk * sz.rows, chunk * sz.rows)
        copy = pltpu.make_async_copy(
            out.at[pl.ds(first, last - first), at, :], result.at[pl.ds(first, last - first), at, :], sent.at[len(copies)]
        )
        copy.start()
        copies.append(copy)

    def finish_copies():
        for copy in copies:
            copy.wait()
        copies.clear()

    def physics():
        def around(f, k):
            here = slice(f * sz.slab + k * sz.rows, f * sz.slab + (k + 1) * sz.rows)
            lane_at = f * sz.lev + k
            return (
                fields[here, :],
                jnp.where(lane == last_lane, to_lane(from_east[0 : sz.rows, :], lane_at, last_lane), moved_e[here, :]),
                jnp.where(lane == 0, to_lane(from_west[0 : sz.rows, :], lane_at, 0), moved_w[here, :]),
            )

        total = jnp.zeros(tile, jnp.float32)
        for k in range(sz.lev - 1, -1, -1):
            at = k * sz.rows
            _, wet_e, wet_w, _, _ = masks(k)
            zonal_mid, _, zonal_west = around(0, k)
            div_far = around_n[5 * sz.slab + at : 5 * sz.slab + at + sz.rows, :]
            total = total + (keep(wet_e, zonal_mid) - keep(wet_w, zonal_west) + div_far)
            out[4, at : at + sz.rows, :] = -total if k > 0 else jnp.zeros(tile, jnp.float32)
            if k % chunk == 0:
                send(4, 5, k // chunk)
        press_e, warm_above = jnp.zeros(tile, jnp.float32), None
        for k in range(sz.lev):
            at = k * sz.rows
            wet, wet_e, wet_w, wet_n, _ = masks(k)
            zonal, merid, temper, saline, visc = (around(f, k) for f in range(5))
            zonal_far, merid_far, temper_far, saline_far, press = (
                around_n[f * sz.slab + at : f * sz.slab + at + sz.rows, :] for f in range(5)
            )
            coef_e = keep(wet_e, 0.5 * (visc[0] + visc[1]))
            coef_w = keep(wet_w, 0.5 * (visc[2] + visc[0]))

            def along_lon(quantity):
                mid, e, w = quantity
                return TIME_STEP * (coef_e * (e - mid) - coef_w * (mid - w))

            warm = temper_far + along_lon(temper)
            mixing = jnp.zeros(tile, jnp.float32)
            if k > 0:
                background = fields[5 * sz.slab + at : 5 * sz.slab + at + sz.rows, :]
                mixing = mixed(warm_above, warm, background, wet)
            warm_above = warm
            press_e = press_e + GRAVITY_SCALE * keep(lev_e > k, HALINE * saline[1] - THERMAL * temper[1])
            zonal_new = zonal_far + along_lon(zonal) - TIME_STEP * (press_e - press)
            merid_new = merid_far + along_lon(merid)
            saline_new = saline_far + along_lon(saline)
            parts = (keep(wet_e, zonal_new), keep(wet_n, merid_new), warm, saline_new, None, mixing)
            for f, part in enumerate(parts):
                if part is not None:
                    out[f, at : at + sz.rows, :] = part
            if k % chunk == chunk - 1:
                send(0, 4, k // chunk)
                send(5, 6, k // chunk)

    tall = (sz.lev, sz.cols)

    def row_strips(step):
        lane16, depth = lane_ids(tall), row_ids(tall).astype(jnp.float32)

        def wet(levels_row):
            return levels_row > depth

        west_corner = from_west[3 * sz.rows : 3 * sz.rows + sz.lev, :]
        east_corner = from_east[3 * sz.rows : 3 * sz.rows + sz.lev, :]
        lane1 = lane_ids((1, sz.cols))
        for r in range(2):
            rows, cross = (south, cross_south) if r == 0 else (north, cross_north)
            strip = low_strip if r == 0 else high_strip
            edge = 0 if r == 0 else last_row
            near_lev = cross[level_row : level_row + 1, :]
            far_lev = cross[level_row + 1 : level_row + 2, :]
            own_lev = lev[edge : edge + 1, :]
            corner_lane = side_base + 2 + r
            lev_at_w = shift_west(near_lev, lane1, to_lane(west_side[0:1, :], corner_lane, 0))
            lev_at_e = shift_east(near_lev, lane1, to_lane(east_side[0:1, :], corner_lane, last_lane))
            wet_near = wet(near_lev)
            zonal = cross[ZONAL_ROW * sz.lev : (ZONAL_ROW + 1) * sz.lev, :]
            p = r * (sz.nf + 2)
            zonal_w = shift_west(zonal, lane16, to_lane(west_corner, p + sz.nf, 0))
            flow_e = keep(wet_near & wet(lev_at_e), zonal)
            flow_w = keep(wet_near & wet(lev_at_w), zonal_w)
            merid = cross[MERID_ROW * sz.lev : (MERID_ROW + 1) * sz.lev, :]
            if r == 0:
                merid_far = cross[MERID_ROW2 * sz.lev : (MERID_ROW2 + 1) * sz.lev, :]
                flow_n = keep(wet_near & wet(own_lev), merid)
                flow_s = keep(wet_near & wet(far_lev), merid_far)
            else:
                flow_n = keep(wet_near & wet(far_lev), merid)
                flow_s = keep(wet_near & wet(own_lev), level_rows(merid_in, 0, last_row, sz))
            weights = Weights(flow_e, flow_w, flow_n, flow_s, step)
            for f in range(sz.nf):
                at = 2 * f * sz.lev
                near, far = rows[at : at + sz.lev, :], rows[at + sz.lev : at + 2 * sz.lev, :]
                inside = level_rows(fields, f * sz.slab, edge, sz)
                at_w = shift_west(near, lane16, to_lane(west_corner, p + f, 0))
                at_e = shift_east(near, lane16, to_lane(east_corner, p + f, last_lane))
                up, down = (inside, far) if r == 0 else (far, inside)
                strip[f * sz.lev : (f + 1) * sz.lev, :] = weights.apply(near, at_e, at_w, up, down)

    def transport(step):
        west_old = from_west[0 : sz.rows, :]
        zero = jnp.zeros(tile, jnp.float32)

        def faces(k):
            if k == sz.lev:
                return zero, zero
            at = k * sz.rows
            speed, mixing = vert[at : at + sz.rows, :], mix[at : at + sz.rows, :]
            return jnp.maximum(speed, 0.0) + mixing, jnp.minimum(speed, 0.0) - mixing

        every = range(sz.nf)

        def stored_weights(k):
            at = k * sz.rows
            return Weights.of(*(wref[i * sz.slab + at : i * sz.slab + at + sz.rows, :] for i in range(5)))

        for k in range(sz.lev):
            at = k * sz.rows
            wet, wet_e, wet_w, wet_n, wet_s = masks(k)
            zonal, merid = zonal_in[at : at + sz.rows, :], merid_in[at : at + sz.rows, :]
            zonal_first = sz.nf * sz.lev
            zonal_west = shift_west(zonal, lane, to_lane(west_old, zonal_first + k, 0))
            beyond = MERID_ROW * sz.lev + k
            merid_south = shift_south(merid, row, cross_south[beyond : beyond + 1, :])
            flow_e, flow_w, flow_n, flow_s = (
                keep(wet_e, zonal), keep(wet_w, zonal_west), keep(wet_n, merid), keep(wet_s, merid_south)
            )
            div[at : at + sz.rows, :] = flow_e - flow_w + (flow_n - flow_s)
            weights = Weights(flow_e, flow_w, flow_n, flow_s, step)
            for i, part in enumerate(weights.parts()):
                wref[i * sz.slab + at : i * sz.slab + at + sz.rows, :] = part
        row_strips(step)
        for k in range(sz.lev):
            at = k * sz.rows
            weights = stored_weights(k)
            for f in every:
                here = slice(f * sz.slab + at, f * sz.slab + at + sz.rows)
                forward[here, :] = weights.apply(*(ref[here, :] for ref in (fields, around_e, around_w, around_n, around_s)))
        at_edge = (lane == 0) | (lane == last_lane)
        total = zero
        for k in range(sz.lev - 1, -1, -1):
            at = k * sz.rows
            total = total + div[at : at + sz.rows, :]
            vert[at : at + sz.rows, :] = -total if k > 0 else zero
            mixing = mixing_in[at : at + sz.rows, :]
            mix[at : at + sz.rows, :] = jnp.where(at_edge, edge_mix[at : at + sz.rows, :], mixing)
        last_ratio = None
        up, down = faces(0)
        lower, inverse = [], []
        for k in range(sz.lev):
            at = k * sz.rows
            up_next, down_next = faces(k + 1)
            pivot = 1.0 + TIME_STEP * (up - down_next)
            lower.append(TIME_STEP * down)
            if k > 0:
                pivot = pivot - lower[k] * last_ratio
            inverse.append(1.0 / pivot)
            last_ratio = -TIME_STEP * up_next * inverse[k]
            ratio[at : at + sz.rows, :] = last_ratio
            inv_ref[at : at + sz.rows, :] = inverse[k]
            pull[at : at + sz.rows, :] = lower[k] * inverse[k]
            up, down = up_next, down_next
        previous = [None] * sz.nf
        for k in range(sz.lev):
            at = k * sz.rows
            weights = stored_weights(k)
            values = [forward[f * sz.slab + at : f * sz.slab + at + sz.rows, :] for f in every]
            to_e, to_w = [turn(value, -1, 1) for value in values], [turn(value, 1, 1) for value in values]
            for f in every:
                here = slice(f * sz.slab + at, f * sz.slab + at + sz.rows)
                beyond = slice(f * sz.lev + k, f * sz.lev + k + 1)
                edge = second[here, :]
                value = weights.apply(
                    values[f],
                    jnp.where(lane == last_lane, edge, to_e[f]),
                    jnp.where(lane == 0, edge, to_w[f]),
                    shift_north(values[f], row, high_strip[beyond, :]),
                    shift_south(values[f], row, low_strip[beyond, :]),
                )
                moved[here, :] = value * inv_ref[at : at + sz.rows, :]
        for k in range(sz.lev):
            at = k * sz.rows
            for f in every:
                here = f * sz.slab + at
                value = moved[here : here + sz.rows, :]
                if k > 0:
                    value = value - pull[at : at + sz.rows, :] * previous[f]
                forward[here : here + sz.rows, :] = value
                previous[f] = value
        for k in range(sz.lev - 1, -1, -1):
            at = k * sz.rows
            wet = lev > k
            for f in range(sz.nf):
                here = f * sz.slab + at
                if k < sz.lev - 1:
                    previous[f] = forward[here : here + sz.rows, :] - ratio[at : at + sz.rows, :] * previous[f]
                out[f, at : at + sz.rows, :] = keep(wet, previous[f])
            if k % chunk == 0:
                send(0, sz.nf, k // chunk)

    @pl.when(is_dynamics)
    def _():
        physics()
        finish_copies()

    @pl.when(jnp.logical_not(is_dynamics))
    def _():
        transport(TIME_STEP / NSUB)
        finish_copies()


def pair_of(index, count, odd):
    if not odd:
        return index ^ 1
    return (((index + 1) ^ 1) - 1) % count


def on_device(sizes_of, fields, levels):
    sz = Sizes(fields, levels)
    count_s, count_o, count_a = sizes_of
    flat = fields.reshape(sz.nf * sz.slab, sz.cols)

    def place(s, o, a):
        return (s * count_o + o) * count_a + a

    def partner(s, o, a, odd, hop):
        b = pair_of(a, count_a, odd)
        if abs(a - b) > 1 and count_o % 2 == 0:
            return place(s, o ^ 1, a)
        return place((s + hop) % count_s, o, b)

    def swap(value, odd, hop=0):
        pairs = [
            (place(s, o, a), partner(s, o, a, odd, hop))
            for s in range(count_s)
            for o in range(count_o)
            for a in range(count_a)
        ]
        return lax.ppermute(value, ("sect", "lon", "lat"), pairs)

    def from_dynamics(value, odd=None):
        mine = lax.axis_index("sect")
        got = None
        for hop in range(1, count_s):
            if odd is None:
                part = lax.ppermute(value, "sect", [(s, (s + hop) % count_s) for s in range(count_s)])
            else:
                part = swap(value, odd, hop)
            got = part if got is None else jnp.where(mine == hop, part, got)
        return got

    def around(value, step):
        return lax.ppermute(value, "lon", [(i, (i + step) % count_o) for i in range(count_o)])

    rows_shape = (2 * sz.nf * sz.lev, sz.cols)
    cross_shape = (LEVEL_ROW * sz.lev + 8, sz.cols)
    columns_shape = (4 * sz.rows + sz.lev, sz.cols)
    side_shape = (4 * sz.rows, sz.cols)
    slab = (sz.slab, sz.cols)
    row_a, row_b, own_side, zonal, merid = call_kernel(
        functools.partial(pack_edges, sz), [rows_shape, rows_shape, side_shape, slab, slab], [flat]
    )
    twin_shape = (4 * sz.rows + LEVEL_ROW * sz.lev, sz.cols)
    (cross_b,) = call_kernel(functools.partial(pack_cross, sz), [cross_shape], [flat, levels])
    row_a = swap(row_a, False)
    levels_a = swap(levels, False)
    row_b = swap(row_b, True)
    (twin,) = call_kernel(
        functools.partial(pack_twin, sz), [twin_shape], [own_side, row_a]
    )
    twin = from_dynamics(twin)
    cross_b = from_dynamics(cross_b, True)
    south, north, corners = call_kernel(
        functools.partial(place_rows, sz), [rows_shape, rows_shape, (sz.rows, sz.cols)], [row_a, row_b]
    )
    (mixing,) = call_kernel(
        functools.partial(pack_mixing, sz), [(sz.slab, sz.cols)], [flat, levels, levels_a, cross_b, south, north]
    )
    to_east, to_west, cross_south, cross_north = call_kernel(
        functools.partial(pack_columns, sz),
        [columns_shape] * 2 + [cross_shape] * 2,
        [levels, levels_a, south, north, corners, twin, cross_b, own_side],
    )
    mixing = from_dynamics(mixing)
    zonal, merid = from_dynamics(zonal), from_dynamics(merid)
    from_east = around(to_west, -1)
    from_west = around(to_east, 1)
    kept, moved_e, moved_w, around_n, around_s = call_kernel(
        functools.partial(shift_fields, sz), [flat.shape] * 5, [flat, levels, south, north, cross_south, cross_north]
    )
    around_e, around_w, second, edge_mix = call_kernel(
        functools.partial(column_edges, sz),
        [flat.shape] * 3 + [slab],
        [levels, cross_south, cross_north, to_east, to_west, twin, from_west, from_east, moved_e, moved_w],
    )
    out_shape = (sz.nf, sz.slab, sz.cols)
    strip = (sz.nf * sz.lev, sz.cols)
    (out,) = call_kernel(
        functools.partial(finish, sz),
        [out_shape],
        [
            kept, levels, south, north, cross_south, cross_north, zonal, merid, mixing, twin, from_west, from_east,
            moved_e, moved_w, around_e, around_w, around_n, around_s, second, edge_mix,
        ],
        [out_shape, slab, slab, slab, strip, strip, slab, flat.shape, slab, (5 * sz.slab, sz.cols), slab, flat.shape],
        copies=3 * CHUNKS,
    )
    return out.reshape(fields.shape)


def solution(mesh):
    sizes_of = (mesh.shape["sect"], mesh.shape["lon"], mesh.shape["lat"])
    return jax.shard_map(
        functools.partial(on_device, sizes_of),
        mesh=mesh,
        in_specs=(P("sect", None, None, "lat", "lon"), P("lat", "lon")),
        out_specs=P("sect", None, None, "lat", "lon"),
        check_vma=False,
    )
```
